128 devices in a mesh: grp: 4 (over z_lo, core), cp: 32 (over x, y, z_hi).
Axes of the slice: x: 4, y: 4, z: 4 (z_hi: 2, z_lo: 2; z = z_hi * 2 + z_lo), core: 2. Of those that a mesh axis runs over, the one named last changes fastest.
Arguments:
- queries: bfloat16 [3, 32, 73728], P(None, 'cp'), may hold values from -25 to 25, as said below
- cache: bfloat16 [3, 65536, 576], P(None, 'cp'), may hold values from -5 to 5
- value_up_weight: bfloat16 [128, 512, 128], P('cp'), may hold values from -0.25 to 0.25
- w_out: bfloat16 [16384, 7168], P('cp'), may hold values from -0.375 to 0.375
- resid: bfloat16 [3, 32, 7168], P(None, 'cp'), may hold values from -1.5 to 1.5
- norm_gain: float32 [7168], replicated, may hold values from 0.5 to 1.5
- routes: int32 [3, 32, 4], P(None, 'cp'), may hold values from 0 to 7, all different within a row
- route_weight: bfloat16 [3, 32, 4], P(None, 'cp'), may hold values from 0.099609375 to 1
- w_gate: bfloat16 [32, 7168, 512], P('cp', 'grp'), may hold values from -0.0625 to 0.0625
- w_up: bfloat16 [32, 7168, 512], P('cp', 'grp'), may hold values from -0.0625 to 0.0625
- w_down: bfloat16 [32, 512, 7168], P('cp', None, 'grp'), may hold values from -0.125 to 0.125
Outputs:
- mixed: bfloat16 [3, 32, 7168], P(None, 'cp')
The draws below stay inside these ranges and needn't reach their ends.
Inputs may be any that keep to these rules, and one draw needn't show every extreme that they name: `queries`: query entries.
All inputs are finite; a program needn't handle non-finite values.
Results may differ from the reference program's by a relative error of at most 0.014.
Values may be sent and summed in bfloat16 or wider, within the bound.
A program may use at most 192 MiB of HBM per device.

```python
import math
import jax
import jax.numpy as jnp
from jax import lax

D = 7168
H = 128
KVL = 512
DV = 128
FE = 2048
SPLIT = 4
TOP = 4
QROWS = 32
CTX_DEV = 2048
QK = 576
FE_DEV = 512
CTX = 65536
SEQS = 3
EXPERTS = 8
N_CP = 32


def base_keys(key):
    return jnp.clip(jax.random.normal(key, (SEQS, CTX, QK), jnp.float32), -5.0, 5.0)


def draw_cache(key, part):
    base_rows = base_keys(key)
    return base_rows.astype(jnp.bfloat16)


def draw_queries(key, part):
    key = jax.random.fold_in(key, 22)
    fresh = jnp.clip(jax.random.normal(key, (SEQS, QROWS, H, QK), jnp.float32), -5.0, 5.0)
    return fresh.reshape(SEQS, QROWS, H * QK).astype(jnp.bfloat16)


def shard_levels(rng, shape, cuts, least, high):
    def one(axis_at, blocks):
        heights = jax.random.uniform(jax.random.fold_in(jax.random.fold_in(rng, 6), axis_at), (blocks,), jnp.float32, least / len(cuts), high / len(cuts))
        return jnp.repeat(jnp.exp(heights), shape[axis_at] // blocks).reshape((-1,) + (1,) * (len(shape) - axis_at - 1))

    factor_of = one(*cuts[0])
    for cut in cuts[1:]:
        factor_of = factor_of * one(*cut)
    return factor_of


def picks_of(own_key, rows, count, top, lift):
    order = jax.random.permutation(jax.random.fold_in(own_key, 1), count)
    pull = order
    for power in range(3):
        pull = pull * pull // count
    pull = pull * lift // count
    tickets = jax.random.randint(jax.random.fold_in(own_key, 2), (rows, count), 0, 4096) + pull
    sure = jax.random.permutation(jax.random.fold_in(own_key, 3), rows)[jnp.arange(count) % rows]
    tickets = jnp.where(jnp.arange(rows)[:, None] == sure[None, :], 1 << 14, tickets)
    merit = tickets * count + jnp.arange(count)
    return lax.top_k(merit.astype(jnp.int32), top)[1].astype(jnp.int32)


def scatter_about(stream_key, dims, width, most, cuts=(), held_as=jnp.bfloat16):
    values = width * jax.random.normal(stream_key, dims, jnp.float32)
    if cuts:
        values = values * shard_levels(stream_key, dims, cuts, -0.22, 0.18)
    return jnp.clip(values, -most, most).astype(held_as)


def setup_inputs(seed: int = 0) -> dict:
    seeds = jax.random.split(jax.random.key(seed), 12)
    return {
        "queries": draw_queries(jax.random.fold_in(seeds[11], 71), 0),
        "cache": draw_cache(jax.random.fold_in(seeds[11], 71), 0),
        "value_up_weight": scatter_about(seeds[2], (H, KVL, DV), KVL ** -0.5, 0.25, ((0, 32),)),
        "w_out": scatter_about(seeds[3], (H * DV, D), (H * DV // 64) ** -0.5, 0.375, ((0, 32),)),
        "resid": scatter_about(seeds[4], (SEQS, QROWS, D), 0.25, 1.5, ((1, 32),)),
        "norm_gain": jnp.clip(1.0 + 0.1 * jax.random.normal(seeds[5], (D,), jnp.float32), 0.5, 1.5),
        "routes": picks_of(seeds[6], SEQS * QROWS, EXPERTS, TOP, 8192).reshape((SEQS, QROWS, TOP)),
        "route_weight": jnp.clip(jnp.exp(math.log(1.0) - 2.306499 * jax.random.uniform(seeds[7], (SEQS, QROWS, TOP), jnp.float32) ** shard_levels(seeds[7], (SEQS, QROWS, TOP), ((1, 32),), -0.2, 0.2)), 0.099609375, 1.0).astype(jnp.bfloat16),
        "w_gate": scatter_about(seeds[8], (N_CP, D, FE_DEV), D ** -0.5, 0.0625, ((0, 32), (1, 4))),
        "w_up": scatter_about(seeds[9], (N_CP, D, FE_DEV), D ** -0.5, 0.0625, ((0, 32), (1, 4))),
        "w_down": scatter_about(seeds[10], (N_CP, FE_DEV, D), FE ** -0.5, 0.125, ((0, 32), (2, 4))),
    }


score_scale = 192.0 ** (-0.5)

def attend_latent(query_block, key_rows, offset, total_len):
    scores = jnp.einsum('qhk,tk->qht', query_block.astype(jnp.float32), key_rows.astype(jnp.float32)) * score_scale
    position_list = offset + jnp.arange(key_rows.shape[0], dtype=jnp.int32)
    query_pos = total_len - query_block.shape[0] + jnp.arange(query_block.shape[0], dtype=jnp.int32)
    allowed = position_list[None, None, :] <= query_pos[:, None, None]
    scores = jnp.where(allowed, scores, -1e+30)
    row_peak = lax.optimization_barrier(jnp.max(scores, axis=-1))
    weights_exp = jnp.where(allowed, jnp.exp(scores - row_peak[..., None]), 0.0)
    row_total = lax.optimization_barrier(jnp.sum(weights_exp, axis=-1))
    rounded = weights_exp.astype(jnp.bfloat16).astype(jnp.float32)
    values = key_rows[:, :KVL].astype(jnp.float32)
    row_output = jnp.einsum('qht,tv->qhv', rounded, values) / row_total[..., None]
    return (row_peak, row_total, row_output)

def reference(queries, cache, value_up_weight, w_out, resid, norm_gain, routes, route_weight, w_gate, w_up, w_down):
    total_len = CTX_DEV * N_CP
    hidden_list = []
    for sequence in range(SEQS):
        query_block = queries[sequence].reshape(QROWS, H, QK)
        seq_cache = cache[sequence]

        def one_block(block_index):
            key_rows = lax.dynamic_slice_in_dim(seq_cache, (block_index * CTX_DEV).astype(jnp.int32), CTX_DEV, 0)
            return attend_latent(query_block, key_rows, block_index * CTX_DEV, total_len)
        row_peak, row_total, row_output = lax.map(one_block, jnp.arange(N_CP, dtype=jnp.int32))
        peak_overall = lax.optimization_barrier(jnp.max(row_peak, axis=0))
        block_weight = row_total * jnp.exp(row_peak - peak_overall[None])
        latent_state = (lax.optimization_barrier(jnp.sum(block_weight[..., None] * row_output, axis=0)) / lax.optimization_barrier(jnp.sum(block_weight, axis=0))[..., None]).astype(jnp.bfloat16)
        head_list = jnp.einsum('mtz,tzu->mtu', latent_state.astype(jnp.float32), value_up_weight.astype(jnp.float32)).astype(jnp.bfloat16)
        head_list = head_list.reshape(QROWS, H * DV)
        attn_rows = jnp.dot(head_list, w_out, preferred_element_type=jnp.float32)
        hidden_list.append((resid[sequence].astype(jnp.float32) + attn_rows).astype(jnp.bfloat16))
    hidden = jnp.concatenate(hidden_list, axis=0)
    hidden_f = hidden.astype(jnp.float32)
    normed = (hidden_f * lax.rsqrt(lax.optimization_barrier(jnp.mean(hidden_f * hidden_f, axis=-1, keepdims=True)) + 1e-06) * norm_gain).astype(jnp.bfloat16)
    flat_routes = routes.reshape(SEQS * QROWS, TOP)
    flat_weight = route_weight.reshape(SEQS * QROWS, TOP).astype(jnp.float32)

    def slice_term(expert_total, slice_index):
        gate_sums = jnp.dot(normed, w_gate[slice_index], preferred_element_type=jnp.float32)
        up_sums = jnp.dot(normed, w_up[slice_index], preferred_element_type=jnp.float32)
        units = (jax.nn.silu(gate_sums) * up_sums).astype(jnp.bfloat16)
        part = jnp.dot(units, w_down[slice_index], preferred_element_type=jnp.float32).astype(jnp.bfloat16)
        factor = lax.optimization_barrier(jnp.sum(jnp.where(flat_routes == slice_index // SPLIT, flat_weight, 0.0), axis=-1))
        return (expert_total + part.astype(jnp.float32) * factor[:, None], None)
    expert_total, unused = lax.scan(slice_term, jnp.zeros((SEQS * QROWS, D), jnp.float32), jnp.arange(N_CP, dtype=jnp.int32))
    mixed = (hidden_f + expert_total).astype(jnp.bfloat16)
    return mixed.reshape(SEQS, QROWS, D)
```

```python
import math

import jax
import jax.numpy as jnp
from jax import lax
from jax.experimental import pallas as pl
from jax.experimental.pallas import tpu as pltpu
from jax.sharding import PartitionSpec as P

D = 7168
KVL = 512
DV = 128
SPLIT = 4
QROWS = 32
CTX_DEV = 2048
QK = 576
QPAD = 640
SEQS = 3
EXPERTS = 8
QUARTER = D // 4
HALF = QUARTER // 2
N_CP = 32
CTX = CTX_DEV * N_CP

SCALE = 192.0 ** (-0.5)
SCALE2 = SCALE * math.log2(math.e)
MESH = pl.DeviceIdType.MESH
F32 = jnp.float32
BF16 = jnp.bfloat16


def place():
    g = lax.axis_index("grp")
    c = lax.axis_index("cp")
    return g, c, c // 8, (c // 2) % 4, c % 2


def mm(a, b):
    return jnp.dot(a, b, preferred_element_type=F32)


def mm_nt(a, b):
    return lax.dot_general(a, b, (((1,), (1,)), ((), ())), preferred_element_type=F32)


def iota(shape, axis):
    return lax.broadcasted_iota(jnp.int32, shape, axis)


class Wire:
    def __init__(self, send_sems, recv_sems):
        self.send_sems, self.recv_sems = send_sems, recv_sems
        self.started = []

    def push(self, src, dst, device):
        at = len(self.started)
        copy = pltpu.make_async_remote_copy(
            src_ref=src,
            dst_ref=dst,
            send_sem=self.send_sems.at[at],
            recv_sem=self.recv_sems.at[at],
            device_id=device,
            device_id_type=MESH,
        )
        copy.start()
        self.started.append(copy)
        return copy

    def finish(self):
        for copy in self.started:
            copy.wait_send()


def greet(peers):
    barrier = pltpu.get_barrier_semaphore()
    for peer in peers:
        pl.semaphore_signal(barrier, inc=1, device_id=peer, device_id_type=MESH)
    pl.semaphore_wait(barrier, len(peers))


def padded_row(shape, axis, part):
    r = iota(shape, axis)
    s, z, b, a = r % 4, (r // 4) % 2, (r // 8) % 4, r // 32
    x, y = (a, b) if part == 0 else (b, a)
    return s, (x * 4 + y) * 2 + z


def unpack(value):
    value = value.reshape(48, QPAD).astype(F32)
    aux = value[:, KVL:]
    lane = iota(aux.shape, 1)
    peak = jnp.sum(jnp.where(lane == 0, aux, 0.0), axis=-1, keepdims=True)
    total = jnp.sum(jnp.where((lane == 1) | (lane == 2), aux, 0.0), axis=-1, keepdims=True)
    return value[:, :KVL], peak, total


def aux_lanes(peak, total):
    lane = iota((peak.shape[0], QPAD - KVL), 1)
    high = total.astype(BF16).astype(F32)
    low = total - high
    return jnp.where(
        lane == 0, peak, jnp.where(lane == 1, high, jnp.where(lane == 2, low, 0.0))
    )


def merge(values):
    items = [unpack(value) for value in values]
    peak = items[0][1]
    for item in items[1:]:
        peak = jnp.maximum(peak, item[1])
    out, total = None, None
    for item in items:
        factor = jnp.exp((item[1] - peak) * SCALE)
        if out is None:
            out, total = item[0] * factor, item[2] * factor
        else:
            out, total = out + item[0] * factor, total + item[2] * factor
    return out, peak, total


def put(ref, merged):
    out, peak, total = merged
    ref[..., :KVL] = out.astype(BF16).reshape(3, 16, KVL)
    ref[..., KVL:] = aux_lanes(peak, total).astype(BF16).reshape(3, 16, QPAD - KVL)


def attend_kernel(
    q_ref, cache_ref, lat_ref, fac_ref,
    qbuf, kv, kpe, score_a, score_b, prob_a, prob_b, oscr, msg, rx1, rx2, rx3, fin, rxz,
    send_sems, recv_sems, local_sems,
):
    g, c, x, y, z = place()
    up = lambda v, d: lax.rem(v + d, 4)

    def at(px, py, pz):
        return (g, (px * 4 + py) * 2 + pz)

    partner = (lax.rem(g + 2, 4), (x * 4 + y) * 2 + (1 - z))
    own = [
        pltpu.make_async_copy(q_ref.at[h], qbuf.at[h, x, y, z], local_sems.at[h]) for h in range(2)
    ]
    for copy in own:
        copy.start()
    loads = [
        pltpu.make_async_copy(cache_ref.at[s], kv.at[s], local_sems.at[2 + s]) for s in range(3)
    ]
    for copy in loads:
        copy.start()

    greet([at(up(x, d), y, z) for d in (1, 2, 3)] + [at(x, up(y, d), z) for d in (1, 2, 3)] + [partner])
    wire = Wire(send_sems, recv_sems)

    zs = [wire.push(q_ref.at[h], qbuf.at[h, x, y, z], partner) for h in range(2)]
    for copy in own:
        copy.wait()
    for copy in loads:
        copy.wait()
    kpe[...] = jnp.zeros_like(kpe)
    for s in range(3):
        kpe[s, :, : QK - KVL] = kv[s, :, KVL:]
    dirs = (1, 3)
    gathers = []
    for h in range(2):
        zs[h].wait_recv()
        first = []
        for d in dirs:
            first.append(wire.push(qbuf.at[h, x, y, 0], qbuf.at[h, x, y, 0], at(up(x, d), y, z)))
            first.append(wire.push(qbuf.at[h, x, y, 1], qbuf.at[h, x, y, 1], at(x, up(y, d), z)))
        gathers.append(first)
    forwards = []
    for h in range(2):
        for copy in gathers[h]:
            copy.wait_recv()
        second = []
        for d, lanes in ((1, pl.ds(0, 256)), (3, pl.ds(256, 384))):
            rear = up(x, 4 - d)
            ref = qbuf.at[h, rear, y, 0, :, :, lanes]
            second.append(wire.push(ref, ref, at(up(x, d), y, z)))
            rear = up(y, 4 - d)
            ref = qbuf.at[h, x, rear, 1, :, :, lanes]
            second.append(wire.push(ref, ref, at(x, up(y, d), z)))
        forwards.append(second)
    gathers = []
    for h in range(2):
        for copy in forwards[h]:
            copy.wait_recv()
        third = []
        for d in dirs:
            ref = qbuf.at[h, :, y, 0]
            third.append(wire.push(ref, ref, at(x, up(y, d), z)))
            ref = qbuf.at[h, x, :, 1]
            third.append(wire.push(ref, ref, at(up(x, d), y, z)))
        gathers.append(third)
    forwards = []
    for h in range(2):
        for copy in gathers[h]:
            copy.wait_recv()
        fourth = []
        for d, pair in ((1, pl.ds(0, 2)), (3, pl.ds(2, 2))):
            ref = qbuf.at[h, pair, up(y, 4 - d), 0]
            fourth.append(wire.push(ref, ref, at(x, up(y, d), z)))
            ref = qbuf.at[h, up(x, 4 - d), pair, 1]
            fourth.append(wire.push(ref, ref, at(up(x, d), y, z)))
        forwards.append(fourth)

    def scores(h, s, part, score):
        q = qbuf[h, 2 * part : 2 * part + 2, :, :, s].reshape(256, QPAD)
        for n in range(4):
            keys = pl.ds(n * 512, 512)
            value = mm_nt(q[:, :KVL], kv[s, keys, :KVL]) + mm_nt(q[:, KVL:], kpe[s, keys])
            if n < 3:
                score[:, keys] = value
            else:
                score[:, 1536:1920] = value[:, :384]
                row = 16 * part + iota((256, 128), 0) // 16
                position = c * CTX_DEV + 1920 + iota((256, 128), 1)
                score[:, 1920:] = jnp.where(
                    position <= CTX - QROWS + row, value[:, 384:], -1e30
                )

    def weigh(h, s, part, score, prob):
        peak = jnp.max(score[...], axis=-1, keepdims=True).astype(BF16).astype(F32)
        total = jnp.zeros((256, 128), F32)
        for n in range(4):
            keys = pl.ds(n * 512, 512)
            weight = jnp.exp2((score[:, keys] - peak) * SCALE2)
            for m in range(4):
                total = total + weight[:, m * 128 : (m + 1) * 128]
            prob[:, keys] = weight.astype(BF16)
        total = jnp.sum(total, axis=-1, keepdims=True)
        out = mm(prob[...], kv[s, :, :KVL])
        for m in range(4):
            oscr[part, m] = out[:, m * 128 : (m + 1) * 128]
        oscr[part, 4] = aux_lanes(peak, total)
        for n in range(16):
            a, b = (n // 4, n % 4) if part == 0 else (n % 4, n // 4)
            for m in range(5):
                lanes = pl.ds(m * 128, 128)
                msg[h, part, a, b, s, :, lanes] = oscr[part, m, pl.ds(n, 16, stride=16), :].astype(BF16)

    def attend(h):
        @pl.loop(0, SEQS)
        def _(s):
            scores(h, s, 0, score_a)
            scores(h, s, 1, score_b)
            weigh(h, s, 0, score_a, prob_a)
            weigh(h, s, 1, score_b, prob_b)

    axes = [
        (x, y, lambda f, e: at(f, e, z)),
        (y, x, lambda f, e: at(e, f, z)),
    ]

    def reduce_1(h):
        copies = []
        for part, (f, e, to) in enumerate(axes):
            far = up(f, 2)
            for at_, d in enumerate((1, 3)):
                copies.append(
                    wire.push(
                        msg.at[h, part, far, pl.ds(2 * at_, 2)], rx1.at[h, part, at_], to(up(f, d), e)
                    )
                )
        return copies

    def reduce_2(h, copies):
        for copy in copies:
            copy.wait_recv()
        copies = []
        for part, (f, e, to) in enumerate(axes):
            for at_, d in enumerate((1, 3)):
                chunk = up(f, d)

                @pl.loop(0, 2)
                def _(j):
                    put(
                        msg.at[h, part, chunk, 2 * at_ + j],
                        merge([msg[h, part, chunk, 2 * at_ + j], rx1[h, part, at_, j]]),
                    )

                copies.append(
                    wire.push(msg.at[h, part, chunk], rx2.at[h, part, at_], to(chunk, e))
                )
        return copies

    def reduce_3(h, copies):
        for copy in copies:
            copy.wait_recv()
        copies = []
        for part, (f, e, to) in enumerate(axes):

            @pl.loop(0, 4)
            def _(j):
                put(
                    msg.at[h, part, f, j],
                    merge([msg[h, part, f, j], rx2[h, part, 0, j], rx2[h, part, 1, j]]),
                )

            for d in (1, 2, 3):
                copies.append(
                    wire.push(
                        msg.at[h, part, f, up(e, d)], rx3.at[h, part, d - 1], to(f, up(e, d))
                    )
                )
        return copies

    def reduce_4(h, copies):
        for copy in copies:
            copy.wait_recv()
        for part, (f, e, to) in enumerate(axes):
            put(
                fin.at[h, part],
                merge([msg[h, part, f, e]] + [rx3[h, part, d] for d in range(3)]),
            )

    for h in range(2):
        for copy in forwards[h]:
            copy.wait_recv()
    attend(0)
    attend(1)
    steps = [reduce_1(0), reduce_1(1)]
    steps = [reduce_2(h, steps[h]) for h in range(2)]
    steps = [reduce_3(h, steps[h]) for h in range(2)]
    for h in range(2):
        reduce_4(h, steps[h])
    last = wire.push(fin.at[1 - z], rxz, partner)

    for part in range(2):
        picked = jnp.zeros((128, 128), F32)
        for s in range(SEQS):
            seq, row = padded_row((128, 512), 0, part)
            j = iota((128, 512), 1)
            pick = ((seq == s) & (j == row * 16)).astype(F32).astype(BF16)
            picked = picked + mm(pick, qbuf[0, :, :, :, s, :, KVL:].reshape(512, 128))
        lane = iota((128, 128), 1)
        chosen = jnp.sum(
            jnp.where(lane == QK - KVL + c // SPLIT, picked, 0.0), axis=-1, keepdims=True
        )
        fac_ref[part] = jnp.broadcast_to(chosen, (128, 128))

    last.wait_recv()
    for part in range(2):
        out, peak, total = merge([fin[z, part], rxz[part]])
        lat_ref[part * 48 : (part + 1) * 48, :] = (out / total).astype(BF16)
    wire.finish()


def tail_kernel(
    lat_ref, fac_ref, vup_ref, wout_ref, resid_ref, gain_ref, wg_ref, wu_ref, wd_ref, out_ref,
    vup, wout, wg, wu, wd, heads, pbuf, rxa, ebuf, rxb, zbuf, rxc, hid, hidf,
    sq, rxs, gs, rxg, units, qbuf, rxq, ybuf, rxy, wbuf, rxw, fo,
    send_sems, recv_sems, local_sems,
):
    g, c, x, y, z = place()
    up = lambda v, d: lax.rem(v + d, 4)

    def at(px, py, pz):
        return (g, (px * 4 + py) * 2 + pz)

    columns = pl.ds(pl.multiple_of(g * QUARTER, 128), QUARTER)
    loads = [
        pltpu.make_async_copy(src, dst, local_sems.at[n])
        for n, (src, dst) in enumerate(
            (
                (vup_ref.at[g], vup),
                (wout_ref.at[:, columns], wout),
                (wg_ref.at[0], wg),
                (wu_ref.at[0], wu),
                (wd_ref.at[0], wd),
            )
        )
    ]
    for copy in loads:
        copy.start()
    mates = [(up(g, d), c) for d in (1, 2, 3)]
    far = at(x, y, 1 - z)
    greet(
        [at(up(x, d), y, z) for d in (1, 2, 3)]
        + [at(x, up(y, d), z) for d in (1, 2, 3)]
        + [far]
        + mates
    )
    wire = Wire(send_sems, recv_sems)
    axes = [
        (x, y, lambda f, e: at(f, e, z)),
        (y, x, lambda f, e: at(e, f, z)),
    ]

    loads[0].wait()
    heads[g] = mm(lat_ref[...], vup[...]).astype(BF16)
    copies = [wire.push(heads.at[g], heads.at[g], mate) for mate in mates]
    spread, gathered = [], []
    for part in range(2):
        seq, row = padded_row((128, 96), 0, part)
        j = iota((128, 96), 1)
        spread.append(
            ((seq < SEQS) & (j == (row // 16) * 48 + seq * 16 + row % 16)).astype(F32).astype(BF16)
        )
        seq, row = padded_row((96, 128), 1, part)
        j = iota((96, 128), 0)
        gathered.append(
            ((seq < SEQS) & (j == (row // 16) * 48 + seq * 16 + row % 16)).astype(F32).astype(BF16)
        )
    for copy in copies:
        copy.wait_recv()
    loads[1].wait()
    for part in range(2):
        cols = pl.ds(part * HALF, HALF)
        seq, row = padded_row((128, 16), 0, part)
        mine = ((row == c) & (seq == iota((128, 16), 1)) & (seq < SEQS)).astype(F32).astype(BF16)
        value = mm(mine, resid_ref[:, cols])
        for k in range(4):
            rows = mm(spread[part], heads[k]).astype(BF16)
            value = value + mm(rows, wout[k * DV : (k + 1) * DV, cols])
        pbuf[part] = value.astype(BF16).reshape(4, 32, HALF)

    def scatter(source, landing):
        copies = []
        for part, (f, e, to) in enumerate(axes):
            for d in (1, 2, 3):
                copies.append(
                    wire.push(source.at[part, up(f, d)], landing.at[part, d - 1], to(up(f, d), e))
                )
        return copies

    def summed(first, landing, part):
        value = first.astype(F32)
        for d in range(3):
            value = value + landing[part, d].astype(F32)
        return value

    copies = scatter(pbuf, rxa)
    for copy in copies:
        copy.wait_recv()
    copies = []
    for part, (f, e, to) in enumerate(axes):
        ebuf[part] = summed(pbuf[part, f], rxa, part).astype(BF16)
        for d in (1, 2, 3):
            copies.append(wire.push(ebuf.at[part], rxb.at[part, d - 1], to(f, up(e, d))))
    for copy in copies:
        copy.wait_recv()
    for part in range(2):
        zbuf[part] = summed(ebuf[part], rxb, part).astype(BF16)
    copy = wire.push(zbuf, rxc, far)
    copy.wait_recv()
    copies = []
    for part, (f, e, to) in enumerate(axes):
        value = (zbuf[part].astype(F32) + rxc[part].astype(F32)).astype(BF16)
        hid[part, f] = value
        hidf[part] = value.astype(F32).reshape(4, 8, HALF)
        for d in (1, 2, 3):
            ref = hid.at[part, f]
            copies.append(wire.push(ref, ref, to(up(f, d), e)))
    for copy in copies:
        copy.wait_recv()

    loads[2].wait()
    loads[3].wait()
    eye = iota((96, 128), 0) == iota((96, 128), 1)
    squares = jnp.zeros((96, 1), F32)
    gate = jnp.zeros((96, 512), F32)
    rise = jnp.zeros((96, 512), F32)
    for part in range(2):
        rows = mm(gathered[part], hid[part].reshape(128, HALF))
        squares = squares + jnp.sum(rows * rows, axis=-1, keepdims=True)
        cols = pl.ds(part * HALF, HALF)
        scaled = (rows * gain_ref[0:1, cols]).astype(BF16)
        gate = gate + mm(scaled, wg[cols, :])
        rise = rise + mm(scaled, wu[cols, :])
    sq[...] = jnp.broadcast_to(
        jnp.sum(jnp.where(eye, squares, 0.0), axis=0, keepdims=True), (8, 128)
    )
    for j in range(4):
        gs[j, :, :128] = gate[:, j * 128 : (j + 1) * 128].astype(BF16)
        gs[j, :, 128:] = rise[:, j * 128 : (j + 1) * 128].astype(BF16)
    copies = []
    for d in (1, 2, 3):
        copies.append(wire.push(sq, rxs.at[d - 1], mates[d - 1]))
        copies.append(wire.push(gs.at[up(g, d)], rxg.at[d - 1], mates[d - 1]))
    for copy in copies:
        copy.wait_recv()
    both = gs[g].astype(F32)
    total = sq[0:1, :]
    for d in range(3):
        both = both + rxg[d].astype(F32)
        total = total + rxs[d, 0:1, :]
    total = jnp.sum(jnp.where(eye, total, 0.0), axis=-1, keepdims=True)
    both = both * lax.rsqrt(total * (1.0 / D) + 1e-06)
    gate, rise = both[:, :128], both[:, 128:]
    units[g] = (gate / (1.0 + jnp.exp(-gate)) * rise).astype(BF16)
    copies = [wire.push(units.at[g], units.at[g], mate) for mate in mates]
    for copy in copies:
        copy.wait_recv()
    loads[4].wait()
    for part in range(2):
        cols = pl.ds(part * HALF, HALF)
        value = jnp.zeros((128, HALF), F32)
        for k in range(4):
            rows = mm(spread[part], units[k]).astype(BF16)
            value = value + mm(rows, wd[k * 128 : (k + 1) * 128, cols])
        value = value.astype(BF16).astype(F32) * fac_ref[part, :, 0:1]
        qbuf[part] = value.astype(BF16).reshape(4, 32, HALF)
    copies = scatter(qbuf, rxq)
    for copy in copies:
        copy.wait_recv()
    copies = []
    for part, (f, e, to) in enumerate(axes):
        ybuf[part] = summed(qbuf[part, f], rxq, part).reshape(4, 8, HALF)
        for d in (1, 2, 3):
            copies.append(wire.push(ybuf.at[part, up(e, d)], rxy.at[part, d - 1], to(f, up(e, d))))
    for copy in copies:
        copy.wait_recv()
    for part, (f, e, to) in enumerate(axes):
        wbuf[part] = summed(ybuf[part, e], rxy, part)
    copy = wire.push(wbuf, rxw, far)
    copy.wait_recv()
    for part, (f, e, to) in enumerate(axes):
        value = hidf[part, e] + (wbuf[part] + rxw[part])
        fo[g, part * 4 : (part + 1) * 4, :] = jnp.where(z == 0, value[0:4], value[4:8])
    copies = [wire.push(fo.at[g], fo.at[g], mate) for mate in mates]
    for copy in copies:
        copy.wait_recv()
    for k in range(4):
        for part in range(2):
            at_ = k * QUARTER + part * HALF
            out_ref[:, at_ : at_ + HALF] = fo[k, part * 4 : part * 4 + SEQS, :].astype(BF16)
    wire.finish()


def vmem():
    return pl.BlockSpec(memory_space=pltpu.VMEM)


def hbm():
    return pl.BlockSpec(memory_space=pl.ANY)


def on_device(
    queries, cache, value_up_weight, w_out, resid, norm_gain, routes, route_weight,
    w_gate, w_up, w_down,
):
    g, c, x, y, z = place()
    pair, core = lax.rem(g // 2 + z, 2), g % 2
    by_column = queries.reshape(SEQS, 16, 8, QK)
    lower = lax.dynamic_index_in_dim(by_column, 2 * pair + core, 2, keepdims=False)
    upper = lax.dynamic_index_in_dim(by_column, 4 + 2 * (1 - pair) + core, 2, keepdims=False)
    matches = routes[:, 0, :, None] == jnp.arange(EXPERTS, dtype=jnp.int32)
    weights = jnp.sum(
        jnp.where(matches, route_weight[:, 0, :, None].astype(F32), 0.0), axis=1
    ).astype(BF16)
    spare = jnp.pad(weights, ((0, 0), (0, QPAD - QK - EXPERTS)))
    spare = jnp.broadcast_to(spare[None, :, None, :], (2, SEQS, 16, QPAD - QK))
    rows = jnp.concatenate([jnp.stack([lower, upper]), spare], axis=-1)

    latent, factor = pl.pallas_call(
        attend_kernel,
        out_shape=(
            jax.ShapeDtypeStruct((96, KVL), BF16),
            jax.ShapeDtypeStruct((2, 128, 128), F32),
        ),
        in_specs=[vmem(), hbm()],
        out_specs=(vmem(), vmem()),
        scratch_shapes=[
            pltpu.VMEM((2, 4, 4, 2, SEQS, 16, QPAD), BF16),
            pltpu.VMEM((SEQS, CTX_DEV, QK), BF16),
            pltpu.VMEM((SEQS, CTX_DEV, 128), BF16),
            pltpu.VMEM((256, CTX_DEV), F32),
            pltpu.VMEM((256, CTX_DEV), F32),
            pltpu.VMEM((256, CTX_DEV), BF16),
            pltpu.VMEM((256, CTX_DEV), BF16),
            pltpu.VMEM((2, 5, 256, 128), F32),
            pltpu.VMEM((2, 2, 4, 4, SEQS, 16, QPAD), BF16),
            pltpu.VMEM((2, 2, 2, 2, SEQS, 16, QPAD), BF16),
            pltpu.VMEM((2, 2, 2, 4, SEQS, 16, QPAD), BF16),
            pltpu.VMEM((2, 2, 3, SEQS, 16, QPAD), BF16),
            pltpu.VMEM((2, 2, SEQS, 16, QPAD), BF16),
            pltpu.VMEM((2, SEQS, 16, QPAD), BF16),
            pltpu.SemaphoreType.DMA((64,)),
            pltpu.SemaphoreType.DMA((64,)),
            pltpu.SemaphoreType.DMA((5,)),
        ],
        compiler_params=pltpu.CompilerParams(
            collective_id=0, has_side_effects=True, vmem_limit_bytes=56 * 1024 * 1024
        ),
    )(rows, cache)

    own_resid = lax.dynamic_slice_in_dim(resid[:, 0], g * QUARTER, QUARTER, 1)
    own_resid = jnp.pad(own_resid, ((0, 16 - SEQS), (0, 0)))
    own_gain = lax.dynamic_slice_in_dim(norm_gain, g * QUARTER, QUARTER, 0)
    own_gain = jnp.broadcast_to(own_gain[None], (8, QUARTER))
    mixed = pl.pallas_call(
        tail_kernel,
        out_shape=jax.ShapeDtypeStruct((SEQS, D), BF16),
        in_specs=[vmem(), vmem(), hbm(), hbm(), vmem(), vmem(), hbm(), hbm(), hbm()],
        out_specs=vmem(),
        scratch_shapes=[
            pltpu.VMEM((KVL, DV), BF16),
            pltpu.VMEM((512, QUARTER), BF16),
            pltpu.VMEM((QUARTER, 512), BF16),
            pltpu.VMEM((QUARTER, 512), BF16),
            pltpu.VMEM((512, QUARTER), BF16),
            pltpu.VMEM((4, 96, DV), BF16),
            pltpu.VMEM((2, 4, 32, HALF), BF16),
            pltpu.VMEM((2, 3, 32, HALF), BF16),
            pltpu.VMEM((2, 32, HALF), BF16),
            pltpu.VMEM((2, 3, 32, HALF), BF16),
            pltpu.VMEM((2, 32, HALF), BF16),
            pltpu.VMEM((2, 32, HALF), BF16),
            pltpu.VMEM((2, 4, 32, HALF), BF16),
            pltpu.VMEM((2, 4, 8, HALF), F32),
            pltpu.VMEM((8, 128), F32),
            pltpu.VMEM((3, 8, 128), F32),
            pltpu.VMEM((4, 96, 256), BF16),
            pltpu.VMEM((3, 96, 256), BF16),
            pltpu.VMEM((4, 96, 128), BF16),
            pltpu.VMEM((2, 4, 32, HALF), BF16),
            pltpu.VMEM((2, 3, 32, HALF), BF16),
            pltpu.VMEM((2, 4, 8, HALF), F32),
            pltpu.VMEM((2, 3, 8, HALF), F32),
            pltpu.VMEM((2, 8, HALF), F32),
            pltpu.VMEM((2, 8, HALF), F32),
            pltpu.VMEM((4, 8, HALF), F32),
            pltpu.SemaphoreType.DMA((50,)),
            pltpu.SemaphoreType.DMA((50,)),
            pltpu.SemaphoreType.DMA((5,)),
        ],
        compiler_params=pltpu.CompilerParams(
            collective_id=1, has_side_effects=True, vmem_limit_bytes=40 * 1024 * 1024
        ),
    )(latent, factor, value_up_weight, w_out, own_resid, own_gain, w_gate, w_up, w_down)
    return mixed.reshape(SEQS, 1, D)


def solution(mesh):
    placed = (
        P(None, "cp", None),
        P(None, "cp", None),
        P("cp", None, None),
        P("cp", None),
        P(None, "cp", None),
        P(),
        P(None, "cp", None),
        P(None, "cp", None),
        P("cp", "grp", None),
        P("cp", "grp", None),
        P("cp", None, "grp"),
    )
    return jax.shard_map(
        on_device, mesh=mesh, in_specs=placed, out_specs=P(None, "cp", None), check_vma=False
    )
```

```python
import math

import jax
import jax.numpy as jnp
from jax import lax
from jax.experimental import pallas as pl
from jax.experimental.pallas import tpu as pltpu
from jax.sharding import PartitionSpec as P

D = 7168
KVL = 512
DV = 128
SPLIT = 4
QROWS = 32
CTX_DEV = 2048
QK = 576
QPAD = 640
SEQS = 3
EXPERTS = 8
QUARTER = D // 4
HALF = QUARTER // 2
N_CP = 32
CTX = CTX_DEV * N_CP

SCALE = 192.0 ** (-0.5)
SCALE2 = SCALE * math.log2(math.e)
MESH = pl.DeviceIdType.MESH
F32 = jnp.float32
BF16 = jnp.bfloat16


def place():
    g = lax.axis_index("grp")
    c = lax.axis_index("cp")
    return g, c, c // 8, (c // 2) % 4, c % 2


def mm(a, b):
    return jnp.dot(a, b, preferred_element_type=F32)


def mm_nt(a, b):
    return lax.dot_general(a, b, (((1,), (1,)), ((), ())), preferred_element_type=F32)


def iota(shape, axis):
    return lax.broadcasted_iota(jnp.int32, shape, axis)


def part_of(ref, *index):
    return ref.at[index] if index else ref


class Wire:
    def __init__(self, send_sems, recv_sems):
        self.send_sems, self.recv_sems = send_sems, recv_sems
        self.started = []

    def push(self, src, dst, device):
        copy = Copy(self, len(self.started), src, dst, device)
        self.started.append(copy)
        copy.make().start()
        return copy

    def finish(self):
        for copy in self.started:
            copy.make().wait_send()


class Copy:
    def __init__(self, wire, at, src, dst, device):
        self.wire, self.at, self.src, self.dst, self.device = wire, at, src, dst, device

    def make(self):
        return pltpu.make_async_remote_copy(
            src_ref=part_of(*self.src),
            dst_ref=part_of(*self.dst),
            send_sem=self.wire.send_sems.at[self.at],
            recv_sem=self.wire.recv_sems.at[self.at],
            device_id=self.device,
            device_id_type=MESH,
        )

    def wait_recv(self):
        self.make().wait_recv()


def arrive(copies):
    for copy in copies:
        copy.wait_recv()


def greet(peers):
    barrier = pltpu.get_barrier_semaphore()
    for peer in peers:
        pl.semaphore_signal(barrier, inc=1, device_id=peer, device_id_type=MESH)
    pl.semaphore_wait(barrier, len(peers))


def padded_row(shape, axis, part):
    r = iota(shape, axis)
    s, z, b, a = r % 4, (r // 4) % 2, (r // 8) % 4, r // 32
    x, y = (a, b) if part == 0 else (b, a)
    return s, (x * 4 + y) * 2 + z


def unpack(value):
    value = value.reshape(-1, QPAD).astype(F32)
    aux = value[:, KVL:]
    lane = iota(aux.shape, 1)
    peak = jnp.sum(jnp.where(lane == 0, aux, 0.0), axis=-1, keepdims=True)
    total = jnp.sum(jnp.where((lane == 1) | (lane == 2), aux, 0.0), axis=-1, keepdims=True)
    return value[:, :KVL], peak, total


def aux_lanes(peak, total):
    lane = iota((peak.shape[0], QPAD - KVL), 1)
    high = total.astype(BF16).astype(F32)
    low = total - high
    return jnp.where(
        lane == 0, peak, jnp.where(lane == 1, high, jnp.where(lane == 2, low, 0.0))
    )


def merge(values):
    items = [unpack(value) for value in values]
    peak = items[0][1]
    for item in items[1:]:
        peak = jnp.maximum(peak, item[1])
    out, total = None, None
    for item in items:
        factor = jnp.exp((item[1] - peak) * SCALE)
        if out is None:
            out, total = item[0] * factor, item[2] * factor
        else:
            out, total = out + item[0] * factor, total + item[2] * factor
    return out, peak, total


def put(ref, merged):
    out, peak, total = merged
    ref[..., :KVL] = out.astype(BF16).reshape(2, 16, KVL)
    ref[..., KVL:] = aux_lanes(peak, total).astype(BF16).reshape(2, 16, QPAD - KVL)


def kernel(
    q_ref, cache_ref, vup_ref, wout_ref, resid_ref, gain_ref, wg_ref, wu_ref, wd_ref, out_ref,
    qbuf, kv, score_a, score_b, prob_a, prob_b, oscr, msg, rx1, rx2, rx3, fin, rxz, lat, fac,
    vup, wout, wg, wu, wd, heads, pbuf, rxa, ebuf, rxb, zbuf, rxc, hid, hidf,
    sq, rxs, gs, rxg, units, part_buf, rxq, ybuf, rxy, wbuf, rxw, fo,
    send_sems, recv_sems, local_sems,
):
    g, c, x, y, z = place()
    up = lambda v, d: lax.rem(v + d, 4)

    def at(px, py, pz):
        return (g, (px * 4 + py) * 2 + pz)

    xs = [x] + [up(x, d) for d in (1, 2, 3)]
    ys = [y] + [up(y, d) for d in (1, 2, 3)]
    to_x = [None] + [at(xs[d], y, z) for d in (1, 2, 3)]
    to_y = [None] + [at(x, ys[d], z) for d in (1, 2, 3)]
    partner = (lax.rem(g + 2, 4), (x * 4 + y) * 2 + (1 - z))
    far = at(x, y, 1 - z)
    gs_of = [g] + [up(g, d) for d in (1, 2, 3)]
    mates = [None] + [(gs_of[d], c) for d in (1, 2, 3)]
    columns = pl.ds(pl.multiple_of(g * QUARTER, 128), QUARTER)
    pairs = [(q_ref.at[s], qbuf.at[s, x, y, z]) for s in range(SEQS)]
    pairs += [(cache_ref.at[s], kv.at[s, pl.ds(0, QK)]) for s in range(SEQS)]
    pairs += [
        (vup_ref.at[g], vup),
        (wout_ref.at[:, columns], wout),
        (wg_ref.at[0], wg),
        (wu_ref.at[0], wu),
        (wd_ref.at[0], wd),
    ]
    loads = [
        pltpu.make_async_copy(src, dst, local_sems.at[n]) for n, (src, dst) in enumerate(pairs)
    ]
    for copy in loads:
        copy.start()

    greet(
        to_x[1:] + to_y[1:] + mates[1:] + [partner, far]
    )
    wire = Wire(send_sems, recv_sems)

    dirs = (1, 3)
    other = 1 - z

    def gather_0(s):
        return [wire.push((q_ref, s), (qbuf, s, x, y, z), partner)]

    def gather_1(s, copies):
        arrive(copies)
        copies = []
        for d in dirs:
            ref = (qbuf, s, x, y, 0)
            copies.append(wire.push(ref, ref, to_x[d]))
            ref = (qbuf, s, x, y, 1)
            copies.append(wire.push(ref, ref, to_y[d]))
        return copies

    def gather_2(s, copies):
        arrive(copies)
        copies = []
        for k, d in enumerate(dirs):
            ref = (qbuf, s, xs[4 - d], y, 0, k)
            copies.append(wire.push(ref, ref, to_x[d]))
            ref = (qbuf, s, x, ys[4 - d], 1, k)
            copies.append(wire.push(ref, ref, to_y[d]))
        return copies

    def gather_3(s, copies):
        arrive(copies)
        copies = []
        for d in dirs:
            ref = (qbuf, s, slice(None), y, 0)
            copies.append(wire.push(ref, ref, to_y[d]))
            ref = (qbuf, s, x, slice(None), 1)
            copies.append(wire.push(ref, ref, to_x[d]))
        return copies

    def gather_4(s, copies):
        arrive(copies)
        copies = []
        for k, d in enumerate(dirs):
            ref = (qbuf, s, pl.ds(2 * k, 2), ys[4 - d], 0)
            copies.append(wire.push(ref, ref, to_y[d]))
            ref = (qbuf, s, xs[4 - d], pl.ds(2 * k, 2), 1)
            copies.append(wire.push(ref, ref, to_x[d]))
        return copies

    def scores(s, half, part, score):
        q = qbuf[s, 2 * part : 2 * part + 2, :, :, half].reshape(256, QPAD)
        for n in range(4):
            keys = pl.ds(n * 512, 512)
            value = mm(q, kv[s, :, keys])
            if n < 3:
                score[:, keys] = value
            else:
                score[:, 1536:1920] = value[:, :384]
                row = 16 * part + iota((256, 128), 0) // 16
                position = c * CTX_DEV + 1920 + iota((256, 128), 1)
                score[:, 1920:] = jnp.where(
                    position <= CTX - QROWS + row, value[:, 384:], -1e30
                )

    def weigh(s, half, part, score, prob):
        peak = jnp.max(score[...], axis=-1, keepdims=True).astype(BF16).astype(F32)
        total = jnp.zeros((256, 128), F32)
        for n in range(4):
            keys = pl.ds(n * 512, 512)
            weight = jnp.exp2((score[:, keys] - peak) * SCALE2)
            for m in range(4):
                total = total + weight[:, m * 128 : (m + 1) * 128]
            prob[:, keys] = weight.astype(BF16)
        total = jnp.sum(total, axis=-1, keepdims=True)
        out = mm_nt(prob[...], kv[s, :KVL, :])
        for m in range(4):
            oscr[part, m] = out[:, m * 128 : (m + 1) * 128]
        oscr[part, 4] = aux_lanes(peak, total)
        for n in range(16):
            a, b = (n // 4, n % 4) if part == 0 else (n % 4, n // 4)
            for m in range(5):
                lanes = pl.ds(m * 128, 128)
                msg[s, part, a, b, half, :, lanes] = oscr[
                    part, m, pl.ds(n, 16, stride=16), :
                ].astype(BF16)

    def attend(t):
        s, half = t // 2, t % 2
        scores(s, half, 0, score_a)
        scores(s, half, 1, score_b)
        weigh(s, half, 0, score_a, prob_a)
        weigh(s, half, 1, score_b, prob_b)

    axes = [(xs, ys, to_x, to_y), (ys, xs, to_y, to_x)]

    def reduce_1(s):
        copies = []
        for part, (fs, es, to_f, to_e) in enumerate(axes):
            for k, d in enumerate(dirs):
                src = (msg, s, part, fs[2], pl.ds(2 * k, 2))
                copies.append(wire.push(src, (rx1, s, part, k), to_f[d]))
        return copies

    def reduce_2(s, copies):
        arrive(copies)
        copies = []
        for part, (fs, es, to_f, to_e) in enumerate(axes):
            for k, d in enumerate(dirs):

                @pl.loop(0, 2)
                def _(j):
                    put(
                        msg.at[s, part, fs[d], 2 * k + j],
                        merge([msg[s, part, fs[d], 2 * k + j], rx1[s, part, k, j]]),
                    )

                copies.append(wire.push((msg, s, part, fs[d]), (rx2, s, part, k), to_f[d]))
        return copies

    def reduce_3(s, copies):
        arrive(copies)
        copies = []
        for part, (fs, es, to_f, to_e) in enumerate(axes):

            @pl.loop(0, 4)
            def _(j):
                put(
                    msg.at[s, part, fs[0], j],
                    merge([msg[s, part, fs[0], j], rx2[s, part, 0, j], rx2[s, part, 1, j]]),
                )

            for d in (1, 2, 3):
                src = (msg, s, part, fs[0], es[d])
                copies.append(wire.push(src, (rx3, s, part, d - 1), to_e[d]))
        return copies

    def reduce_4(s, copies):
        arrive(copies)
        for part, (fs, es, to_f, to_e) in enumerate(axes):
            out, peak, total = merge(
                [msg[s, part, fs[0], es[0]]] + [rx3[s, part, d] for d in range(3)]
            )
            fin[s, :, part, :, :KVL] = out.astype(BF16).reshape(2, 16, KVL)
            fin[s, :, part, :, KVL:] = aux_lanes(peak, total).astype(BF16).reshape(
                2, 16, QPAD - KVL
            )
        return [wire.push((fin, s, other), (rxz, s), partner)]

    def reduce_5(s, copies):
        arrive(copies)
        out, peak, total = merge([fin[s, z], rxz[s]])
        lat[s * QROWS : (s + 1) * QROWS, :] = (out / total).astype(BF16)

    zs = [gather_0(s) for s in range(SEQS)]
    for copy in loads[:3]:
        copy.wait()
    got = [None] * SEQS
    got[0] = gather_1(0, zs[0])
    kv[:, QK:, :] = jnp.zeros((SEQS, QPAD - QK, CTX_DEV), BF16)
    got[0] = gather_2(0, got[0])
    got[0] = gather_3(0, got[0])
    got[1] = gather_1(1, zs[1])
    got[0] = gather_4(0, got[0])
    got[1] = gather_2(1, got[1])
    for copy in loads[3:6]:
        copy.wait()
    arrive(got[0])
    got[1] = gather_3(1, got[1])
    red = [None] * SEQS

    @pl.loop(0, 6)
    def _(t):
        @pl.when(t == 1)
        def _():
            got[1] = gather_4(1, got[1])
            got[2] = gather_1(2, zs[2])
            got[2] = gather_2(2, got[2])

        @pl.when(t == 2)
        def _():
            arrive(got[1])
            got[2] = gather_3(2, got[2])
            red[0] = reduce_1(0)

        @pl.when(t == 3)
        def _():
            got[2] = gather_4(2, got[2])
            red[0] = reduce_2(0, red[0])

        @pl.when(t == 4)
        def _():
            arrive(got[2])
            red[0] = reduce_3(0, red[0])
            red[1] = reduce_1(1)

        @pl.when(t == 5)
        def _():
            red[0] = reduce_4(0, red[0])
            red[1] = reduce_2(1, red[1])

        attend(t)

    red[2] = reduce_1(2)
    red[1] = reduce_3(1, red[1])
    red[2] = reduce_2(2, red[2])
    red[1] = reduce_4(1, red[1])
    red[2] = reduce_3(2, red[2])

    for part in range(2):
        picked = jnp.zeros((128, 128), F32)
        for s in range(SEQS):
            seq, row = padded_row((128, 512), 0, part)
            j = iota((128, 512), 1)
            pick = ((seq == s) & (j == row * 16)).astype(F32).astype(BF16)
            picked = picked + mm(pick, qbuf[s, :, :, :, 0, :, KVL:].reshape(512, 128))
        lane = iota((128, 128), 1)
        chosen = jnp.sum(
            jnp.where(lane == QK - KVL + c // SPLIT, picked, 0.0), axis=-1, keepdims=True
        )
        fac[part] = jnp.broadcast_to(chosen, (128, 128))

    red[2] = reduce_4(2, red[2])
    for s in range(SEQS):
        reduce_5(s, red[s])

    loads[6].wait()
    heads[g] = mm(lat[...], vup[...]).astype(BF16)
    copies = [wire.push((heads, g), (heads, g), mates[d]) for d in (1, 2, 3)]
    spread, gathered = [], []
    for part in range(2):
        seq, row = padded_row((128, 96), 0, part)
        j = iota((128, 96), 1)
        spread.append(
            ((seq < SEQS) & (j == seq * QROWS + row)).astype(F32).astype(BF16)
        )
        seq, row = padded_row((96, 128), 1, part)
        j = iota((96, 128), 0)
        gathered.append(
            ((seq < SEQS) & (j == seq * QROWS + row)).astype(F32).astype(BF16)
        )
    arrive(copies)
    loads[7].wait()
    for part in range(2):
        cols = pl.ds(part * HALF, HALF)
        seq, row = padded_row((128, 16), 0, part)
        mine = ((row == c) & (seq == iota((128, 16), 1)) & (seq < SEQS)).astype(F32).astype(BF16)
        value = mm(mine, resid_ref[:, cols])
        for k in range(4):
            rows = mm(spread[part], heads[k]).astype(BF16)
            value = value + mm(rows, wout[k * DV : (k + 1) * DV, cols])
        pbuf[part] = value.astype(BF16).reshape(4, 32, HALF)

    def scatter(source, landing):
        copies = []
        for part, (fs, es, to_f, to_e) in enumerate(axes):
            for d in (1, 2, 3):
                copies.append(wire.push((source, part, fs[d]), (landing, part, d - 1), to_f[d]))
        return copies

    def summed(first, landing, part):
        value = first.astype(F32)
        for d in range(3):
            value = value + landing[part, d].astype(F32)
        return value

    copies = scatter(pbuf, rxa)
    arrive(copies)
    copies = []
    for part, (fs, es, to_f, to_e) in enumerate(axes):
        ebuf[part] = summed(pbuf[part, fs[0]], rxa, part).astype(BF16)
        for d in (1, 2, 3):
            copies.append(wire.push((ebuf, part), (rxb, part, d - 1), to_e[d]))
    arrive(copies)
    for part in range(2):
        zbuf[part] = summed(ebuf[part], rxb, part).astype(BF16)
    copy = wire.push((zbuf,), (rxc,), far)
    copy.wait_recv()
    copies = []
    for part, (fs, es, to_f, to_e) in enumerate(axes):
        value = (zbuf[part].astype(F32) + rxc[part].astype(F32)).astype(BF16)
        hid[part, fs[0]] = value
        hidf[part] = value.astype(F32).reshape(4, 8, HALF)
        for d in (1, 2, 3):
            ref = (hid, part, fs[0])
            copies.append(wire.push(ref, ref, to_f[d]))
    arrive(copies)

    loads[8].wait()
    loads[9].wait()
    eye = iota((96, 128), 0) == iota((96, 128), 1)
    squares = jnp.zeros((96, 1), F32)
    gate = jnp.zeros((96, 512), F32)
    rise = jnp.zeros((96, 512), F32)
    for part in range(2):
        rows = mm(gathered[part], hid[part].reshape(128, HALF))
        squares = squares + jnp.sum(rows * rows, axis=-1, keepdims=True)
        cols = pl.ds(part * HALF, HALF)
        scaled = (rows * gain_ref[0:1, cols]).astype(BF16)
        gate = gate + mm(scaled, wg[cols, :])
        rise = rise + mm(scaled, wu[cols, :])
    sq[...] = jnp.broadcast_to(
        jnp.sum(jnp.where(eye, squares, 0.0), axis=0, keepdims=True), (8, 128)
    )
    for j in range(4):
        gs[j, :, :128] = gate[:, j * 128 : (j + 1) * 128].astype(BF16)
        gs[j, :, 128:] = rise[:, j * 128 : (j + 1) * 128].astype(BF16)
    copies = []
    for d in (1, 2, 3):
        copies.append(wire.push((sq,), (rxs, d - 1), mates[d]))
        copies.append(wire.push((gs, gs_of[d]), (rxg, d - 1), mates[d]))
    arrive(copies)
    both = gs[g].astype(F32)
    total = sq[0:1, :]
    for d in range(3):
        both = both + rxg[d].astype(F32)
        total = total + rxs[d, 0:1, :]
    total = jnp.sum(jnp.where(eye, total, 0.0), axis=-1, keepdims=True)
    both = both * lax.rsqrt(total * (1.0 / D) + 1e-06)
    gate, rise = both[:, :128], both[:, 128:]
    units[g] = (gate / (1.0 + jnp.exp(-gate)) * rise).astype(BF16)
    copies = [wire.push((units, g), (units, g), mates[d]) for d in (1, 2, 3)]
    arrive(copies)
    loads[10].wait()
    for part in range(2):
        cols = pl.ds(part * HALF, HALF)
        value = jnp.zeros((128, HALF), F32)
        for k in range(4):
            rows = mm(spread[part], units[k]).astype(BF16)
            value = value + mm(rows, wd[k * 128 : (k + 1) * 128, cols])
        value = value.astype(BF16).astype(F32) * fac[part, :, 0:1]
        part_buf[part] = value.astype(BF16).reshape(4, 32, HALF)
    copies = scatter(part_buf, rxq)
    arrive(copies)
    copies = []
    for part, (fs, es, to_f, to_e) in enumerate(axes):
        ybuf[part] = summed(part_buf[part, fs[0]], rxq, part).reshape(4, 8, HALF)
        for d in (1, 2, 3):
            copies.append(wire.push((ybuf, part, es[d]), (rxy, part, d - 1), to_e[d]))
    arrive(copies)
    for part, (fs, es, to_f, to_e) in enumerate(axes):
        wbuf[part] = summed(ybuf[part, es[0]], rxy, part)
    copy = wire.push((wbuf,), (rxw,), far)
    copy.wait_recv()
    for part, (fs, es, to_f, to_e) in enumerate(axes):
        value = hidf[part, es[0]] + (wbuf[part] + rxw[part])
        fo[g, part * 4 : (part + 1) * 4, :] = jnp.where(z == 0, value[0:4], value[4:8])
    copies = [wire.push((fo, g), (fo, g), mates[d]) for d in (1, 2, 3)]
    arrive(copies)
    for k in range(4):
        for part in range(2):
            at_ = k * QUARTER + part * HALF
            out_ref[:, at_ : at_ + HALF] = fo[k, part * 4 : part * 4 + SEQS, :].astype(BF16)
    wire.finish()


def vmem():
    return pl.BlockSpec(memory_space=pltpu.VMEM)


def hbm():
    return pl.BlockSpec(memory_space=pl.ANY)


def on_device(
    queries, cache, value_up_weight, w_out, resid, norm_gain, routes, route_weight,
    w_gate, w_up, w_down,
):
    g, c, x, y, z = place()
    pair, core = lax.rem(g // 2 + z, 2), g % 2
    by_column = queries.reshape(SEQS, 16, 8, QK)
    lower = lax.dynamic_index_in_dim(by_column, 2 * pair + core, 2, keepdims=False)
    upper = lax.dynamic_index_in_dim(by_column, 4 + 2 * (1 - pair) + core, 2, keepdims=False)
    matches = routes[:, 0, :, None] == jnp.arange(EXPERTS, dtype=jnp.int32)
    weights = jnp.sum(
        jnp.where(matches, route_weight[:, 0, :, None].astype(F32), 0.0), axis=1
    ).astype(BF16)
    spare = jnp.pad(weights, ((0, 0), (0, QPAD - QK - EXPERTS)))
    spare = jnp.broadcast_to(spare[:, None, None, :], (SEQS, 2, 16, QPAD - QK))
    rows = jnp.concatenate([jnp.stack([lower, upper], axis=1), spare], axis=-1)

    own_resid = lax.dynamic_slice_in_dim(resid[:, 0], g * QUARTER, QUARTER, 1)
    own_resid = jnp.pad(own_resid, ((0, 16 - SEQS), (0, 0)))
    own_gain = lax.dynamic_slice_in_dim(norm_gain, g * QUARTER, QUARTER, 0)
    own_gain = jnp.broadcast_to(own_gain[None], (8, QUARTER))
    mixed = pl.pallas_call(
        kernel,
        out_shape=jax.ShapeDtypeStruct((SEQS, D), BF16),
        in_specs=[vmem(), hbm(), hbm(), hbm(), vmem(), vmem(), hbm(), hbm(), hbm()],
        out_specs=vmem(),
        scratch_shapes=[
            pltpu.VMEM((SEQS, 4, 4, 2, 2, 16, QPAD), BF16),
            pltpu.VMEM((SEQS, QPAD, CTX_DEV), BF16),
            pltpu.VMEM((256, CTX_DEV), F32),
            pltpu.VMEM((256, CTX_DEV), F32),
            pltpu.VMEM((256, CTX_DEV), BF16),
            pltpu.VMEM((256, CTX_DEV), BF16),
            pltpu.VMEM((2, 5, 256, 128), F32),
            pltpu.VMEM((SEQS, 2, 4, 4, 2, 16, QPAD), BF16),
            pltpu.VMEM((SEQS, 2, 2, 2, 2, 16, QPAD), BF16),
            pltpu.VMEM((SEQS, 2, 2, 4, 2, 16, QPAD), BF16),
            pltpu.VMEM((SEQS, 2, 3, 2, 16, QPAD), BF16),
            pltpu.VMEM((SEQS, 2, 2, 16, QPAD), BF16),
            pltpu.VMEM((SEQS, 2, 16, QPAD), BF16),
            pltpu.VMEM((96, KVL), BF16),
            pltpu.VMEM((2, 128, 128), F32),
            pltpu.VMEM((KVL, DV), BF16),
            pltpu.VMEM((512, QUARTER), BF16),
            pltpu.VMEM((QUARTER, 512), BF16),
            pltpu.VMEM((QUARTER, 512), BF16),
            pltpu.VMEM((512, QUARTER), BF16),
            pltpu.VMEM((4, 96, DV), BF16),
            pltpu.VMEM((2, 4, 32, HALF), BF16),
            pltpu.VMEM((2, 3, 32, HALF), BF16),
            pltpu.VMEM((2, 32, HALF), BF16),
            pltpu.VMEM((2, 3, 32, HALF), BF16),
            pltpu.VMEM((2, 32, HALF), BF16),
            pltpu.VMEM((2, 32, HALF), BF16),
            pltpu.VMEM((2, 4, 32, HALF), BF16),
            pltpu.VMEM((2, 4, 8, HALF), F32),
            pltpu.VMEM((8, 128), F32),
            pltpu.VMEM((3, 8, 128), F32),
            pltpu.VMEM((4, 96, 256), BF16),
            pltpu.VMEM((3, 96, 256), BF16),
            pltpu.VMEM((4, 96, 128), BF16),
            pltpu.VMEM((2, 4, 32, HALF), BF16),
            pltpu.VMEM((2, 3, 32, HALF), BF16),
            pltpu.VMEM((2, 4, 8, HALF), F32),
            pltpu.VMEM((2, 3, 8, HALF), F32),
            pltpu.VMEM((2, 8, HALF), F32),
            pltpu.VMEM((2, 8, HALF), F32),
            pltpu.VMEM((4, 8, HALF), F32),
            pltpu.SemaphoreType.DMA((160,)),
            pltpu.SemaphoreType.DMA((160,)),
            pltpu.SemaphoreType.DMA((11,)),
        ],
        compiler_params=pltpu.CompilerParams(
            collective_id=0, has_side_effects=True, vmem_limit_bytes=60 * 1024 * 1024
        ),
    )(rows, jnp.swapaxes(cache, 1, 2), value_up_weight, w_out, own_resid, own_gain, w_gate, w_up, w_down)
    return mixed.reshape(SEQS, 1, D)


def solution(mesh):
    placed = (
        P(None, "cp", None),
        P(None, "cp", None),
        P("cp", None, None),
        P("cp", None),
        P(None, "cp", None),
        P(),
        P(None, "cp", None),
        P(None, "cp", None),
        P("cp", "grp", None),
        P("cp", "grp", None),
        P("cp", None, "grp"),
    )
    return jax.shard_map(
        on_device, mesh=mesh, in_specs=placed, out_specs=P(None, "cp", None), check_vma=False
    )
```

```python
import math

import jax
import jax.numpy as jnp
from jax import lax
from jax.experimental import pallas as pl
from jax.experimental.pallas import tpu as pltpu
from jax.sharding import PartitionSpec as P

D = 7168
KVL = 512
DV = 128
SPLIT = 4
QROWS = 32
CTX_DEV = 2048
QK = 576
QPAD = 640
SEQS = 3
EXPERTS = 8
QUARTER = D // 4
HALF = QUARTER // 2
N_CP = 32
CTX = CTX_DEV * N_CP

SCALE = 192.0 ** (-0.5)
SCALE2 = SCALE * math.log2(math.e)
MESH = pl.DeviceIdType.MESH
F32 = jnp.float32
BF16 = jnp.bfloat16


def place():
    g = lax.axis_index("grp")
    c = lax.axis_index("cp")
    return g, c, c // 8, (c // 2) % 4, c % 2


def mm(a, b):
    return jnp.dot(a, b, preferred_element_type=F32)


def mm_nt(a, b):
    return lax.dot_general(a, b, (((1,), (1,)), ((), ())), preferred_element_type=F32)


def iota(shape, axis):
    return lax.broadcasted_iota(jnp.int32, shape, axis)


def part_of(ref, *index):
    return ref.at[index] if index else ref


class Wire:
    def __init__(self, send_sems, recv_sems):
        self.send_sems, self.recv_sems = send_sems, recv_sems
        self.started = []

    def push(self, src, dst, device):
        copy = Copy(self, len(self.started), src, dst, device)
        self.started.append(copy)
        copy.make().start()
        return copy

    def finish(self):
        for copy in self.started:
            copy.make().wait_send()


class Copy:
    def __init__(self, wire, at, src, dst, device):
        self.wire, self.at, self.src, self.dst, self.device = wire, at, src, dst, device

    def make(self):
        return pltpu.make_async_remote_copy(
            src_ref=part_of(*self.src),
            dst_ref=part_of(*self.dst),
            send_sem=self.wire.send_sems.at[self.at],
            recv_sem=self.wire.recv_sems.at[self.at],
            device_id=self.device,
            device_id_type=MESH,
        )

    def wait_recv(self):
        self.make().wait_recv()


def arrive(copies):
    for copy in copies:
        copy.wait_recv()


def greet(peers):
    barrier = pltpu.get_barrier_semaphore()
    for peer in peers:
        pl.semaphore_signal(barrier, inc=1, device_id=peer, device_id_type=MESH)
    pl.semaphore_wait(barrier, len(peers))


def padded_row(shape, axis, part):
    r = iota(shape, axis)
    s, z, b, a = r % 4, (r // 4) % 2, (r // 8) % 4, r // 32
    x, y = (a, b) if part == 0 else (b, a)
    return s, (x * 4 + y) * 2 + z


def unpack(value):
    value = value.reshape(-1, QPAD).astype(F32)
    aux = value[:, KVL:]
    lane = iota(aux.shape, 1)
    peak = jnp.sum(jnp.where(lane == 0, aux, 0.0), axis=-1, keepdims=True)
    total = jnp.sum(jnp.where((lane == 1) | (lane == 2), aux, 0.0), axis=-1, keepdims=True)
    return value[:, :KVL], peak, total


def aux_lanes(peak, total):
    lane = iota((peak.shape[0], QPAD - KVL), 1)
    high = total.astype(BF16).astype(F32)
    low = total - high
    return jnp.where(
        lane == 0, peak, jnp.where(lane == 1, high, jnp.where(lane == 2, low, 0.0))
    )


def merge(values):
    items = [unpack(value) for value in values]
    peak = items[0][1]
    for item in items[1:]:
        peak = jnp.maximum(peak, item[1])
    out, total = None, None
    for item in items:
        factor = jnp.exp((item[1] - peak) * SCALE)
        if out is None:
            out, total = item[0] * factor, item[2] * factor
        else:
            out, total = out + item[0] * factor, total + item[2] * factor
    return out, peak, total


def put(ref, merged):
    out, peak, total = merged
    ref[..., :KVL] = out.astype(BF16).reshape(*ref.shape[:-1], KVL)
    ref[..., KVL:] = aux_lanes(peak, total).astype(BF16).reshape(*ref.shape[:-1], QPAD - KVL)


def kernel(
    q_ref, cache_ref, vup_ref, wout_ref, resid_ref, gain_ref, routes_ref, weight_ref,
    wg_ref, wu_ref, wd_ref, out_ref,
    qbuf, kv, score_a, score_b, prob_a, prob_b, oscr, msg, rx1, rx2, rx3, fin, rxz, lat,
    vup, wout, wg, wu, wd, own_resid, heads, pbuf, rxa, ebuf, rxb, zbuf, rxc, hid, hidf,
    sq, rxs, gs, rxg, units, part_buf, rxq, ybuf, rxy, wbuf, rxw, fo,
    send_sems, recv_sems, local_sems,
):
    g, c, x, y, z = place()
    up = lambda v, d: lax.rem(v + d, 4)

    def at(px, py, pz):
        return (g, (px * 4 + py) * 2 + pz)

    xs = [x] + [up(x, d) for d in (1, 2, 3)]
    ys = [y] + [up(y, d) for d in (1, 2, 3)]
    to_x = [None] + [at(xs[d], y, z) for d in (1, 2, 3)]
    to_y = [None] + [at(x, ys[d], z) for d in (1, 2, 3)]
    partner = (lax.rem(g + 2, 4), (x * 4 + y) * 2 + (1 - z))
    far = at(x, y, 1 - z)
    gs_of = [g] + [up(g, d) for d in (1, 2, 3)]
    mates = [None] + [(gs_of[d], c) for d in (1, 2, 3)]
    columns = pl.ds(pl.multiple_of(g * QUARTER, 128), QUARTER)
    pairs = [(q_ref, qbuf.at[:, x, y, z])]
    pairs += [(cache_ref.at[s], kv.at[s, pl.ds(0, QK)]) for s in range(SEQS)]
    pairs += [
        (vup_ref.at[g], vup),
        (wout_ref.at[:, columns], wout),
        (wg_ref.at[0], wg),
        (wu_ref.at[0], wu),
        (wd_ref.at[0], wd),
    ]
    loads = [
        pltpu.make_async_copy(src, dst, local_sems.at[n]) for n, (src, dst) in enumerate(pairs)
    ]
    for copy in loads:
        copy.start()

    greet(
        to_x[1:] + to_y[1:] + mates[1:] + [partner, far]
    )
    wire = Wire(send_sems, recv_sems)

    chunks = [(0, 2), (2, 2), (4, 2)]
    dirs = (1, 3)
    other = 1 - z

    def gather_0(k, _):
        span = pl.ds(*chunks[k])
        return [wire.push((q_ref, span), (qbuf, span, x, y, z), partner)]

    def gather_1(k, copies):
        arrive(copies)
        span = pl.ds(*chunks[k])
        copies = []
        for d in (1, 2, 3):
            ref = (qbuf, span, x, y, 0)
            copies.append(wire.push(ref, ref, to_x[d]))
            ref = (qbuf, span, x, y, 1)
            copies.append(wire.push(ref, ref, to_y[d]))
        return copies

    def gather_3(k, copies):
        arrive(copies)
        span = pl.ds(*chunks[k])
        copies = []
        for d in dirs:
            ref = (qbuf, span, slice(None), y, 0)
            copies.append(wire.push(ref, ref, to_y[d]))
            ref = (qbuf, span, x, slice(None), 1)
            copies.append(wire.push(ref, ref, to_x[d]))
        return copies

    def gather_4(k, copies):
        arrive(copies)
        span = pl.ds(*chunks[k])
        copies = []
        for n, d in enumerate(dirs):
            ref = (qbuf, span, pl.ds(2 * n, 2), ys[4 - d], 0)
            copies.append(wire.push(ref, ref, to_y[d]))
            ref = (qbuf, span, xs[4 - d], pl.ds(2 * n, 2), 1)
            copies.append(wire.push(ref, ref, to_x[d]))
        return copies

    def gather_5(k, copies):
        arrive(copies)

    def scores(t, s, part, score):
        q = qbuf[t, 2 * part : 2 * part + 2].reshape(256, QPAD)
        for n in range(4):
            keys = pl.ds(n * 512, 512)
            value = mm(q, kv[s, :, keys])
            if n < 3:
                score[:, keys] = value
            else:
                score[:, 1536:1920] = value[:, :384]
                row = 16 * part + iota((256, 128), 0) // 16
                position = c * CTX_DEV + 1920 + iota((256, 128), 1)
                score[:, 1920:] = jnp.where(
                    position <= CTX - QROWS + row, value[:, 384:], -1e30
                )

    def weigh(t, s, part, score, prob):
        peak = jnp.max(score[...], axis=-1, keepdims=True).astype(BF16).astype(F32)
        total = jnp.zeros((256, 128), F32)
        for n in range(4):
            keys = pl.ds(n * 512, 512)
            weight = jnp.exp2((score[:, keys] - peak) * SCALE2)
            for m in range(4):
                total = total + weight[:, m * 128 : (m + 1) * 128]
            prob[:, keys] = weight.astype(BF16)
        total = jnp.sum(total, axis=-1, keepdims=True)
        out = mm_nt(prob[...], kv[s, :KVL, :])
        for m in range(4):
            oscr[part, m] = out[:, m * 128 : (m + 1) * 128]
        oscr[part, 4] = aux_lanes(peak, total)
        for n in range(16):
            a, b = (n // 4, n % 4) if part == 0 else (n % 4, n // 4)
            for m in range(5):
                lanes = pl.ds(m * 128, 128)
                msg[t, part, a, b, :, lanes] = oscr[
                    part, m, pl.ds(n, 16, stride=16), :
                ].astype(BF16)

    def attend(t):
        s = t // 2
        scores(t, s, 0, score_a)
        scores(t, s, 1, score_b)
        weigh(t, s, 0, score_a, prob_a)
        weigh(t, s, 1, score_b, prob_b)

    axes = [(xs, ys, to_x, to_y), (ys, xs, to_y, to_x)]

    def reduce_1(k, _):
        span = pl.ds(*chunks[k])
        copies = []
        for part, (fs, es, to_f, to_e) in enumerate(axes):
            for n, d in enumerate(dirs):
                src = (msg, span, part, fs[2], pl.ds(2 * n, 2))
                copies.append(wire.push(src, (rx1, span, part, n), to_f[d]))
        return copies

    def reduce_2(k, copies):
        arrive(copies)
        span = pl.ds(*chunks[k])
        copies = []
        for part, (fs, es, to_f, to_e) in enumerate(axes):
            for n, d in enumerate(dirs):

                @pl.loop(chunks[k][0], sum(chunks[k]))
                def _(t):
                    ref = msg.at[t, part, fs[d], pl.ds(2 * n, 2)]
                    put(ref, merge([ref[...], rx1[t, part, n]]))

                copies.append(
                    wire.push((msg, span, part, fs[d]), (rx2, span, part, n), to_f[d])
                )
        return copies

    def reduce_3(k, copies):
        arrive(copies)
        span = pl.ds(*chunks[k])
        copies = []
        for part, (fs, es, to_f, to_e) in enumerate(axes):

            @pl.loop(2 * chunks[k][0], 2 * sum(chunks[k]))
            def _(at_):
                t, units = at_ // 2, pl.ds(2 * (at_ % 2), 2)
                ref = msg.at[t, part, fs[0], units]
                put(ref, merge([ref[...], rx2[t, part, 0, units], rx2[t, part, 1, units]]))

            for d in (1, 2, 3):
                src = (msg, span, part, fs[0], es[d])
                copies.append(wire.push(src, (rx3, span, part, d - 1), to_e[d]))
        return copies

    def reduce_4(k, copies):
        arrive(copies)

        @pl.loop(chunks[k][0], sum(chunks[k]))
        def _(t):
            for part, (fs, es, to_f, to_e) in enumerate(axes):
                put(
                    fin.at[t, part],
                    merge([msg[t, part, fs[0], es[0]]] + [rx3[t, part, d] for d in range(3)]),
                )

        done = [t // 2 for t in range(chunks[k][0], sum(chunks[k])) if t % 2]
        return [(s, wire.push((fin, 2 * s + other), (rxz, s), partner)) for s in done]

    def reduce_5(k, copies):
        for s, copy in copies:
            copy.wait_recv()
            out, peak, total = merge([fin[2 * s + z], rxz[s]])
            lat[s * QROWS : (s + 1) * QROWS, :] = (out / total).astype(BF16)

    state = [None] * len(chunks)

    def run(steps):
        for step, k in steps:
            state[k] = step(k, state[k])

    loads[0].wait()
    run([(gather_0, 0)])
    kv[:, QK:, :] = jnp.zeros((SEQS, QPAD - QK, CTX_DEV), BF16)
    run([(gather_1, 0), (gather_0, 1), (gather_3, 0), (gather_1, 1), (gather_0, 2)])
    run([(gather_1, 2), (gather_4, 0), (gather_3, 1), (gather_3, 2)])
    for copy in loads[1:4]:
        copy.wait()
    run([(gather_5, 0)])
    between = {
        1: [(gather_4, 1)],
        2: [(gather_4, 2), (reduce_1, 0), (gather_5, 1)],
        3: [],
        4: [(gather_5, 2), (reduce_1, 1), (reduce_2, 0)],
        5: [(reduce_2, 1)],
    }

    @pl.loop(0, 6)
    def _(t):
        for at_, steps in between.items():
            if steps:

                @pl.when(t == at_)
                def _():
                    run(steps)

        attend(t)

    run([(reduce_1, 2), (reduce_3, 0), (reduce_3, 1), (reduce_2, 2), (reduce_4, 0), (reduce_4, 1)])
    run([(reduce_5, 0), (reduce_3, 2), (reduce_5, 1), (reduce_4, 2), (reduce_5, 2)])

    loads[4].wait()
    heads[g] = mm(lat[...], vup[...]).astype(BF16)
    copies = [wire.push((heads, g), (heads, g), mates[d]) for d in (1, 2, 3)]
    spread, gathered = [], []
    for part in range(2):
        seq, row = padded_row((128, 96), 0, part)
        j = iota((128, 96), 1)
        spread.append(
            ((seq < SEQS) & (j == seq * QROWS + row)).astype(F32).astype(BF16)
        )
        seq, row = padded_row((96, 128), 1, part)
        j = iota((96, 128), 0)
        gathered.append(
            ((seq < SEQS) & (j == seq * QROWS + row)).astype(F32).astype(BF16)
        )
    arrive(copies)
    loads[5].wait()
    own_resid[...] = jnp.zeros((16, QUARTER), BF16)
    own_resid[0:SEQS, :] = resid_ref[0, :, columns]
    lane = iota((1, 128), 1)
    gates = jnp.zeros((1, 128), F32)
    for s in range(SEQS):
        for r in range(4):
            here = lane == s * EXPERTS + routes_ref[s, :, r : r + 1]
            gates = gates + jnp.where(here, weight_ref[0, s : s + 1, r : r + 1].astype(F32), 0.0)
    for part in range(2):
        cols = pl.ds(part * HALF, HALF)
        seq, row = padded_row((128, 16), 0, part)
        mine = ((row == c) & (seq == iota((128, 16), 1)) & (seq < SEQS)).astype(F32).astype(BF16)
        value = mm(mine, own_resid[:, cols])
        for k in range(4):
            rows = mm(spread[part], heads[k]).astype(BF16)
            value = value + mm(rows, wout[k * DV : (k + 1) * DV, cols])
        pbuf[part] = value.astype(BF16).reshape(4, 32, HALF)
        if part == 0:
            seq, row = padded_row((128, 128), 0, part)
            head = jnp.where((seq == SEQS) & (row == c), gates, value[:, :128])
            pbuf[part, :, :, :128] = head.astype(BF16).reshape(4, 32, 128)

    def scatter(source, landing):
        copies = []
        for part, (fs, es, to_f, to_e) in enumerate(axes):
            for d in (1, 2, 3):
                copies.append(wire.push((source, part, fs[d]), (landing, part, d - 1), to_f[d]))
        return copies

    def summed(first, landing, part):
        value = first.astype(F32)
        for d in range(3):
            value = value + landing[part, d].astype(F32)
        return value

    copies = scatter(pbuf, rxa)
    arrive(copies)
    copies = []
    for part, (fs, es, to_f, to_e) in enumerate(axes):
        ebuf[part] = summed(pbuf[part, fs[0]], rxa, part).astype(BF16)
        for d in (1, 2, 3):
            copies.append(wire.push((ebuf, part), (rxb, part, d - 1), to_e[d]))
    arrive(copies)
    for part in range(2):
        zbuf[part] = summed(ebuf[part], rxb, part).astype(BF16)
    copy = wire.push((zbuf,), (rxc,), far)
    copy.wait_recv()
    copies = []
    for part, (fs, es, to_f, to_e) in enumerate(axes):
        value = (zbuf[part].astype(F32) + rxc[part].astype(F32)).astype(BF16)
        hid[part, fs[0]] = value
        hidf[part] = value.astype(F32).reshape(4, 8, HALF)
        for d in (1, 2, 3):
            ref = (hid, part, fs[0])
            copies.append(wire.push(ref, ref, to_f[d]))
    arrive(copies)

    loads[6].wait()
    loads[7].wait()
    eye = iota((96, 128), 0) == iota((96, 128), 1)
    squares = jnp.zeros((96, 1), F32)
    gate = jnp.zeros((96, 512), F32)
    rise = jnp.zeros((96, 512), F32)
    for part in range(2):
        rows = mm(gathered[part], hid[part].reshape(128, HALF))
        squares = squares + jnp.sum(rows * rows, axis=-1, keepdims=True)
        cols = pl.ds(part * HALF, HALF)
        scaled = jnp.concatenate(
            [
                rows[:, n * 128 : (n + 1) * 128] * gain_ref[pl.ds(g * 14 + part * 7 + n, 1), :]
                for n in range(7)
            ],
            axis=1,
        ).astype(BF16)
        gate = gate + mm(scaled, wg[cols, :])
        rise = rise + mm(scaled, wu[cols, :])
    sq[...] = jnp.broadcast_to(
        jnp.sum(jnp.where(eye, squares, 0.0), axis=0, keepdims=True), (8, 128)
    )
    for j in range(4):
        gs[j, :, :128] = gate[:, j * 128 : (j + 1) * 128].astype(BF16)
        gs[j, :, 128:] = rise[:, j * 128 : (j + 1) * 128].astype(BF16)
    copies = []
    for d in (1, 2, 3):
        copies.append(wire.push((sq,), (rxs, d - 1), mates[d]))
        copies.append(wire.push((gs, gs_of[d]), (rxg, d - 1), mates[d]))
    table = hid[0, :, :, :128].reshape(128, 128)
    factors = []
    for part in range(2):
        seq, row = padded_row((128, 128), 0, part)
        pick = (iota((128, 128), 1) == row * 4 + SEQS).astype(F32).astype(BF16)
        here = iota((128, 128), 1) == seq * EXPERTS + c // SPLIT
        factors.append(
            jnp.sum(jnp.where(here, mm(pick, table), 0.0), axis=-1, keepdims=True)
        )
    arrive(copies)
    both = gs[g].astype(F32)
    total = sq[0:1, :]
    for d in range(3):
        both = both + rxg[d].astype(F32)
        total = total + rxs[d, 0:1, :]
    total = jnp.sum(jnp.where(eye, total, 0.0), axis=-1, keepdims=True)
    both = both * lax.rsqrt(total * (1.0 / D) + 1e-06)
    gate, rise = both[:, :128], both[:, 128:]
    units[g] = (gate / (1.0 + jnp.exp(-gate)) * rise).astype(BF16)
    copies = [wire.push((units, g), (units, g), mates[d]) for d in (1, 2, 3)]
    arrive(copies)
    loads[8].wait()
    for part in range(2):
        cols = pl.ds(part * HALF, HALF)
        value = jnp.zeros((128, HALF), F32)
        for k in range(4):
            rows = mm(spread[part], units[k]).astype(BF16)
            value = value + mm(rows, wd[k * 128 : (k + 1) * 128, cols])
        value = value.astype(BF16).astype(F32) * factors[part]
        part_buf[part] = value.astype(BF16).reshape(4, 32, HALF)
    copies = scatter(part_buf, rxq)
    arrive(copies)
    copies = []
    for part, (fs, es, to_f, to_e) in enumerate(axes):
        ybuf[part] = summed(part_buf[part, fs[0]], rxq, part).reshape(4, 8, HALF)
        for d in (1, 2, 3):
            copies.append(wire.push((ybuf, part, es[d]), (rxy, part, d - 1), to_e[d]))
    arrive(copies)
    for part, (fs, es, to_f, to_e) in enumerate(axes):
        wbuf[part] = summed(ybuf[part, es[0]], rxy, part)
    copy = wire.push((wbuf,), (rxw,), far)
    copy.wait_recv()
    for part, (fs, es, to_f, to_e) in enumerate(axes):
        value = hidf[part, es[0]] + (wbuf[part] + rxw[part])
        fo[g, part * 4 : (part + 1) * 4, :] = jnp.where(z == 0, value[0:4], value[4:8])
    copies = [wire.push((fo, g), (fo, g), mates[d]) for d in (1, 2, 3)]
    arrive(copies)
    for k in range(4):
        for part in range(2):
            at_ = k * QUARTER + part * HALF
            out_ref[:, at_ : at_ + HALF] = fo[k, part * 4 : part * 4 + SEQS, :].astype(BF16)
    wire.finish()


def vmem():
    return pl.BlockSpec(memory_space=pltpu.VMEM)


def hbm():
    return pl.BlockSpec(memory_space=pl.ANY)


def on_device(
    queries, cache, value_up_weight, w_out, resid, norm_gain, routes, route_weight,
    w_gate, w_up, w_down,
):
    g, c, x, y, z = place()
    pair, core = lax.rem(g // 2 + z, 2), g % 2
    by_column = queries.reshape(SEQS, 16, 8, QK)
    lower = lax.dynamic_index_in_dim(by_column, 2 * pair + core, 2, keepdims=False)
    upper = lax.dynamic_index_in_dim(by_column, 4 + 2 * (1 - pair) + core, 2, keepdims=False)
    rows = jnp.stack([lower, upper], axis=1).reshape(2 * SEQS, 16, QK)
    rows = jnp.pad(rows, ((0, 0), (0, 0), (0, QPAD - QK)))
    mixed = pl.pallas_call(
        kernel,
        out_shape=jax.ShapeDtypeStruct((SEQS, D), BF16),
        in_specs=[vmem(), hbm(), hbm(), hbm(), vmem(), vmem(), vmem(), vmem(), hbm(), hbm(), hbm()],
        out_specs=vmem(),
        scratch_shapes=[
            pltpu.VMEM((6, 4, 4, 2, 16, QPAD), BF16),
            pltpu.VMEM((SEQS, QPAD, CTX_DEV), BF16),
            pltpu.VMEM((256, CTX_DEV), F32),
            pltpu.VMEM((256, CTX_DEV), F32),
            pltpu.VMEM((256, CTX_DEV), BF16),
            pltpu.VMEM((256, CTX_DEV), BF16),
            pltpu.VMEM((2, 5, 256, 128), F32),
            pltpu.VMEM((6, 2, 4, 4, 16, QPAD), BF16),
            pltpu.VMEM((6, 2, 2, 2, 16, QPAD), BF16),
            pltpu.VMEM((6, 2, 2, 4, 16, QPAD), BF16),
            pltpu.VMEM((6, 2, 3, 16, QPAD), BF16),
            pltpu.VMEM((6, 2, 16, QPAD), BF16),
            pltpu.VMEM((SEQS, 2, 16, QPAD), BF16),
            pltpu.VMEM((96, KVL), BF16),
            pltpu.VMEM((KVL, DV), BF16),
            pltpu.VMEM((512, QUARTER), BF16),
            pltpu.VMEM((QUARTER, 512), BF16),
            pltpu.VMEM((QUARTER, 512), BF16),
            pltpu.VMEM((512, QUARTER), BF16),
            pltpu.VMEM((16, QUARTER), BF16),
            pltpu.VMEM((4, 96, DV), BF16),
            pltpu.VMEM((2, 4, 32, HALF), BF16),
            pltpu.VMEM((2, 3, 32, HALF), BF16),
            pltpu.VMEM((2, 32, HALF), BF16),
            pltpu.VMEM((2, 3, 32, HALF), BF16),
            pltpu.VMEM((2, 32, HALF), BF16),
            pltpu.VMEM((2, 32, HALF), BF16),
            pltpu.VMEM((2, 4, 32, HALF), BF16),
            pltpu.VMEM((2, 4, 8, HALF), F32),
            pltpu.VMEM((8, 128), F32),
            pltpu.VMEM((3, 8, 128), F32),
            pltpu.VMEM((4, 96, 256), BF16),
            pltpu.VMEM((3, 96, 256), BF16),
            pltpu.VMEM((4, 96, 128), BF16),
            pltpu.VMEM((2, 4, 32, HALF), BF16),
            pltpu.VMEM((2, 3, 32, HALF), BF16),
            pltpu.VMEM((2, 4, 8, HALF), F32),
            pltpu.VMEM((2, 3, 8, HALF), F32),
            pltpu.VMEM((2, 8, HALF), F32),
            pltpu.VMEM((2, 8, HALF), F32),
            pltpu.VMEM((4, 8, HALF), F32),
            pltpu.SemaphoreType.DMA((160,)),
            pltpu.SemaphoreType.DMA((160,)),
            pltpu.SemaphoreType.DMA((11,)),
        ],
        compiler_params=pltpu.CompilerParams(
            collective_id=0, has_side_effects=True, vmem_limit_bytes=60 * 1024 * 1024
        ),
    )(
        rows,
        jnp.swapaxes(cache, 1, 2),
        value_up_weight,
        w_out,
        jnp.swapaxes(resid, 0, 1),
        norm_gain.reshape(D // 128, 128),
        routes,
        jnp.swapaxes(route_weight, 0, 1),
        w_gate,
        w_up,
        w_down,
    )
    return mixed.reshape(SEQS, 1, D)


def solution(mesh):
    placed = (
        P(None, "cp", None),
        P(None, "cp", None),
        P("cp", None, None),
        P("cp", None),
        P(None, "cp", None),
        P(),
        P(None, "cp", None),
        P(None, "cp", None),
        P("cp", "grp", None),
        P("cp", "grp", None),
        P("cp", None, "grp"),
    )
    return jax.shard_map(
        on_device, mesh=mesh, in_specs=placed, out_specs=P(None, "cp", None), check_vma=False
    )
```

```python
import math

import jax
import jax.numpy as jnp
from jax import lax
from jax.experimental import pallas as pl
from jax.experimental.pallas import tpu as pltpu
from jax.sharding import PartitionSpec as P

D = 7168
KVL = 512
DV = 128
SPLIT = 4
QROWS = 32
CTX_DEV = 2048
QK = 576
QPAD = 640
SEQS = 3
EXPERTS = 8
QUARTER = D // 4
HALF = QUARTER // 2
N_CP = 32
CTX = CTX_DEV * N_CP

SCALE = 192.0 ** (-0.5)
SCALE2 = SCALE * math.log2(math.e)
MESH = pl.DeviceIdType.MESH
F32 = jnp.float32
BF16 = jnp.bfloat16


def place():
    g = lax.axis_index("grp")
    c = lax.axis_index("cp")
    return g, c, c // 8, (c // 2) % 4, c % 2


def mm(a, b):
    return jnp.dot(a, b, preferred_element_type=F32)


def mm_nt(a, b):
    return lax.dot_general(a, b, (((1,), (1,)), ((), ())), preferred_element_type=F32)


def iota(shape, axis):
    return lax.broadcasted_iota(jnp.int32, shape, axis)


def part_of(ref, *index):
    return ref.at[index] if index else ref


class Wire:
    def __init__(self, send_sems, recv_sems):
        self.send_sems, self.recv_sems = send_sems, recv_sems
        self.started = []

    def push(self, src, dst, device):
        copy = Copy(self, len(self.started), src, dst, device)
        self.started.append(copy)
        copy.make().start()
        return copy

    def finish(self):
        for copy in self.started:
            copy.make().wait_send()


class Copy:
    def __init__(self, wire, at, src, dst, device):
        self.wire, self.at, self.src, self.dst, self.device = wire, at, src, dst, device

    def make(self):
        return pltpu.make_async_remote_copy(
            src_ref=part_of(*self.src),
            dst_ref=part_of(*self.dst),
            send_sem=self.wire.send_sems.at[self.at],
            recv_sem=self.wire.recv_sems.at[self.at],
            device_id=self.device,
            device_id_type=MESH,
        )

    def wait_recv(self):
        self.make().wait_recv()


def arrive(copies):
    for copy in copies:
        copy.wait_recv()


def greet(peers):
    barrier = pltpu.get_barrier_semaphore()
    for peer in peers:
        pl.semaphore_signal(barrier, inc=1, device_id=peer, device_id_type=MESH)
    pl.semaphore_wait(barrier, len(peers))


def padded_row(shape, axis, part):
    r = iota(shape, axis)
    s, z, b, a = r % 4, (r // 4) % 2, (r // 8) % 4, r // 32
    x, y = (a, b) if part == 0 else (b, a)
    return s, (x * 4 + y) * 2 + z


def unpack(value):
    value = value.reshape(-1, QPAD).astype(F32)
    aux = value[:, KVL:]
    lane = iota(aux.shape, 1)
    peak = jnp.sum(jnp.where(lane == 0, aux, 0.0), axis=-1, keepdims=True)
    total = jnp.sum(jnp.where((lane == 1) | (lane == 2), aux, 0.0), axis=-1, keepdims=True)
    return value[:, :KVL], peak, total


def aux_lanes(peak, total):
    lane = iota((peak.shape[0], QPAD - KVL), 1)
    high = total.astype(BF16).astype(F32)
    low = total - high
    return jnp.where(
        lane == 0, peak, jnp.where(lane == 1, high, jnp.where(lane == 2, low, 0.0))
    )


def merge(values):
    items = [unpack(value) for value in values]
    peak = items[0][1]
    for item in items[1:]:
        peak = jnp.maximum(peak, item[1])
    out, total = None, None
    for item in items:
        factor = jnp.exp((item[1] - peak) * SCALE)
        if out is None:
            out, total = item[0] * factor, item[2] * factor
        else:
            out, total = out + item[0] * factor, total + item[2] * factor
    return out, peak, total


def put(ref, merged):
    out, peak, total = merged
    ref[..., :KVL] = out.astype(BF16).reshape(*ref.shape[:-1], KVL)
    ref[..., KVL:] = aux_lanes(peak, total).astype(BF16).reshape(*ref.shape[:-1], QPAD - KVL)


def kernel(
    q_ref, cache_ref, vup_ref, wout_ref, resid_ref, gain_ref, routes_ref, weight_ref,
    wg_ref, wu_ref, wd_ref, out_ref,
    qbuf, kv, score_a, score_b, prob_a, prob_b, oscr, msg, rx1, rx2, rx3, fin, rxz, lat,
    vup, wout, wg, wu, wd, own_resid, heads, pbuf, rxa, ebuf, rxb, zbuf, rxc, hid, hidf,
    sq, rxs, gs, rxg, units, part_buf, rxq, ybuf, rxy, wbuf, rxw, fo,
    send_sems, recv_sems, local_sems,
):
    g, c, x, y, z = place()
    up = lambda v, d: lax.rem(v + d, 4)

    def at(px, py, pz):
        return (g, (px * 4 + py) * 2 + pz)

    xs = [x] + [up(x, d) for d in (1, 2, 3)]
    ys = [y] + [up(y, d) for d in (1, 2, 3)]
    to_x = [None] + [at(xs[d], y, z) for d in (1, 2, 3)]
    to_y = [None] + [at(x, ys[d], z) for d in (1, 2, 3)]
    partner = (lax.rem(g + 2, 4), (x * 4 + y) * 2 + (1 - z))
    far = at(x, y, 1 - z)
    gs_of = [g] + [up(g, d) for d in (1, 2, 3)]
    mates = [None] + [(gs_of[d], c) for d in (1, 2, 3)]
    columns = pl.ds(pl.multiple_of(g * QUARTER, 128), QUARTER)
    pairs = [(q_ref, qbuf.at[:, x, y, z])]
    pairs += [(cache_ref.at[s], kv.at[s, pl.ds(0, QK)]) for s in range(SEQS)]
    pairs += [
        (vup_ref.at[g], vup),
        (wout_ref.at[:, columns], wout),
        (wg_ref.at[0], wg),
        (wu_ref.at[0], wu),
        (wd_ref.at[0], wd),
    ]
    loads = [
        pltpu.make_async_copy(src, dst, local_sems.at[n]) for n, (src, dst) in enumerate(pairs)
    ]
    for copy in loads:
        copy.start()

    greet(
        to_x[1:] + to_y[1:] + mates[1:] + [partner, far]
    )
    wire = Wire(send_sems, recv_sems)

    chunks = [(0, 1), (1, 1), (2, 1), (3, 1), (4, 1), (5, 1)]
    dirs = (1, 3)
    other = 1 - z

    def gather_0(k, _):
        span = pl.ds(*chunks[k])
        return [wire.push((q_ref, span), (qbuf, span, x, y, z), partner)]

    def gather_1(k, copies):
        arrive(copies)
        span = pl.ds(*chunks[k])
        copies = []
        for d in (1, 2, 3):
            ref = (qbuf, span, x, y, 0)
            copies.append(wire.push(ref, ref, to_x[d]))
            ref = (qbuf, span, x, y, 1)
            copies.append(wire.push(ref, ref, to_y[d]))
        return copies

    def gather_3(k, copies):
        arrive(copies)
        span = pl.ds(*chunks[k])
        copies = []
        for d in dirs:
            ref = (qbuf, span, slice(None), y, 0)
            copies.append(wire.push(ref, ref, to_y[d]))
            ref = (qbuf, span, x, slice(None), 1)
            copies.append(wire.push(ref, ref, to_x[d]))
        return copies

    def gather_4(k, copies):
        arrive(copies)
        span = pl.ds(*chunks[k])
        copies = []
        for n, d in enumerate(dirs):
            ref = (qbuf, span, pl.ds(2 * n, 2), ys[4 - d], 0)
            copies.append(wire.push(ref, ref, to_y[d]))
            ref = (qbuf, span, xs[4 - d], pl.ds(2 * n, 2), 1)
            copies.append(wire.push(ref, ref, to_x[d]))
        return copies

    def gather_5(k, copies):
        arrive(copies)

    def scores(t, s, part, score):
        q = qbuf[t, 2 * part : 2 * part + 2].reshape(256, QPAD)
        for n in range(4):
            keys = pl.ds(n * 512, 512)
            value = mm(q, kv[s, :, keys])
            if n < 3:
                score[:, keys] = value
            else:
                score[:, 1536:1920] = value[:, :384]
                row = 16 * part + iota((256, 128), 0) // 16
                position = c * CTX_DEV + 1920 + iota((256, 128), 1)
                score[:, 1920:] = jnp.where(
                    position <= CTX - QROWS + row, value[:, 384:], -1e30
                )

    def weigh(t, s, part, score, prob):
        peak = jnp.max(score[...], axis=-1, keepdims=True).astype(BF16).astype(F32)
        total = jnp.zeros((256, 128), F32)
        for n in range(4):
            keys = pl.ds(n * 512, 512)
            weight = jnp.exp2((score[:, keys] - peak) * SCALE2)
            for m in range(4):
                total = total + weight[:, m * 128 : (m + 1) * 128]
            prob[:, keys] = weight.astype(BF16)
        total = jnp.sum(total, axis=-1, keepdims=True)
        out = mm_nt(prob[...], kv[s, :KVL, :])
        for m in range(4):
            oscr[part, m] = out[:, m * 128 : (m + 1) * 128]
        oscr[part, 4] = aux_lanes(peak, total)
        for n in range(16):
            a, b = (n // 4, n % 4) if part == 0 else (n % 4, n // 4)
            for m in range(5):
                lanes = pl.ds(m * 128, 128)
                msg[t, part, a, b, :, lanes] = oscr[
                    part, m, pl.ds(n, 16, stride=16), :
                ].astype(BF16)

    def attend(t):
        s = t // 2
        scores(t, s, 0, score_a)
        scores(t, s, 1, score_b)
        weigh(t, s, 0, score_a, prob_a)
        weigh(t, s, 1, score_b, prob_b)

    axes = [(xs, ys, to_x, to_y), (ys, xs, to_y, to_x)]

    def reduce_1(k, _):
        span = pl.ds(*chunks[k])
        copies = []
        for part, (fs, es, to_f, to_e) in enumerate(axes):
            for n, d in enumerate(dirs):
                src = (msg, span, part, fs[2], pl.ds(2 * n, 2))
                copies.append(wire.push(src, (rx1, span, part, n), to_f[d]))
        return copies

    def reduce_2(k, copies):
        arrive(copies)
        span = pl.ds(*chunks[k])
        copies = []
        for part, (fs, es, to_f, to_e) in enumerate(axes):
            for n, d in enumerate(dirs):

                @pl.loop(chunks[k][0], sum(chunks[k]))
                def _(t):
                    ref = msg.at[t, part, fs[d], pl.ds(2 * n, 2)]
                    put(ref, merge([ref[...], rx1[t, part, n]]))

                copies.append(
                    wire.push((msg, span, part, fs[d]), (rx2, span, part, n), to_f[d])
                )
        return copies

    def reduce_3(k, copies):
        arrive(copies)
        span = pl.ds(*chunks[k])
        copies = []
        for part, (fs, es, to_f, to_e) in enumerate(axes):

            @pl.loop(2 * chunks[k][0], 2 * sum(chunks[k]))
            def _(at_):
                t, units = at_ // 2, pl.ds(2 * (at_ % 2), 2)
                ref = msg.at[t, part, fs[0], units]
                put(ref, merge([ref[...], rx2[t, part, 0, units], rx2[t, part, 1, units]]))

            for d in (1, 2, 3):
                src = (msg, span, part, fs[0], es[d])
                copies.append(wire.push(src, (rx3, span, part, d - 1), to_e[d]))
        return copies

    def reduce_4(k, copies):
        arrive(copies)

        @pl.loop(chunks[k][0], sum(chunks[k]))
        def _(t):
            for part, (fs, es, to_f, to_e) in enumerate(axes):
                put(
                    fin.at[t, part],
                    merge([msg[t, part, fs[0], es[0]]] + [rx3[t, part, d] for d in range(3)]),
                )

        done = [t // 2 for t in range(chunks[k][0], sum(chunks[k])) if t % 2]
        return [(s, wire.push((fin, 2 * s + other), (rxz, s), partner)) for s in done]

    def reduce_5(k, copies):
        for s, copy in copies:
            copy.wait_recv()
            out, peak, total = merge([fin[2 * s + z], rxz[s]])
            lat[s * QROWS : (s + 1) * QROWS, :] = (out / total).astype(BF16)

    state = [None] * len(chunks)

    def run(steps):
        for step, k in steps:
            state[k] = step(k, state[k])

    loads[0].wait()
    run([(gather_0, 0), (gather_0, 1)])
    kv[:, QK:, :] = jnp.zeros((SEQS, QPAD - QK, CTX_DEV), BF16)
    run([(gather_1, 0), (gather_0, 2), (gather_1, 1)])
    run([(gather_3, 0), (gather_0, 3), (gather_1, 2)])
    run([(gather_3, 1), (gather_0, 4), (gather_1, 3)])
    run([(gather_4, 0), (gather_0, 5), (gather_3, 2)])
    run([(gather_1, 4), (gather_4, 1), (gather_1, 5)])
    run([(gather_3, 3)])
    for copy in loads[1:4]:
        copy.wait()
    run([(gather_5, 0)])
    between = {
        1: [
            (gather_4, 2),
            (reduce_1, 0),
            (gather_5, 1),
            (gather_3, 4),
        ],
        2: [
            (gather_4, 3),
            (gather_5, 2),
            (gather_3, 5),
            (reduce_1, 1),
        ],
        3: [
            (reduce_1, 2),
            (gather_4, 4),
            (reduce_2, 0),
            (gather_5, 3),
        ],
        4: [
            (reduce_2, 1),
            (gather_4, 5),
            (reduce_1, 3),
            (reduce_2, 2),
            (gather_5, 4),
        ],
        5: [
            (reduce_3, 0),
            (reduce_3, 1),
            (gather_5, 5),
            (reduce_1, 4),
        ],
    }

    @pl.loop(0, 6)
    def _(t):
        for at_, steps in between.items():
            if steps:

                @pl.when(t == at_)
                def _():
                    run(steps)

        attend(t)

    run([(reduce_1, 5), (reduce_4, 0), (reduce_3, 2)])
    run([(reduce_4, 1), (reduce_2, 3), (reduce_2, 4)])
    run([(reduce_5, 0), (reduce_2, 5), (reduce_5, 1)])
    run([(reduce_4, 2), (reduce_3, 3), (reduce_5, 2)])
    run([(reduce_3, 4), (reduce_3, 5), (reduce_4, 3)])
    run([(reduce_4, 4), (reduce_4, 5), (reduce_5, 3)])
    run([(reduce_5, 4), (reduce_5, 5)])

    loads[4].wait()
    heads[g] = mm(lat[...], vup[...]).astype(BF16)
    copies = [wire.push((heads, g), (heads, g), mates[d]) for d in (1, 2, 3)]
    spread, gathered = [], []
    for part in range(2):
        seq, row = padded_row((128, 96), 0, part)
        j = iota((128, 96), 1)
        spread.append(
            ((seq < SEQS) & (j == seq * QROWS + row)).astype(F32).astype(BF16)
        )
        seq, row = padded_row((96, 128), 1, part)
        j = iota((96, 128), 0)
        gathered.append(
            ((seq < SEQS) & (j == seq * QROWS + row)).astype(F32).astype(BF16)
        )
    arrive(copies)
    loads[5].wait()
    own_resid[...] = jnp.zeros((16, QUARTER), BF16)
    own_resid[0:SEQS, :] = resid_ref[0, :, columns]
    lane = iota((1, 128), 1)
    gates = jnp.zeros((1, 128), F32)
    for s in range(SEQS):
        for r in range(4):
            here = lane == s * EXPERTS + routes_ref[s, :, r : r + 1]
            gates = gates + jnp.where(here, weight_ref[0, s : s + 1, r : r + 1].astype(F32), 0.0)
    for part in range(2):
        cols = pl.ds(part * HALF, HALF)
        seq, row = padded_row((128, 16), 0, part)
        mine = ((row == c) & (seq == iota((128, 16), 1)) & (seq < SEQS)).astype(F32).astype(BF16)
        value = mm(mine, own_resid[:, cols])
        for k in range(4):
            rows = mm(spread[part], heads[k]).astype(BF16)
            value = value + mm(rows, wout[k * DV : (k + 1) * DV, cols])
        pbuf[part] = value.astype(BF16).reshape(4, 32, HALF)
        if part == 0:
            seq, row = padded_row((128, 128), 0, part)
            head = jnp.where((seq == SEQS) & (row == c), gates, value[:, :128])
            pbuf[part, :, :, :128] = head.astype(BF16).reshape(4, 32, 128)

    def scatter(source, landing):
        copies = []
        for part, (fs, es, to_f, to_e) in enumerate(axes):
            for d in (1, 2, 3):
                copies.append(wire.push((source, part, fs[d]), (landing, part, d - 1), to_f[d]))
        return copies

    def summed(first, landing, part):
        value = first.astype(F32)
        for d in range(3):
            value = value + landing[part, d].astype(F32)
        return value

    copies = scatter(pbuf, rxa)
    arrive(copies)
    copies = []
    for part, (fs, es, to_f, to_e) in enumerate(axes):
        ebuf[part] = summed(pbuf[part, fs[0]], rxa, part).astype(BF16)
        for d in (1, 2, 3):
            copies.append(wire.push((ebuf, part), (rxb, part, d - 1), to_e[d]))
    arrive(copies)
    for part in range(2):
        zbuf[part] = summed(ebuf[part], rxb, part).astype(BF16)
    copy = wire.push((zbuf,), (rxc,), far)
    copy.wait_recv()
    copies = []
    for part, (fs, es, to_f, to_e) in enumerate(axes):
        value = (zbuf[part].astype(F32) + rxc[part].astype(F32)).astype(BF16)
        hid[part, fs[0]] = value
        hidf[part] = value.astype(F32).reshape(4, 8, HALF)
        for d in (1, 2, 3):
            ref = (hid, part, fs[0])
            copies.append(wire.push(ref, ref, to_f[d]))
    arrive(copies)

    loads[6].wait()
    loads[7].wait()
    eye = iota((96, 128), 0) == iota((96, 128), 1)
    squares = jnp.zeros((96, 1), F32)
    gate = jnp.zeros((96, 512), F32)
    rise = jnp.zeros((96, 512), F32)
    for part in range(2):
        rows = mm(gathered[part], hid[part].reshape(128, HALF))
        squares = squares + jnp.sum(rows * rows, axis=-1, keepdims=True)
        cols = pl.ds(part * HALF, HALF)
        scaled = jnp.concatenate(
            [
                rows[:, n * 128 : (n + 1) * 128] * gain_ref[pl.ds(g * 14 + part * 7 + n, 1), :]
                for n in range(7)
            ],
            axis=1,
        ).astype(BF16)
        gate = gate + mm(scaled, wg[cols, :])
        rise = rise + mm(scaled, wu[cols, :])
    sq[...] = jnp.broadcast_to(
        jnp.sum(jnp.where(eye, squares, 0.0), axis=0, keepdims=True), (8, 128)
    )
    for j in range(4):
        gs[j, :, :128] = gate[:, j * 128 : (j + 1) * 128].astype(BF16)
        gs[j, :, 128:] = rise[:, j * 128 : (j + 1) * 128].astype(BF16)
    copies = []
    for d in (1, 2, 3):
        copies.append(wire.push((sq,), (rxs, d - 1), mates[d]))
        copies.append(wire.push((gs, gs_of[d]), (rxg, d - 1), mates[d]))
    table = hid[0, :, :, :128].reshape(128, 128)
    factors = []
    for part in range(2):
        seq, row = padded_row((128, 128), 0, part)
        pick = (iota((128, 128), 1) == row * 4 + SEQS).astype(F32).astype(BF16)
        here = iota((128, 128), 1) == seq * EXPERTS + c // SPLIT
        factors.append(
            jnp.sum(jnp.where(here, mm(pick, table), 0.0), axis=-1, keepdims=True)
        )
    arrive(copies)
    both = gs[g].astype(F32)
    total = sq[0:1, :]
    for d in range(3):
        both = both + rxg[d].astype(F32)
        total = total + rxs[d, 0:1, :]
    total = jnp.sum(jnp.where(eye, total, 0.0), axis=-1, keepdims=True)
    both = both * lax.rsqrt(total * (1.0 / D) + 1e-06)
    gate, rise = both[:, :128], both[:, 128:]
    units[g] = (gate / (1.0 + jnp.exp(-gate)) * rise).astype(BF16)
    copies = [wire.push((units, g), (units, g), mates[d]) for d in (1, 2, 3)]
    arrive(copies)
    loads[8].wait()
    for part in range(2):
        cols = pl.ds(part * HALF, HALF)
        value = jnp.zeros((128, HALF), F32)
        for k in range(4):
            rows = mm(spread[part], units[k]).astype(BF16)
            value = value + mm(rows, wd[k * 128 : (k + 1) * 128, cols])
        value = value.astype(BF16).astype(F32) * factors[part]
        part_buf[part] = value.astype(BF16).reshape(4, 32, HALF)
    copies = scatter(part_buf, rxq)
    arrive(copies)
    copies = []
    for part, (fs, es, to_f, to_e) in enumerate(axes):
        ybuf[part] = summed(part_buf[part, fs[0]], rxq, part).reshape(4, 8, HALF)
        for d in (1, 2, 3):
            copies.append(wire.push((ybuf, part, es[d]), (rxy, part, d - 1), to_e[d]))
    arrive(copies)
    for part, (fs, es, to_f, to_e) in enumerate(axes):
        wbuf[part] = summed(ybuf[part, es[0]], rxy, part)
    copy = wire.push((wbuf,), (rxw,), far)
    copy.wait_recv()
    for part, (fs, es, to_f, to_e) in enumerate(axes):
        value = hidf[part, es[0]] + (wbuf[part] + rxw[part])
        fo[g, part * 4 : (part + 1) * 4, :] = jnp.where(z == 0, value[0:4], value[4:8])
    copies = [wire.push((fo, g), (fo, g), mates[d]) for d in (1, 2, 3)]
    arrive(copies)
    for k in range(4):
        for part in range(2):
            at_ = k * QUARTER + part * HALF
            out_ref[:, at_ : at_ + HALF] = fo[k, part * 4 : part * 4 + SEQS, :].astype(BF16)
    wire.finish()


def vmem():
    return pl.BlockSpec(memory_space=pltpu.VMEM)


def hbm():
    return pl.BlockSpec(memory_space=pl.ANY)


def on_device(
    queries, cache, value_up_weight, w_out, resid, norm_gain, routes, route_weight,
    w_gate, w_up, w_down,
):
    g, c, x, y, z = place()
    pair, core = lax.rem(g // 2 + z, 2), g % 2
    by_column = queries.reshape(SEQS, 16, 8, QK)
    lower = lax.dynamic_index_in_dim(by_column, 2 * pair + core, 2, keepdims=False)
    upper = lax.dynamic_index_in_dim(by_column, 4 + 2 * (1 - pair) + core, 2, keepdims=False)
    rows = jnp.stack([lower, upper], axis=1).reshape(2 * SEQS, 16, QK)
    rows = jnp.pad(rows, ((0, 0), (0, 0), (0, QPAD - QK)))
    mixed = pl.pallas_call(
        kernel,
        out_shape=jax.ShapeDtypeStruct((SEQS, D), BF16),
        in_specs=[vmem(), hbm(), hbm(), hbm(), vmem(), vmem(), vmem(), vmem(), hbm(), hbm(), hbm()],
        out_specs=vmem(),
        scratch_shapes=[
            pltpu.VMEM((6, 4, 4, 2, 16, QPAD), BF16),
            pltpu.VMEM((SEQS, QPAD, CTX_DEV), BF16),
            pltpu.VMEM((256, CTX_DEV), F32),
            pltpu.VMEM((256, CTX_DEV), F32),
            pltpu.VMEM((256, CTX_DEV), BF16),
            pltpu.VMEM((256, CTX_DEV), BF16),
            pltpu.VMEM((2, 5, 256, 128), F32),
            pltpu.VMEM((6, 2, 4, 4, 16, QPAD), BF16),
            pltpu.VMEM((6, 2, 2, 2, 16, QPAD), BF16),
            pltpu.VMEM((6, 2, 2, 4, 16, QPAD), BF16),
            pltpu.VMEM((6, 2, 3, 16, QPAD), BF16),
            pltpu.VMEM((6, 2, 16, QPAD), BF16),
            pltpu.VMEM((SEQS, 2, 16, QPAD), BF16),
            pltpu.VMEM((96, KVL), BF16),
            pltpu.VMEM((KVL, DV), BF16),
            pltpu.VMEM((512, QUARTER), BF16),
            pltpu.VMEM((QUARTER, 512), BF16),
            pltpu.VMEM((QUARTER, 512), BF16),
            pltpu.VMEM((512, QUARTER), BF16),
            pltpu.VMEM((16, QUARTER), BF16),
            pltpu.VMEM((4, 96, DV), BF16),
            pltpu.VMEM((2, 4, 32, HALF), BF16),
            pltpu.VMEM((2, 3, 32, HALF), BF16),
            pltpu.VMEM((2, 32, HALF), BF16),
            pltpu.VMEM((2, 3, 32, HALF), BF16),
            pltpu.VMEM((2, 32, HALF), BF16),
            pltpu.VMEM((2, 32, HALF), BF16),
            pltpu.VMEM((2, 4, 32, HALF), BF16),
            pltpu.VMEM((2, 4, 8, HALF), F32),
            pltpu.VMEM((8, 128), F32),
            pltpu.VMEM((3, 8, 128), F32),
            pltpu.VMEM((4, 96, 256), BF16),
            pltpu.VMEM((3, 96, 256), BF16),
            pltpu.VMEM((4, 96, 128), BF16),
            pltpu.VMEM((2, 4, 32, HALF), BF16),
            pltpu.VMEM((2, 3, 32, HALF), BF16),
            pltpu.VMEM((2, 4, 8, HALF), F32),
            pltpu.VMEM((2, 3, 8, HALF), F32),
            pltpu.VMEM((2, 8, HALF), F32),
            pltpu.VMEM((2, 8, HALF), F32),
            pltpu.VMEM((4, 8, HALF), F32),
            pltpu.SemaphoreType.DMA((240,)),
            pltpu.SemaphoreType.DMA((240,)),
            pltpu.SemaphoreType.DMA((11,)),
        ],
        compiler_params=pltpu.CompilerParams(
            collective_id=0, has_side_effects=True, vmem_limit_bytes=60 * 1024 * 1024
        ),
    )(
        rows,
        jnp.swapaxes(cache, 1, 2),
        value_up_weight,
        w_out,
        jnp.swapaxes(resid, 0, 1),
        norm_gain.reshape(D // 128, 128),
        routes,
        jnp.swapaxes(route_weight, 0, 1),
        w_gate,
        w_up,
        w_down,
    )
    return mixed.reshape(SEQS, 1, D)


def solution(mesh):
    placed = (
        P(None, "cp", None),
        P(None, "cp", None),
        P("cp", None, None),
        P("cp", None),
        P(None, "cp", None),
        P(),
        P(None, "cp", None),
        P(None, "cp", None),
        P("cp", "grp", None),
        P("cp", "grp", None),
        P("cp", None, "grp"),
    )
    return jax.shard_map(
        on_device, mesh=mesh, in_specs=placed, out_specs=P(None, "cp", None), check_vma=False
    )
```

```python
import math

import jax
import jax.numpy as jnp
from jax import lax
from jax.experimental import pallas as pl
from jax.experimental.pallas import tpu as pltpu
from jax.sharding import PartitionSpec as P

D = 7168
KVL = 512
DV = 128
SPLIT = 4
QROWS = 32
CTX_DEV = 2048
QK = 576
QPAD = 640
SEQS = 3
EXPERTS = 8
QUARTER = D // 4
HALF = QUARTER // 2
N_CP = 32
CTX = CTX_DEV * N_CP

SCALE = 192.0 ** (-0.5)
SCALE2 = SCALE * math.log2(math.e)
MESH = pl.DeviceIdType.MESH
F32 = jnp.float32
BF16 = jnp.bfloat16


def place():
    g = lax.axis_index("grp")
    c = lax.axis_index("cp")
    return g, c, c // 8, (c // 2) % 4, c % 2


def mm(a, b):
    return jnp.dot(a, b, preferred_element_type=F32)


def mm_nt(a, b):
    return lax.dot_general(a, b, (((1,), (1,)), ((), ())), preferred_element_type=F32)


def iota(shape, axis):
    return lax.broadcasted_iota(jnp.int32, shape, axis)


def part_of(ref, *index):
    return ref.at[index] if index else ref


class Wire:
    def __init__(self, send_sems, recv_sems):
        self.send_sems, self.recv_sems = send_sems, recv_sems
        self.started = []

    def push(self, src, dst, device):
        copy = Copy(self, len(self.started), src, dst, device)
        self.started.append(copy)
        copy.make().start()
        return copy

    def finish(self):
        for copy in self.started:
            copy.make().wait_send()


class Copy:
    def __init__(self, wire, at, src, dst, device):
        self.wire, self.at, self.src, self.dst, self.device = wire, at, src, dst, device

    def make(self):
        return pltpu.make_async_remote_copy(
            src_ref=part_of(*self.src),
            dst_ref=part_of(*self.dst),
            send_sem=self.wire.send_sems.at[self.at],
            recv_sem=self.wire.recv_sems.at[self.at],
            device_id=self.device,
            device_id_type=MESH,
        )

    def wait_recv(self):
        self.make().wait_recv()


def arrive(copies):
    for copy in copies:
        copy.wait_recv()


def fold(value):
    rest = jnp.concatenate([value[:, 512:], jnp.zeros((8, 128), value.dtype)], axis=1)
    return jnp.concatenate([value[:, :512], rest], axis=0).astype(BF16)


def unfold(value):
    value = value.astype(F32)
    return jnp.concatenate([value[:8], value[8:, : HALF - 512]], axis=1)


def greet(peers):
    barrier = pltpu.get_barrier_semaphore()
    for peer in peers:
        pl.semaphore_signal(barrier, inc=1, device_id=peer, device_id_type=MESH)
    pl.semaphore_wait(barrier, len(peers))


def padded_row(shape, axis, part):
    r = iota(shape, axis)
    s, z, b, a = r % 4, (r // 4) % 2, (r // 8) % 4, r // 32
    x, y = (a, b) if part == 0 else (b, a)
    return s, (x * 4 + y) * 2 + z


def unpack(value):
    value = value.reshape(-1, QPAD).astype(F32)
    aux = value[:, KVL:]
    lane = iota(aux.shape, 1)
    peak = jnp.sum(jnp.where(lane == 0, aux, 0.0), axis=-1, keepdims=True)
    total = jnp.sum(jnp.where((lane == 1) | (lane == 2), aux, 0.0), axis=-1, keepdims=True)
    return value[:, :KVL], peak, total


def aux_lanes(peak, total):
    lane = iota((peak.shape[0], QPAD - KVL), 1)
    high = total.astype(BF16).astype(F32)
    low = total - high
    return jnp.where(
        lane == 0, peak, jnp.where(lane == 1, high, jnp.where(lane == 2, low, 0.0))
    )


def merge(values):
    items = [unpack(value) for value in values]
    peak = items[0][1]
    for item in items[1:]:
        peak = jnp.maximum(peak, item[1])
    out, total = None, None
    for item in items:
        factor = jnp.exp((item[1] - peak) * SCALE)
        if out is None:
            out, total = item[0] * factor, item[2] * factor
        else:
            out, total = out + item[0] * factor, total + item[2] * factor
    return out, peak, total


def put(ref, merged):
    out, peak, total = merged
    ref[..., :KVL] = out.astype(BF16).reshape(*ref.shape[:-1], KVL)
    ref[..., KVL:] = aux_lanes(peak, total).astype(BF16).reshape(*ref.shape[:-1], QPAD - KVL)


def kernel(
    q_ref, cache_ref, vup_ref, wout_ref, resid_ref, gain_ref, routes_ref, weight_ref,
    wg_ref, wu_ref, wd_ref, out_ref,
    qbuf, kv, score_a, score_b, prob_a, prob_b, oscr, msg, rx1, rx2, rx3, fin, rxz, lat,
    vup, wout, wg, wu, wd, own_resid, heads, pbuf, rxa, ebuf, rxb, zbuf, hid, hidf,
    sq, rxs, gs, rxg, units, part_buf, rxq, ybuf, rxy, wbuf, gone, fo,
    send_sems, recv_sems, local_sems,
):
    g, c, x, y, z = place()
    up = lambda v, d: lax.rem(v + d, 4)

    def at(px, py, pz):
        return (g, (px * 4 + py) * 2 + pz)

    xs = [x] + [up(x, d) for d in (1, 2, 3)]
    ys = [y] + [up(y, d) for d in (1, 2, 3)]
    to_x = [None] + [at(xs[d], y, z) for d in (1, 2, 3)]
    to_y = [None] + [at(x, ys[d], z) for d in (1, 2, 3)]
    partner = (lax.rem(g + 2, 4), (x * 4 + y) * 2 + (1 - z))
    far = at(x, y, 1 - z)
    far_x = [None] + [at(xs[d], y, 1 - z) for d in (1, 2, 3)]
    far_y = [None] + [at(x, ys[d], 1 - z) for d in (1, 2, 3)]
    gs_of = [g] + [up(g, d) for d in (1, 2, 3)]
    mates = [None] + [(gs_of[d], c) for d in (1, 2, 3)]
    far_mates = [(gs_of[d], (x * 4 + y) * 2 + (1 - z)) for d in range(4)]
    columns = pl.ds(pl.multiple_of(g * QUARTER, 128), QUARTER)
    pairs = [(q_ref, qbuf.at[:, x, y, z])]
    pairs += [(cache_ref.at[s], kv.at[s]) for s in range(SEQS)]
    pairs += [
        (vup_ref.at[g], vup),
        (wout_ref.at[:, columns], wout),
        (wg_ref.at[0], wg),
        (wu_ref.at[0], wu),
        (wd_ref.at[0], wd),
    ]
    loads = [
        pltpu.make_async_copy(src, dst, local_sems.at[n]) for n, (src, dst) in enumerate(pairs)
    ]
    for copy in loads:
        copy.start()

    greet(
        to_x[1:] + to_y[1:] + mates[1:] + far_x[1:] + far_y[1:] + far_mates
    )
    wire = Wire(send_sems, recv_sems)

    chunks = [(0, 1), (1, 1), (2, 1), (3, 1), (4, 1), (5, 1)]
    dirs = (1, 3)
    other = 1 - z

    def gather_0(k, _):
        span = pl.ds(*chunks[k])
        return [wire.push((q_ref, span), (qbuf, span, x, y, z), partner)]

    def gather_1(k, copies):
        arrive(copies)
        span = pl.ds(*chunks[k])
        copies = []
        for d in (1, 2, 3):
            ref = (qbuf, span, x, y, 0)
            copies.append(wire.push(ref, ref, to_x[d]))
            ref = (qbuf, span, x, y, 1)
            copies.append(wire.push(ref, ref, to_y[d]))
        return copies

    def gather_3(k, copies):
        arrive(copies)
        span = pl.ds(*chunks[k])
        copies = []
        for d in dirs:
            ref = (qbuf, span, slice(None), y, 0)
            copies.append(wire.push(ref, ref, to_y[d]))
            ref = (qbuf, span, x, slice(None), 1)
            copies.append(wire.push(ref, ref, to_x[d]))
        return copies

    def gather_4(k, copies):
        arrive(copies)
        span = pl.ds(*chunks[k])
        copies = []
        for n, d in enumerate(dirs):
            ref = (qbuf, span, pl.ds(2 * n, 2), ys[4 - d], 0)
            copies.append(wire.push(ref, ref, to_y[d]))
            ref = (qbuf, span, xs[4 - d], pl.ds(2 * n, 2), 1)
            copies.append(wire.push(ref, ref, to_x[d]))
        return copies

    def gather_5(k, copies):
        arrive(copies)

    def scores(t, s, part, score):
        q = qbuf[t, 2 * part : 2 * part + 2].reshape(256, QK)
        for n in range(4):
            keys = pl.ds(n * 512, 512)
            value = mm(q, kv[s, :, keys])
            if n < 3:
                score[:, keys] = value
            else:
                score[:, 1536:1920] = value[:, :384]
                row = 16 * part + iota((256, 128), 0) // 16
                position = c * CTX_DEV + 1920 + iota((256, 128), 1)
                score[:, 1920:] = jnp.where(
                    position <= CTX - QROWS + row, value[:, 384:], -1e30
                )

    def weigh(t, s, part, score, prob):
        peak = jnp.max(score[...], axis=-1, keepdims=True).astype(BF16).astype(F32)
        total = jnp.zeros((256, 128), F32)
        for n in range(4):
            keys = pl.ds(n * 512, 512)
            weight = jnp.exp2((score[:, keys] - peak) * SCALE2)
            for m in range(4):
                total = total + weight[:, m * 128 : (m + 1) * 128]
            prob[:, keys] = weight.astype(BF16)
        total = jnp.sum(total, axis=-1, keepdims=True)
        out = mm_nt(prob[...], kv[s, :KVL, :])
        for m in range(4):
            oscr[part, m] = out[:, m * 128 : (m + 1) * 128]
        oscr[part, 4] = aux_lanes(peak, total)
        for n in range(16):
            a, b = (n // 4, n % 4) if part == 0 else (n % 4, n // 4)
            for m in range(5):
                lanes = pl.ds(m * 128, 128)
                msg[t, part, a, b, :, lanes] = oscr[
                    part, m, pl.ds(n, 16, stride=16), :
                ].astype(BF16)

    def attend(t):
        s = t // 2
        scores(t, s, 0, score_a)
        scores(t, s, 1, score_b)
        weigh(t, s, 0, score_a, prob_a)
        weigh(t, s, 1, score_b, prob_b)

    axes = [(xs, ys, to_x, to_y), (ys, xs, to_y, to_x)]
    far_e = [far_y, far_x]

    def reduce_1(k, _):
        span = pl.ds(*chunks[k])
        copies = []
        for part, (fs, es, to_f, to_e) in enumerate(axes):
            for n, d in enumerate(dirs):
                src = (msg, span, part, fs[2], pl.ds(2 * n, 2))
                copies.append(wire.push(src, (rx1, span, part, n), to_f[d]))
        return copies

    def reduce_2(k, copies):
        arrive(copies)
        span = pl.ds(*chunks[k])
        copies = []
        for part, (fs, es, to_f, to_e) in enumerate(axes):
            for n, d in enumerate(dirs):

                @pl.loop(chunks[k][0], sum(chunks[k]))
                def _(t):
                    ref = msg.at[t, part, fs[d], pl.ds(2 * n, 2)]
                    put(ref, merge([ref[...], rx1[t, part, n]]))

                copies.append(
                    wire.push((msg, span, part, fs[d]), (rx2, span, part, n), to_f[d])
                )
        return copies

    def reduce_3(k, copies):
        arrive(copies)
        span = pl.ds(*chunks[k])
        copies = []
        for part, (fs, es, to_f, to_e) in enumerate(axes):

            @pl.loop(2 * chunks[k][0], 2 * sum(chunks[k]))
            def _(at_):
                t, units = at_ // 2, pl.ds(2 * (at_ % 2), 2)
                ref = msg.at[t, part, fs[0], units]
                put(ref, merge([ref[...], rx2[t, part, 0, units], rx2[t, part, 1, units]]))

            for d in (1, 2, 3):
                src = (msg, span, part, fs[0], es[d])
                copies.append(wire.push(src, (rx3, span, part, d - 1), to_e[d]))
        return copies

    def reduce_4(k, copies):
        arrive(copies)

        @pl.loop(chunks[k][0], sum(chunks[k]))
        def _(t):
            for part, (fs, es, to_f, to_e) in enumerate(axes):
                put(
                    fin.at[t, part],
                    merge([msg[t, part, fs[0], es[0]]] + [rx3[t, part, d] for d in range(3)]),
                )

        done = [t // 2 for t in range(chunks[k][0], sum(chunks[k])) if t % 2]
        return [(s, wire.push((fin, 2 * s + other), (rxz, s), partner)) for s in done]

    def reduce_5(k, copies):
        for s, copy in copies:
            copy.wait_recv()
            out, peak, total = merge([fin[2 * s + z], rxz[s]])
            lat[s * QROWS : (s + 1) * QROWS, :] = (out / total).astype(BF16)

    state = [None] * len(chunks)

    def run(steps):
        for step, k in steps:
            state[k] = step(k, state[k])

    loads[0].wait()
    run([(gather_0, 0), (gather_0, 1)])
    run([(gather_1, 0), (gather_0, 2), (gather_1, 1)])
    run([(gather_3, 0), (gather_0, 3), (gather_1, 2)])
    run([(gather_3, 1), (gather_0, 4), (gather_1, 3)])
    run([(gather_4, 0), (gather_0, 5), (gather_3, 2)])
    run([(gather_1, 4), (gather_4, 1), (gather_1, 5)])
    run([(gather_3, 3)])
    for copy in loads[1:4]:
        copy.wait()
    run([(gather_5, 0)])
    between = {
        1: [
            (gather_4, 2),
            (reduce_1, 0),
            (gather_5, 1),
            (gather_3, 4),
        ],
        2: [
            (gather_4, 3),
            (gather_5, 2),
            (gather_3, 5),
            (reduce_1, 1),
        ],
        3: [
            (reduce_1, 2),
            (gather_4, 4),
            (reduce_2, 0),
            (gather_5, 3),
        ],
        4: [
            (reduce_2, 1),
            (gather_4, 5),
            (reduce_1, 3),
            (reduce_2, 2),
            (gather_5, 4),
        ],
        5: [
            (reduce_3, 0),
            (reduce_3, 1),
            (gather_5, 5),
            (reduce_1, 4),
        ],
    }

    @pl.loop(0, 6)
    def _(t):
        for at_, steps in between.items():
            if steps:

                @pl.when(t == at_)
                def _():
                    run(steps)

        attend(t)

    run([(reduce_1, 5), (reduce_4, 0), (reduce_3, 2)])
    run([(reduce_4, 1), (reduce_2, 3), (reduce_2, 4)])
    run([(reduce_5, 0), (reduce_2, 5), (reduce_5, 1)])
    run([(reduce_4, 2), (reduce_3, 3), (reduce_5, 2)])
    run([(reduce_3, 4), (reduce_3, 5), (reduce_4, 3)])
    run([(reduce_4, 4), (reduce_4, 5), (reduce_5, 3)])
    run([(reduce_5, 4), (reduce_5, 5)])

    loads[4].wait()
    heads[g] = mm(lat[...], vup[...]).astype(BF16)
    copies = [wire.push((heads, g), (heads, g), mates[d]) for d in (1, 2, 3)]
    spread, gathered = [], []
    for part in range(2):
        seq, row = padded_row((128, 96), 0, part)
        j = iota((128, 96), 1)
        spread.append(
            ((seq < SEQS) & (j == seq * QROWS + row)).astype(F32).astype(BF16)
        )
        seq, row = padded_row((96, 128), 1, part)
        j = iota((96, 128), 0)
        gathered.append(
            ((seq < SEQS) & (j == seq * QROWS + row)).astype(F32).astype(BF16)
        )
    arrive(copies)
    loads[5].wait()
    own_resid[...] = jnp.zeros((16, QUARTER), BF16)
    own_resid[0:SEQS, :] = resid_ref[0, :, columns]
    lane = iota((1, 128), 1)
    gates = jnp.zeros((1, 128), F32)
    for s in range(SEQS):
        for r in range(4):
            here = lane == s * EXPERTS + routes_ref[s, :, r : r + 1]
            gates = gates + jnp.where(here, weight_ref[0, s : s + 1, r : r + 1].astype(F32), 0.0)
    for part in range(2):
        cols = pl.ds(part * HALF, HALF)
        seq, row = padded_row((128, 16), 0, part)
        mine = ((row == c) & (seq == iota((128, 16), 1)) & (seq < SEQS)).astype(F32).astype(BF16)
        value = mm(mine, own_resid[:, cols])
        for k in range(4):
            rows = mm(spread[part], heads[k]).astype(BF16)
            value = value + mm(rows, wout[k * DV : (k + 1) * DV, cols])
        pbuf[part] = value.astype(BF16).reshape(4, 32, HALF)
        if part == 0:
            seq, row = padded_row((128, 128), 0, part)
            head = jnp.where((seq == SEQS) & (row == c), gates, value[:, :128])
            pbuf[part, :, :, :128] = head.astype(BF16).reshape(4, 32, 128)

    def scatter(source, landing):
        copies = []
        for part, (fs, es, to_f, to_e) in enumerate(axes):
            for d in (1, 2, 3):
                copies.append(wire.push((source, part, fs[d]), (landing, part, d - 1), to_f[d]))
        return copies

    def summed(first, landing, part):
        value = first.astype(F32)
        for d in range(3):
            value = value + landing[part, d].astype(F32)
        return value

    copies = scatter(pbuf, rxa)
    arrive(copies)
    copies = []
    for part, (fs, es, to_f, to_e) in enumerate(axes):
        value = summed(pbuf[part, fs[0]], rxa, part)
        for k in range(4):
            ebuf[part, k] = fold(value[k * 8 : (k + 1) * 8])
        for d in (1, 2, 3):
            copies.append(wire.push((ebuf, part, es[d]), (rxb, part, d - 1), to_e[d]))
    arrive(copies)
    copies = []
    for part, (fs, es, to_f, to_e) in enumerate(axes):
        zbuf[part, z, es[0]] = summed(ebuf[part, es[0]], rxb, part).astype(BF16)
        ref = (zbuf, part, z, es[0])
        for peer in [far] + to_e[1:] + far_e[part][1:]:
            copies.append(wire.push(ref, ref, peer))
    arrive(copies)
    copies = []
    for part, (fs, es, to_f, to_e) in enumerate(axes):
        for k in range(4):
            hidf[part, k] = (
                (unfold(zbuf[part, 0, k]) + unfold(zbuf[part, 1, k])).astype(BF16).astype(F32)
            )
        hid[part, fs[0]] = hidf[part].reshape(32, HALF).astype(BF16)
        for d in (1, 2, 3):
            ref = (hid, part, fs[0])
            copies.append(wire.push(ref, ref, to_f[d]))
    arrive(copies)

    loads[6].wait()
    loads[7].wait()
    eye = iota((96, 128), 0) == iota((96, 128), 1)
    squares = jnp.zeros((96, 1), F32)
    gate = jnp.zeros((96, 512), F32)
    rise = jnp.zeros((96, 512), F32)
    for part in range(2):
        rows = mm(gathered[part], hid[part].reshape(128, HALF))
        squares = squares + jnp.sum(rows * rows, axis=-1, keepdims=True)
        cols = pl.ds(part * HALF, HALF)
        scaled = jnp.concatenate(
            [
                rows[:, n * 128 : (n + 1) * 128] * gain_ref[pl.ds(g * 14 + part * 7 + n, 1), :]
                for n in range(7)
            ],
            axis=1,
        ).astype(BF16)
        gate = gate + mm(scaled, wg[cols, :])
        rise = rise + mm(scaled, wu[cols, :])
    sq[...] = jnp.broadcast_to(
        jnp.sum(jnp.where(eye, squares, 0.0), axis=0, keepdims=True), (8, 128)
    )
    for j in range(4):
        gs[j, :, :128] = gate[:, j * 128 : (j + 1) * 128].astype(BF16)
        gs[j, :, 128:] = rise[:, j * 128 : (j + 1) * 128].astype(BF16)
    copies = []
    for d in (1, 2, 3):
        copies.append(wire.push((sq,), (rxs, d - 1), mates[d]))
        copies.append(wire.push((gs, gs_of[d]), (rxg, d - 1), mates[d]))
    table = hid[0, :, :, :128].reshape(128, 128)
    factors = []
    for part in range(2):
        seq, row = padded_row((128, 128), 0, part)
        pick = (iota((128, 128), 1) == row * 4 + SEQS).astype(F32).astype(BF16)
        here = iota((128, 128), 1) == seq * EXPERTS + c // SPLIT
        factors.append(
            jnp.sum(jnp.where(here, mm(pick, table), 0.0), axis=-1, keepdims=True)
        )
    arrive(copies)
    both = gs[g].astype(F32)
    total = sq[0:1, :]
    for d in range(3):
        both = both + rxg[d].astype(F32)
        total = total + rxs[d, 0:1, :]
    total = jnp.sum(jnp.where(eye, total, 0.0), axis=-1, keepdims=True)
    both = both * lax.rsqrt(total * (1.0 / D) + 1e-06)
    gate, rise = both[:, :128], both[:, 128:]
    units[g] = (gate / (1.0 + jnp.exp(-gate)) * rise).astype(BF16)
    copies = [wire.push((units, g), (units, g), mates[d]) for d in (1, 2, 3)]
    arrive(copies)
    loads[8].wait()
    for part in range(2):
        cols = pl.ds(part * HALF, HALF)
        value = jnp.zeros((128, HALF), F32)
        for k in range(4):
            rows = mm(spread[part], units[k]).astype(BF16)
            value = value + mm(rows, wd[k * 128 : (k + 1) * 128, cols])
        value = value.astype(BF16).astype(F32) * factors[part]
        part_buf[part] = value.astype(BF16).reshape(4, 32, HALF)
    copies = scatter(part_buf, rxq)
    arrive(copies)
    copies = []
    for part, (fs, es, to_f, to_e) in enumerate(axes):
        ybuf[part] = summed(part_buf[part, fs[0]], rxq, part).reshape(4, 8, HALF)
        for d in (1, 2, 3):
            copies.append(wire.push((ybuf, part, es[d]), (rxy, part, d - 1), to_e[d]))
    arrive(copies)
    for part, (fs, es, to_f, to_e) in enumerate(axes):
        wbuf[part] = summed(ybuf[part, es[0]], rxy, part)
    for part, (fs, es, to_f, to_e) in enumerate(axes):
        value, whole = wbuf[part], hidf[part, es[0]] + wbuf[part]
        fo[0, g, part * 4 : (part + 1) * 4, :] = jnp.where(z == 0, whole[0:4], whole[4:8])
        gone[part * 4 : (part + 1) * 4, :] = jnp.where(z == 0, value[4:8], value[0:4])
    copies = [wire.push((gone,), (fo, 1, g), far_mates[d]) for d in range(4)]
    copies += [wire.push((fo, 0, g), (fo, 0, g), mates[d]) for d in (1, 2, 3)]
    arrive(copies)
    for k in range(4):
        both = fo[0, k] + fo[1, k]
        for part in range(2):
            at_ = k * QUARTER + part * HALF
            out_ref[:, at_ : at_ + HALF] = both[part * 4 : part * 4 + SEQS].astype(BF16)
    wire.finish()


def vmem():
    return pl.BlockSpec(memory_space=pltpu.VMEM)


def hbm():
    return pl.BlockSpec(memory_space=pl.ANY)


def on_device(
    queries, cache, value_up_weight, w_out, resid, norm_gain, routes, route_weight,
    w_gate, w_up, w_down,
):
    g, c, x, y, z = place()
    pair, core = lax.rem(g // 2 + z, 2), g % 2
    by_column = queries.reshape(SEQS, 16, 8, QK)
    lower = lax.dynamic_index_in_dim(by_column, 2 * pair + core, 2, keepdims=False)
    upper = lax.dynamic_index_in_dim(by_column, 4 + 2 * (1 - pair) + core, 2, keepdims=False)
    rows = jnp.stack([lower, upper], axis=1).reshape(2 * SEQS, 16, QK)
    mixed = pl.pallas_call(
        kernel,
        out_shape=jax.ShapeDtypeStruct((SEQS, D), BF16),
        in_specs=[vmem(), hbm(), hbm(), hbm(), vmem(), vmem(), vmem(), vmem(), hbm(), hbm(), hbm()],
        out_specs=vmem(),
        scratch_shapes=[
            pltpu.VMEM((6, 4, 4, 2, 16, QK), BF16),
            pltpu.VMEM((SEQS, QK, CTX_DEV), BF16),
            pltpu.VMEM((256, CTX_DEV), F32),
            pltpu.VMEM((256, CTX_DEV), F32),
            pltpu.VMEM((256, CTX_DEV), BF16),
            pltpu.VMEM((256, CTX_DEV), BF16),
            pltpu.VMEM((2, 5, 256, 128), F32),
            pltpu.VMEM((6, 2, 4, 4, 16, QPAD), BF16),
            pltpu.VMEM((6, 2, 2, 2, 16, QPAD), BF16),
            pltpu.VMEM((6, 2, 2, 4, 16, QPAD), BF16),
            pltpu.VMEM((6, 2, 3, 16, QPAD), BF16),
            pltpu.VMEM((6, 2, 16, QPAD), BF16),
            pltpu.VMEM((SEQS, 2, 16, QPAD), BF16),
            pltpu.VMEM((96, KVL), BF16),
            pltpu.VMEM((KVL, DV), BF16),
            pltpu.VMEM((512, QUARTER), BF16),
            pltpu.VMEM((QUARTER, 512), BF16),
            pltpu.VMEM((QUARTER, 512), BF16),
            pltpu.VMEM((512, QUARTER), BF16),
            pltpu.VMEM((16, QUARTER), BF16),
            pltpu.VMEM((4, 96, DV), BF16),
            pltpu.VMEM((2, 4, 32, HALF), BF16),
            pltpu.VMEM((2, 3, 32, HALF), BF16),
            pltpu.VMEM((2, 4, 16, 512), BF16),
            pltpu.VMEM((2, 3, 16, 512), BF16),
            pltpu.VMEM((2, 2, 4, 16, 512), BF16),
            pltpu.VMEM((2, 4, 32, HALF), BF16),
            pltpu.VMEM((2, 4, 8, HALF), F32),
            pltpu.VMEM((8, 128), F32),
            pltpu.VMEM((3, 8, 128), F32),
            pltpu.VMEM((4, 96, 256), BF16),
            pltpu.VMEM((3, 96, 256), BF16),
            pltpu.VMEM((4, 96, 128), BF16),
            pltpu.VMEM((2, 4, 32, HALF), BF16),
            pltpu.VMEM((2, 3, 32, HALF), BF16),
            pltpu.VMEM((2, 4, 8, HALF), F32),
            pltpu.VMEM((2, 3, 8, HALF), F32),
            pltpu.VMEM((2, 8, HALF), F32),
            pltpu.VMEM((8, HALF), F32),
            pltpu.VMEM((2, 4, 8, HALF), F32),
            pltpu.SemaphoreType.DMA((250,)),
            pltpu.SemaphoreType.DMA((250,)),
            pltpu.SemaphoreType.DMA((11,)),
        ],
        compiler_params=pltpu.CompilerParams(
            collective_id=0, has_side_effects=True, vmem_limit_bytes=60 * 1024 * 1024
        ),
    )(
        rows,
        jnp.swapaxes(cache, 1, 2),
        value_up_weight,
        w_out,
        jnp.swapaxes(resid, 0, 1),
        norm_gain.reshape(D // 128, 128),
        routes,
        jnp.swapaxes(route_weight, 0, 1),
        w_gate,
        w_up,
        w_down,
    )
    return mixed.reshape(SEQS, 1, D)


def solution(mesh):
    placed = (
        P(None, "cp", None),
        P(None, "cp", None),
        P("cp", None, None),
        P("cp", None),
        P(None, "cp", None),
        P(),
        P(None, "cp", None),
        P(None, "cp", None),
        P("cp", "grp", None),
        P("cp", "grp", None),
        P("cp", None, "grp"),
    )
    return jax.shard_map(
        on_device, mesh=mesh, in_specs=placed, out_specs=P(None, "cp", None), check_vma=False
    )
```

```python
import math

import jax
import jax.numpy as jnp
from jax import lax
from jax.experimental import pallas as pl
from jax.experimental.pallas import tpu as pltpu
from jax.sharding import PartitionSpec as P

D = 7168
KVL = 512
DV = 128
SPLIT = 4
QROWS = 32
CTX_DEV = 2048
QK = 576
QPAD = 640
SEQS = 3
EXPERTS = 8
QUARTER = D // 4
HALF = QUARTER // 2
N_CP = 32
CTX = CTX_DEV * N_CP

SCALE = 192.0 ** (-0.5)
SCALE2 = SCALE * math.log2(math.e)
MESH = pl.DeviceIdType.MESH
F32 = jnp.float32
BF16 = jnp.bfloat16


def place():
    g = lax.axis_index("grp")
    c = lax.axis_index("cp")
    return g, c, c // 8, (c // 2) % 4, c % 2


def mm(a, b):
    return jnp.dot(a, b, preferred_element_type=F32)


def mm_nt(a, b):
    return lax.dot_general(a, b, (((1,), (1,)), ((), ())), preferred_element_type=F32)


def iota(shape, axis):
    return lax.broadcasted_iota(jnp.int32, shape, axis)


def part_of(ref, *index):
    return ref.at[index] if index else ref


class Wire:
    def __init__(self, send_sems, recv_sems):
        self.send_sems, self.recv_sems = send_sems, recv_sems
        self.started = []

    def push(self, src, dst, device):
        copy = Copy(self, len(self.started), src, dst, device)
        self.started.append(copy)
        copy.make().start()
        return copy

    def finish(self):
        for copy in self.started:
            copy.make().wait_send()


class Copy:
    def __init__(self, wire, at, src, dst, device):
        self.wire, self.at, self.src, self.dst, self.device = wire, at, src, dst, device

    def make(self):
        return pltpu.make_async_remote_copy(
            src_ref=part_of(*self.src),
            dst_ref=part_of(*self.dst),
            send_sem=self.wire.send_sems.at[self.at],
            recv_sem=self.wire.recv_sems.at[self.at],
            device_id=self.device,
            device_id_type=MESH,
        )

    def wait_recv(self):
        self.make().wait_recv()


def arrive(copies):
    for copy in copies:
        copy.wait_recv()


def fold(value):
    rest = jnp.concatenate([value[:, 512:], jnp.zeros((8, 128), value.dtype)], axis=1)
    return jnp.concatenate([value[:, :512], rest], axis=0).astype(BF16)


def unfold(value):
    value = value.astype(F32)
    return jnp.concatenate([value[:8], value[8:, : HALF - 512]], axis=1)


def greet(peers):
    barrier = pltpu.get_barrier_semaphore()
    for peer in peers:
        pl.semaphore_signal(barrier, inc=1, device_id=peer, device_id_type=MESH)
    pl.semaphore_wait(barrier, len(peers))


def padded_row(shape, axis, part):
    r = iota(shape, axis)
    s, z, b, a = r % 4, (r // 4) % 2, (r // 8) % 4, r // 32
    x, y = (a, b) if part == 0 else (b, a)
    return s, (x * 4 + y) * 2 + z


def unpack(value):
    value = value.reshape(-1, QPAD).astype(F32)
    aux = value[:, KVL:]
    lane = iota(aux.shape, 1)
    peak = jnp.sum(jnp.where(lane == 0, aux, 0.0), axis=-1, keepdims=True)
    total = jnp.sum(jnp.where((lane == 1) | (lane == 2), aux, 0.0), axis=-1, keepdims=True)
    return value[:, :KVL], peak, total


def aux_lanes(peak, total):
    lane = iota((peak.shape[0], QPAD - KVL), 1)
    high = total.astype(BF16).astype(F32)
    low = total - high
    return jnp.where(
        lane == 0, peak, jnp.where(lane == 1, high, jnp.where(lane == 2, low, 0.0))
    )


def merge(values):
    items = [unpack(value) for value in values]
    peak = items[0][1]
    for item in items[1:]:
        peak = jnp.maximum(peak, item[1])
    out, total = None, None
    for item in items:
        factor = jnp.exp((item[1] - peak) * SCALE)
        if out is None:
            out, total = item[0] * factor, item[2] * factor
        else:
            out, total = out + item[0] * factor, total + item[2] * factor
    return out, peak, total


def put(ref, merged):
    out, peak, total = merged
    ref[..., :KVL] = out.astype(BF16).reshape(*ref.shape[:-1], KVL)
    ref[..., KVL:] = aux_lanes(peak, total).astype(BF16).reshape(*ref.shape[:-1], QPAD - KVL)


def kernel(
    lower_ref, upper_ref, cache_ref, vup_ref, wout_ref, resid_ref, gain_ref, routes_ref, weight_ref,
    wg_ref, wu_ref, wd_ref, out_ref,
    qbuf, kv, score_a, score_b, prob_a, prob_b, oscr, msg, rx1, rx2, rx3, fin, rxz, lat,
    vup, wout, wg, wu, wd, own_resid, heads, pbuf, rxa, ebuf, rxb, zbuf, hid, hidf,
    sq, rxs, gs, rxg, units, part_buf, rxq, ybuf, rxy, wbuf, gone, fo,
    send_sems, recv_sems, local_sems,
):
    g, c, x, y, z = place()
    up = lambda v, d: lax.rem(v + d, 4)

    def at(px, py, pz):
        return (g, (px * 4 + py) * 2 + pz)

    xs = [x] + [up(x, d) for d in (1, 2, 3)]
    ys = [y] + [up(y, d) for d in (1, 2, 3)]
    to_x = [None] + [at(xs[d], y, z) for d in (1, 2, 3)]
    to_y = [None] + [at(x, ys[d], z) for d in (1, 2, 3)]
    partner = (lax.rem(g + 2, 4), (x * 4 + y) * 2 + (1 - z))
    far = at(x, y, 1 - z)
    far_x = [None] + [at(xs[d], y, 1 - z) for d in (1, 2, 3)]
    far_y = [None] + [at(x, ys[d], 1 - z) for d in (1, 2, 3)]
    gs_of = [g] + [up(g, d) for d in (1, 2, 3)]
    mates = [None] + [(gs_of[d], c) for d in (1, 2, 3)]
    far_mates = [(gs_of[d], (x * 4 + y) * 2 + (1 - z)) for d in range(4)]
    columns = pl.ds(pl.multiple_of(g * QUARTER, 128), QUARTER)
    q_refs = [(lower_ref, upper_ref)[t % 2].at[t // 2] for t in range(6)]
    pairs = [(q_refs[t], qbuf.at[t, x, y, z]) for t in range(6)]
    pairs += [(cache_ref.at[s], kv.at[s]) for s in range(SEQS)]
    pairs += [
        (vup_ref.at[g], vup),
        (wout_ref.at[:, columns], wout),
        (wg_ref.at[0], wg),
        (wu_ref.at[0], wu),
        (wd_ref.at[0], wd),
    ]
    loads = [
        pltpu.make_async_copy(src, dst, local_sems.at[n]) for n, (src, dst) in enumerate(pairs)
    ]
    for copy in loads:
        copy.start()

    greet(
        to_x[1:] + to_y[1:] + mates[1:] + far_x[1:] + far_y[1:] + far_mates
    )
    wire = Wire(send_sems, recv_sems)

    chunks = [(0, 1), (1, 1), (2, 1), (3, 1), (4, 1), (5, 1)]
    dirs = (1, 3)
    other = 1 - z

    def gather_0(k, _):
        return [wire.push((q_refs[k],), (qbuf, k, x, y, z), partner)]

    def gather_1(k, copies):
        arrive(copies)
        span = pl.ds(*chunks[k])
        copies = []
        for d in (1, 2, 3):
            ref = (qbuf, span, x, y, 0)
            copies.append(wire.push(ref, ref, to_x[d]))
            ref = (qbuf, span, x, y, 1)
            copies.append(wire.push(ref, ref, to_y[d]))
        return copies

    def gather_3(k, copies):
        arrive(copies)
        span = pl.ds(*chunks[k])
        copies = []
        for d in dirs:
            ref = (qbuf, span, slice(None), y, 0)
            copies.append(wire.push(ref, ref, to_y[d]))
            ref = (qbuf, span, x, slice(None), 1)
            copies.append(wire.push(ref, ref, to_x[d]))
        return copies

    def gather_4(k, copies):
        arrive(copies)
        span = pl.ds(*chunks[k])
        copies = []
        for n, d in enumerate(dirs):
            ref = (qbuf, span, pl.ds(2 * n, 2), ys[4 - d], 0)
            copies.append(wire.push(ref, ref, to_y[d]))
            ref = (qbuf, span, xs[4 - d], pl.ds(2 * n, 2), 1)
            copies.append(wire.push(ref, ref, to_x[d]))
        return copies

    def gather_5(k, copies):
        arrive(copies)

    def scores(t, s, part, score):
        q = qbuf[t, 2 * part : 2 * part + 2].reshape(256, QK)
        for n in range(4):
            keys = pl.ds(n * 512, 512)
            value = mm(q, kv[s, :, keys])
            if n < 3:
                score[:, keys] = value
            else:
                score[:, 1536:1920] = value[:, :384]
                row = 16 * part + iota((256, 128), 0) // 16
                position = c * CTX_DEV + 1920 + iota((256, 128), 1)
                score[:, 1920:] = jnp.where(
                    position <= CTX - QROWS + row, value[:, 384:], -1e30
                )

    def weigh(t, s, part, score, prob):
        peak = jnp.max(score[...], axis=-1, keepdims=True).astype(BF16).astype(F32)
        total = jnp.zeros((256, 128), F32)
        for n in range(4):
            keys = pl.ds(n * 512, 512)
            weight = jnp.exp2((score[:, keys] - peak) * SCALE2)
            for m in range(4):
                total = total + weight[:, m * 128 : (m + 1) * 128]
            prob[:, keys] = weight.astype(BF16)
        total = jnp.sum(total, axis=-1, keepdims=True)
        out = mm_nt(prob[...], kv[s, :KVL, :])
        for m in range(4):
            oscr[part, m] = out[:, m * 128 : (m + 1) * 128]
        oscr[part, 4] = aux_lanes(peak, total)
        for n in range(16):
            a, b = (n // 4, n % 4) if part == 0 else (n % 4, n // 4)
            for m in range(5):
                lanes = pl.ds(m * 128, 128)
                msg[t, part, a, b, :, lanes] = oscr[
                    part, m, pl.ds(n, 16, stride=16), :
                ].astype(BF16)

    def attend(t):
        s = t // 2
        scores(t, s, 0, score_a)
        scores(t, s, 1, score_b)
        weigh(t, s, 0, score_a, prob_a)
        weigh(t, s, 1, score_b, prob_b)

    axes = [(xs, ys, to_x, to_y), (ys, xs, to_y, to_x)]
    far_e = [far_y, far_x]

    def reduce_1(k, _):
        span = pl.ds(*chunks[k])
        copies = []
        for part, (fs, es, to_f, to_e) in enumerate(axes):
            for n, d in enumerate(dirs):
                src = (msg, span, part, fs[2], pl.ds(2 * n, 2))
                copies.append(wire.push(src, (rx1, span, part, n), to_f[d]))
        return copies

    def reduce_2(k, copies):
        arrive(copies)
        span = pl.ds(*chunks[k])
        copies = []
        for part, (fs, es, to_f, to_e) in enumerate(axes):
            for n, d in enumerate(dirs):

                @pl.loop(chunks[k][0], sum(chunks[k]))
                def _(t):
                    ref = msg.at[t, part, fs[d], pl.ds(2 * n, 2)]
                    put(ref, merge([ref[...], rx1[t, part, n]]))

                copies.append(
                    wire.push((msg, span, part, fs[d]), (rx2, span, part, n), to_f[d])
                )
        return copies

    def reduce_3(k, copies):
        arrive(copies)
        span = pl.ds(*chunks[k])
        copies = []
        for part, (fs, es, to_f, to_e) in enumerate(axes):

            @pl.loop(2 * chunks[k][0], 2 * sum(chunks[k]))
            def _(at_):
                t, units = at_ // 2, pl.ds(2 * (at_ % 2), 2)
                ref = msg.at[t, part, fs[0], units]
                put(ref, merge([ref[...], rx2[t, part, 0, units], rx2[t, part, 1, units]]))

            for d in (1, 2, 3):
                src = (msg, span, part, fs[0], es[d])
                copies.append(wire.push(src, (rx3, span, part, d - 1), to_e[d]))
        return copies

    def reduce_4(k, copies):
        arrive(copies)

        @pl.loop(chunks[k][0], sum(chunks[k]))
        def _(t):
            for part, (fs, es, to_f, to_e) in enumerate(axes):
                put(
                    fin.at[t, part],
                    merge([msg[t, part, fs[0], es[0]]] + [rx3[t, part, d] for d in range(3)]),
                )

        finished.add(k)
        if {2 * (k // 2), 2 * (k // 2) + 1} <= finished:
            return [(k // 2, wire.push((fin, 2 * (k // 2) + other), (rxz, k // 2), partner))]
        return []

    def reduce_5(k, copies):
        for s, copy in copies:
            copy.wait_recv()
            out, peak, total = merge([fin[2 * s + z], rxz[s]])
            lat[s * QROWS : (s + 1) * QROWS, :] = (out / total).astype(BF16)

    state, finished = [None] * len(chunks), set()

    def run(steps):
        for step, k in steps:
            state[k] = step(k, state[k])

    for copy in loads[:6]:
        copy.wait()
    run([(gather_0, 0), (gather_0, 1), (gather_0, 2)])
    run([(gather_1, 0), (gather_1, 1), (gather_1, 2)])
    run([(gather_3, 0), (gather_3, 1), (gather_0, 3)])
    run([(gather_3, 2), (gather_0, 4), (gather_1, 3)])
    run([(gather_4, 0), (gather_0, 5), (gather_1, 4)])
    run([(gather_4, 1), (gather_1, 5), (gather_4, 2)])
    run([(gather_3, 3)])
    for copy in loads[6:9]:
        copy.wait()
    run([(gather_5, 0)])
    between = {
        1: [
            (reduce_1, 0),
            (gather_3, 5),
            (gather_5, 2),
            (gather_5, 1),
            (gather_3, 4),
        ],
        2: [
            (gather_4, 3),
            (reduce_1, 1),
            (reduce_2, 0),
        ],
        3: [
            (gather_4, 5),
            (gather_5, 3),
            (reduce_1, 2),
            (gather_4, 4),
        ],
        4: [
            (reduce_1, 3),
            (reduce_2, 1),
            (gather_5, 5),
            (reduce_3, 0),
            (reduce_2, 2),
        ],
        5: [
            (reduce_1, 5),
            (reduce_2, 3),
            (reduce_3, 1),
            (gather_5, 4),
        ],
    }

    @pl.loop(0, 6)
    def _(t):
        for at_, steps in between.items():
            if steps:

                @pl.when(t == at_)
                def _():
                    run(steps)

        attend(jnp.where(t >= 4, 9 - t, t))

    run([(reduce_1, 4), (reduce_2, 5), (reduce_4, 0)])
    run([(reduce_3, 2), (reduce_3, 3), (reduce_4, 1)])
    run([(reduce_2, 4), (reduce_5, 0), (reduce_3, 5)])
    run([(reduce_5, 1), (reduce_4, 2), (reduce_4, 3)])
    run([(reduce_3, 4), (reduce_5, 2), (reduce_4, 5)])
    run([(reduce_5, 3), (reduce_4, 4), (reduce_5, 5)])
    run([(reduce_5, 4)])

    loads[9].wait()
    heads[g] = mm(lat[...], vup[...]).astype(BF16)
    copies = [wire.push((heads, g), (heads, g), mates[d]) for d in (1, 2, 3)]
    spread, gathered = [], []
    for part in range(2):
        seq, row = padded_row((128, 96), 0, part)
        j = iota((128, 96), 1)
        spread.append(
            ((seq < SEQS) & (j == seq * QROWS + row)).astype(F32).astype(BF16)
        )
        seq, row = padded_row((96, 128), 1, part)
        j = iota((96, 128), 0)
        gathered.append(
            ((seq < SEQS) & (j == seq * QROWS + row)).astype(F32).astype(BF16)
        )
    arrive(copies)
    loads[10].wait()
    own_resid[...] = jnp.zeros((16, QUARTER), BF16)
    own_resid[0:SEQS, :] = resid_ref[0, :, columns]
    lane = iota((1, 128), 1)
    gates = jnp.zeros((1, 128), F32)
    for s in range(SEQS):
        for r in range(4):
            here = lane == s * EXPERTS + routes_ref[s, :, r : r + 1]
            gates = gates + jnp.where(here, weight_ref[0, s : s + 1, r : r + 1].astype(F32), 0.0)
    for part in range(2):
        cols = pl.ds(part * HALF, HALF)
        seq, row = padded_row((128, 16), 0, part)
        mine = ((row == c) & (seq == iota((128, 16), 1)) & (seq < SEQS)).astype(F32).astype(BF16)
        value = mm(mine, own_resid[:, cols])
        for k in range(4):
            rows = mm(spread[part], heads[k]).astype(BF16)
            value = value + mm(rows, wout[k * DV : (k + 1) * DV, cols])
        pbuf[part] = value.astype(BF16).reshape(4, 32, HALF)
        if part == 0:
            seq, row = padded_row((128, 128), 0, part)
            head = jnp.where((seq == SEQS) & (row == c), gates, value[:, :128])
            pbuf[part, :, :, :128] = head.astype(BF16).reshape(4, 32, 128)

    def scatter(source, landing):
        copies = []
        for part, (fs, es, to_f, to_e) in enumerate(axes):
            for d in (1, 2, 3):
                copies.append(wire.push((source, part, fs[d]), (landing, part, d - 1), to_f[d]))
        return copies

    def summed(first, landing, part):
        value = first.astype(F32)
        for d in range(3):
            value = value + landing[part, d].astype(F32)
        return value

    copies = scatter(pbuf, rxa)
    arrive(copies)
    copies = []
    for part, (fs, es, to_f, to_e) in enumerate(axes):
        value = summed(pbuf[part, fs[0]], rxa, part)
        for k in range(4):
            ebuf[part, k] = fold(value[k * 8 : (k + 1) * 8])
        for d in (1, 2, 3):
            copies.append(wire.push((ebuf, part, es[d]), (rxb, part, d - 1), to_e[d]))
    arrive(copies)
    copies = []
    for part, (fs, es, to_f, to_e) in enumerate(axes):
        zbuf[part, z, es[0]] = summed(ebuf[part, es[0]], rxb, part).astype(BF16)
        ref = (zbuf, part, z, es[0])
        for peer in [far] + to_e[1:] + far_e[part][1:]:
            copies.append(wire.push(ref, ref, peer))
    arrive(copies)
    copies = []
    for part, (fs, es, to_f, to_e) in enumerate(axes):
        for k in range(4):
            hidf[part, k] = (
                (unfold(zbuf[part, 0, k]) + unfold(zbuf[part, 1, k])).astype(BF16).astype(F32)
            )
        hid[part, fs[0]] = hidf[part].reshape(32, HALF).astype(BF16)
        for d in (1, 2, 3):
            ref = (hid, part, fs[0])
            copies.append(wire.push(ref, ref, to_f[d]))
    arrive(copies)

    loads[11].wait()
    loads[12].wait()
    eye = iota((96, 128), 0) == iota((96, 128), 1)
    squares = jnp.zeros((96, 1), F32)
    gate = jnp.zeros((96, 512), F32)
    rise = jnp.zeros((96, 512), F32)
    for part in range(2):
        rows = mm(gathered[part], hid[part].reshape(128, HALF))
        squares = squares + jnp.sum(rows * rows, axis=-1, keepdims=True)
        cols = pl.ds(part * HALF, HALF)
        scaled = jnp.concatenate(
            [
                rows[:, n * 128 : (n + 1) * 128] * gain_ref[pl.ds(g * 14 + part * 7 + n, 1), :]
                for n in range(7)
            ],
            axis=1,
        ).astype(BF16)
        gate = gate + mm(scaled, wg[cols, :])
        rise = rise + mm(scaled, wu[cols, :])
    sq[...] = jnp.broadcast_to(
        jnp.sum(jnp.where(eye, squares, 0.0), axis=0, keepdims=True), (8, 128)
    )
    for j in range(4):
        gs[j, :, :128] = gate[:, j * 128 : (j + 1) * 128].astype(BF16)
        gs[j, :, 128:] = rise[:, j * 128 : (j + 1) * 128].astype(BF16)
    copies = []
    for d in (1, 2, 3):
        copies.append(wire.push((sq,), (rxs, d - 1), mates[d]))
        copies.append(wire.push((gs, gs_of[d]), (rxg, d - 1), mates[d]))
    table = hid[0, :, :, :128].reshape(128, 128)
    factors = []
    for part in range(2):
        seq, row = padded_row((128, 128), 0, part)
        pick = (iota((128, 128), 1) == row * 4 + SEQS).astype(F32).astype(BF16)
        here = iota((128, 128), 1) == seq * EXPERTS + c // SPLIT
        factors.append(
            jnp.sum(jnp.where(here, mm(pick, table), 0.0), axis=-1, keepdims=True)
        )
    arrive(copies)
    both = gs[g].astype(F32)
    total = sq[0:1, :]
    for d in range(3):
        both = both + rxg[d].astype(F32)
        total = total + rxs[d, 0:1, :]
    total = jnp.sum(jnp.where(eye, total, 0.0), axis=-1, keepdims=True)
    both = both * lax.rsqrt(total * (1.0 / D) + 1e-06)
    gate, rise = both[:, :128], both[:, 128:]
    units[g] = (gate / (1.0 + jnp.exp(-gate)) * rise).astype(BF16)
    copies = [wire.push((units, g), (units, g), mates[d]) for d in (1, 2, 3)]
    arrive(copies)
    loads[13].wait()
    for part in range(2):
        cols = pl.ds(part * HALF, HALF)
        value = jnp.zeros((128, HALF), F32)
        for k in range(4):
            rows = mm(spread[part], units[k]).astype(BF16)
            value = value + mm(rows, wd[k * 128 : (k + 1) * 128, cols])
        value = value.astype(BF16).astype(F32) * factors[part]
        part_buf[part] = value.astype(BF16).reshape(4, 32, HALF)
    copies = scatter(part_buf, rxq)
    arrive(copies)
    copies = []
    for part, (fs, es, to_f, to_e) in enumerate(axes):
        ybuf[part] = summed(part_buf[part, fs[0]], rxq, part).reshape(4, 8, HALF)
        for d in (1, 2, 3):
            copies.append(wire.push((ybuf, part, es[d]), (rxy, part, d - 1), to_e[d]))
    arrive(copies)
    for part, (fs, es, to_f, to_e) in enumerate(axes):
        wbuf[part] = summed(ybuf[part, es[0]], rxy, part)
    for part, (fs, es, to_f, to_e) in enumerate(axes):
        value, whole = wbuf[part], hidf[part, es[0]] + wbuf[part]
        fo[0, g, part * 4 : (part + 1) * 4, :] = jnp.where(z == 0, whole[0:4], whole[4:8])
        gone[part * 4 : (part + 1) * 4, :] = jnp.where(z == 0, value[4:8], value[0:4])
    copies = [wire.push((gone,), (fo, 1, g), far_mates[d]) for d in range(4)]
    copies += [wire.push((fo, 0, g), (fo, 0, g), mates[d]) for d in (1, 2, 3)]
    arrive(copies)
    for k in range(4):
        both = fo[0, k] + fo[1, k]
        for part in range(2):
            at_ = k * QUARTER + part * HALF
            out_ref[:, at_ : at_ + HALF] = both[part * 4 : part * 4 + SEQS].astype(BF16)
    wire.finish()


def vmem():
    return pl.BlockSpec(memory_space=pltpu.VMEM)


def hbm():
    return pl.BlockSpec(memory_space=pl.ANY)


def on_device(
    queries, cache, value_up_weight, w_out, resid, norm_gain, routes, route_weight,
    w_gate, w_up, w_down,
):
    g, c, x, y, z = place()
    pair, core = lax.rem(g // 2 + z, 2), g % 2
    by_column = queries.reshape(SEQS, 16, 8, QK)
    lower = lax.dynamic_index_in_dim(by_column, 2 * pair + core, 2, keepdims=False)
    upper = lax.dynamic_index_in_dim(by_column, 4 + 2 * (1 - pair) + core, 2, keepdims=False)
    mixed = pl.pallas_call(
        kernel,
        out_shape=jax.ShapeDtypeStruct((SEQS, D), BF16),
        in_specs=[vmem(), vmem(), hbm(), hbm(), hbm(), vmem(), vmem(), vmem(), vmem(), hbm(), hbm(), hbm()],
        out_specs=vmem(),
        scratch_shapes=[
            pltpu.VMEM((6, 4, 4, 2, 16, QK), BF16),
            pltpu.VMEM((SEQS, QK, CTX_DEV), BF16),
            pltpu.VMEM((256, CTX_DEV), F32),
            pltpu.VMEM((256, CTX_DEV), F32),
            pltpu.VMEM((256, CTX_DEV), BF16),
            pltpu.VMEM((256, CTX_DEV), BF16),
            pltpu.VMEM((2, 5, 256, 128), F32),
            pltpu.VMEM((6, 2, 4, 4, 16, QPAD), BF16),
            pltpu.VMEM((6, 2, 2, 2, 16, QPAD), BF16),
            pltpu.VMEM((6, 2, 2, 4, 16, QPAD), BF16),
            pltpu.VMEM((6, 2, 3, 16, QPAD), BF16),
            pltpu.VMEM((6, 2, 16, QPAD), BF16),
            pltpu.VMEM((SEQS, 2, 16, QPAD), BF16),
            pltpu.VMEM((96, KVL), BF16),
            pltpu.VMEM((KVL, DV), BF16),
            pltpu.VMEM((512, QUARTER), BF16),
            pltpu.VMEM((QUARTER, 512), BF16),
            pltpu.VMEM((QUARTER, 512), BF16),
            pltpu.VMEM((512, QUARTER), BF16),
            pltpu.VMEM((16, QUARTER), BF16),
            pltpu.VMEM((4, 96, DV), BF16),
            pltpu.VMEM((2, 4, 32, HALF), BF16),
            pltpu.VMEM((2, 3, 32, HALF), BF16),
            pltpu.VMEM((2, 4, 16, 512), BF16),
            pltpu.VMEM((2, 3, 16, 512), BF16),
            pltpu.VMEM((2, 2, 4, 16, 512), BF16),
            pltpu.VMEM((2, 4, 32, HALF), BF16),
            pltpu.VMEM((2, 4, 8, HALF), F32),
            pltpu.VMEM((8, 128), F32),
            pltpu.VMEM((3, 8, 128), F32),
            pltpu.VMEM((4, 96, 256), BF16),
            pltpu.VMEM((3, 96, 256), BF16),
            pltpu.VMEM((4, 96, 128), BF16),
            pltpu.VMEM((2, 4, 32, HALF), BF16),
            pltpu.VMEM((2, 3, 32, HALF), BF16),
            pltpu.VMEM((2, 4, 8, HALF), F32),
            pltpu.VMEM((2, 3, 8, HALF), F32),
            pltpu.VMEM((2, 8, HALF), F32),
            pltpu.VMEM((8, HALF), F32),
            pltpu.VMEM((2, 4, 8, HALF), F32),
            pltpu.SemaphoreType.DMA((250,)),
            pltpu.SemaphoreType.DMA((250,)),
            pltpu.SemaphoreType.DMA((14,)),
        ],
        compiler_params=pltpu.CompilerParams(
            collective_id=0, has_side_effects=True, vmem_limit_bytes=52 * 1024 * 1024
        ),
    )(
        lower,
        upper,
        jnp.swapaxes(cache, 1, 2),
        value_up_weight,
        w_out,
        jnp.swapaxes(resid, 0, 1),
        norm_gain.reshape(D // 128, 128),
        routes,
        jnp.swapaxes(route_weight, 0, 1),
        w_gate,
        w_up,
        w_down,
    )
    return mixed.reshape(SEQS, 1, D)


def solution(mesh):
    placed = (
        P(None, "cp", None),
        P(None, "cp", None),
        P("cp", None, None),
        P("cp", None),
        P(None, "cp", None),
        P(),
        P(None, "cp", None),
        P(None, "cp", None),
        P("cp", "grp", None),
        P("cp", "grp", None),
        P("cp", None, "grp"),
    )
    return jax.shard_map(
        on_device, mesh=mesh, in_specs=placed, out_specs=P(None, "cp", None), check_vma=False
    )
```

```python
import math

import jax
import jax.numpy as jnp
from jax import lax
from jax.experimental import pallas as pl
from jax.experimental.pallas import tpu as pltpu
from jax.sharding import PartitionSpec as P

D = 7168
KVL = 512
DV = 128
SPLIT = 4
QROWS = 32
CTX_DEV = 2048
QK = 576
QPAD = 640
SEQS = 3
EXPERTS = 8
QUARTER = D // 4
HALF = QUARTER // 2
N_CP = 32
CTX = CTX_DEV * N_CP

SCALE = 192.0 ** (-0.5)
SCALE2 = SCALE * math.log2(math.e)
MESH = pl.DeviceIdType.MESH
F32 = jnp.float32
BF16 = jnp.bfloat16


def place():
    g = lax.axis_index("grp")
    c = lax.axis_index("cp")
    return g, c, c // 8, (c // 2) % 4, c % 2


def mm(a, b):
    return jnp.dot(a, b, preferred_element_type=F32)


def mm_nt(a, b):
    return lax.dot_general(a, b, (((1,), (1,)), ((), ())), preferred_element_type=F32)


def iota(shape, axis):
    return lax.broadcasted_iota(jnp.int32, shape, axis)


def part_of(ref, *index):
    return ref.at[index] if index else ref


class Wire:
    def __init__(self, send_sems, recv_sems):
        self.send_sems, self.recv_sems = send_sems, recv_sems
        self.started = []

    def push(self, src, dst, device):
        copy = Copy(self, len(self.started), src, dst, device)
        self.started.append(copy)
        copy.make().start()
        return copy

    def finish(self):
        for copy in self.started:
            copy.make().wait_send()


class Copy:
    def __init__(self, wire, at, src, dst, device):
        self.wire, self.at, self.src, self.dst, self.device = wire, at, src, dst, device

    def make(self):
        return pltpu.make_async_remote_copy(
            src_ref=part_of(*self.src),
            dst_ref=part_of(*self.dst),
            send_sem=self.wire.send_sems.at[self.at],
            recv_sem=self.wire.recv_sems.at[self.at],
            device_id=self.device,
            device_id_type=MESH,
        )

    def wait_recv(self):
        self.make().wait_recv()


def arrive(copies):
    for copy in copies:
        copy.wait_recv()


def fold(value):
    rest = jnp.concatenate([value[:, 512:], jnp.zeros((8, 128), value.dtype)], axis=1)
    return jnp.concatenate([value[:, :512], rest], axis=0).astype(BF16)


def unfold(value):
    value = value.astype(F32)
    return jnp.concatenate([value[:8], value[8:, : HALF - 512]], axis=1)


def greet(peers):
    barrier = pltpu.get_barrier_semaphore()
    for peer in peers:
        pl.semaphore_signal(barrier, inc=1, device_id=peer, device_id_type=MESH)
    pl.semaphore_wait(barrier, len(peers))


def padded_row(shape, axis, part):
    r = iota(shape, axis)
    s, z, b, a = r % 4, (r // 4) % 2, (r // 8) % 4, r // 32
    x, y = (a, b) if part == 0 else (b, a)
    return s, (x * 4 + y) * 2 + z


def unpack(value):
    value = value.reshape(-1, QPAD).astype(F32)
    aux = value[:, KVL:]
    lane = iota(aux.shape, 1)
    peak = jnp.sum(jnp.where(lane == 0, aux, 0.0), axis=-1, keepdims=True)
    total = jnp.sum(jnp.where((lane == 1) | (lane == 2), aux, 0.0), axis=-1, keepdims=True)
    return value[:, :KVL], peak, total


def aux_lanes(peak, total):
    lane = iota((peak.shape[0], QPAD - KVL), 1)
    high = total.astype(BF16).astype(F32)
    low = total - high
    return jnp.where(
        lane == 0, peak, jnp.where(lane == 1, high, jnp.where(lane == 2, low, 0.0))
    )


def merge(values):
    items = [unpack(value) for value in values]
    peak = items[0][1]
    for item in items[1:]:
        peak = jnp.maximum(peak, item[1])
    out, total = None, None
    for item in items:
        factor = jnp.exp((item[1] - peak) * SCALE)
        if out is None:
            out, total = item[0] * factor, item[2] * factor
        else:
            out, total = out + item[0] * factor, total + item[2] * factor
    return out, peak, total


def put(ref, merged):
    out, peak, total = merged
    ref[..., :KVL] = out.astype(BF16).reshape(*ref.shape[:-1], KVL)
    ref[..., KVL:] = aux_lanes(peak, total).astype(BF16).reshape(*ref.shape[:-1], QPAD - KVL)


def kernel(
    lower_ref, upper_ref, cache_ref, vup_ref, wout_ref, resid_ref, gain_ref, routes_ref, weight_ref,
    wg_ref, wu_ref, wd_ref, out_ref,
    qbuf, kv, score_a, score_b, prob_a, prob_b, oscr, msg, rx1, rx2, rx3, fin, rxz,
    vup, wout, wg, wu, wd, own_resid, heads, pbuf, rxa, ebuf, rxb, zbuf, hid, hidf,
    sq, rxs, gs, rxg, units, part_buf, rxq, ybuf, rxy, wbuf, gone, fo,
    send_sems, recv_sems, local_sems,
):
    g, c, x, y, z = place()
    up = lambda v, d: lax.rem(v + d, 4)

    def at(px, py, pz):
        return (g, (px * 4 + py) * 2 + pz)

    xs = [x] + [up(x, d) for d in (1, 2, 3)]
    ys = [y] + [up(y, d) for d in (1, 2, 3)]
    to_x = [None] + [at(xs[d], y, z) for d in (1, 2, 3)]
    to_y = [None] + [at(x, ys[d], z) for d in (1, 2, 3)]
    partner = (lax.rem(g + 2, 4), (x * 4 + y) * 2 + (1 - z))
    far = at(x, y, 1 - z)
    far_x = [None] + [at(xs[d], y, 1 - z) for d in (1, 2, 3)]
    far_y = [None] + [at(x, ys[d], 1 - z) for d in (1, 2, 3)]
    gs_of = [g] + [up(g, d) for d in (1, 2, 3)]
    mates = [None] + [(gs_of[d], c) for d in (1, 2, 3)]
    far_mates = [(gs_of[d], (x * 4 + y) * 2 + (1 - z)) for d in range(4)]
    columns = pl.ds(pl.multiple_of(g * QUARTER, 128), QUARTER)
    q_refs = [(lower_ref, upper_ref)[t % 2].at[t // 2] for t in range(6)]
    pairs = [(q_refs[t], qbuf.at[t, x, y, z]) for t in range(6)]
    pairs += [(cache_ref.at[s], kv.at[s]) for s in range(SEQS)]
    pairs += [
        (vup_ref.at[g], vup),
        (wout_ref.at[:, columns], wout),
        (wg_ref.at[0], wg),
        (wu_ref.at[0], wu),
        (wd_ref.at[0], wd),
    ]
    loads = [
        pltpu.make_async_copy(src, dst, local_sems.at[n]) for n, (src, dst) in enumerate(pairs)
    ]
    for copy in loads:
        copy.start()

    greet(
        to_x[1:] + to_y[1:] + mates[1:] + far_x[1:] + far_y[1:] + far_mates
    )
    wire = Wire(send_sems, recv_sems)

    chunks = [(0, 1), (1, 1), (2, 1), (3, 1), (4, 1), (5, 1)]
    dirs = (1, 3)
    other = 1 - z

    def gather_0(k, _):
        return [wire.push((q_refs[k],), (qbuf, k, x, y, z), partner)]

    def gather_1(k, copies):
        arrive(copies)
        span = pl.ds(*chunks[k])
        copies = []
        for d in (1, 2, 3):
            ref = (qbuf, span, x, y, 0)
            copies.append(wire.push(ref, ref, to_x[d]))
            ref = (qbuf, span, x, y, 1)
            copies.append(wire.push(ref, ref, to_y[d]))
        return copies

    def gather_3(k, copies):
        arrive(copies)
        span = pl.ds(*chunks[k])
        copies = []
        for d in dirs:
            ref = (qbuf, span, slice(None), y, 0)
            copies.append(wire.push(ref, ref, to_y[d]))
            ref = (qbuf, span, x, slice(None), 1)
            copies.append(wire.push(ref, ref, to_x[d]))
        return copies

    def gather_4(k, copies):
        arrive(copies)
        span = pl.ds(*chunks[k])
        copies = []
        for n, d in enumerate(dirs):
            ref = (qbuf, span, pl.ds(2 * n, 2), ys[4 - d], 0)
            copies.append(wire.push(ref, ref, to_y[d]))
            ref = (qbuf, span, xs[4 - d], pl.ds(2 * n, 2), 1)
            copies.append(wire.push(ref, ref, to_x[d]))
        return copies

    def gather_5(k, copies):
        arrive(copies)

    def scores(t, s, part, score):
        q = qbuf[t, 2 * part : 2 * part + 2].reshape(256, QK)
        for n in range(4):
            keys = pl.ds(n * 512, 512)
            value = mm(q, kv[s, :, keys])
            if n < 3:
                score[:, keys] = value
            else:
                score[:, 1536:1920] = value[:, :384]
                row = 16 * part + iota((256, 128), 0) // 16
                position = c * CTX_DEV + 1920 + iota((256, 128), 1)
                score[:, 1920:] = jnp.where(
                    position <= CTX - QROWS + row, value[:, 384:], -1e30
                )

    def weigh(t, s, part, score, prob):
        peak = jnp.max(score[...], axis=-1, keepdims=True).astype(BF16).astype(F32)
        total = jnp.zeros((256, 128), F32)
        for n in range(4):
            keys = pl.ds(n * 512, 512)
            weight = jnp.exp2((score[:, keys] - peak) * SCALE2)
            for m in range(4):
                total = total + weight[:, m * 128 : (m + 1) * 128]
            prob[:, keys] = weight.astype(BF16)
        total = jnp.sum(total, axis=-1, keepdims=True)
        out = mm_nt(prob[...], kv[s, :KVL, :])
        for m in range(4):
            oscr[part, m] = out[:, m * 128 : (m + 1) * 128]
        oscr[part, 4] = aux_lanes(peak, total)
        for n in range(16):
            a, b = (n // 4, n % 4) if part == 0 else (n % 4, n // 4)
            for m in range(5):
                lanes = pl.ds(m * 128, 128)
                msg[t, part, a, b, :, lanes] = oscr[
                    part, m, pl.ds(n, 16, stride=16), :
                ].astype(BF16)

    def attend(t):
        s = t // 2
        scores(t, s, 0, score_a)
        scores(t, s, 1, score_b)
        weigh(t, s, 0, score_a, prob_a)
        weigh(t, s, 1, score_b, prob_b)

    axes = [(xs, ys, to_x, to_y), (ys, xs, to_y, to_x)]
    far_e = [far_y, far_x]

    def reduce_1(k, _):
        span = pl.ds(*chunks[k])
        copies = []
        for part, (fs, es, to_f, to_e) in enumerate(axes):
            for n, d in enumerate(dirs):
                src = (msg, span, part, fs[2], pl.ds(2 * n, 2))
                copies.append(wire.push(src, (rx1, span, part, n), to_f[d]))
        return copies

    def reduce_2(k, copies):
        arrive(copies)
        span = pl.ds(*chunks[k])
        copies = []
        for part, (fs, es, to_f, to_e) in enumerate(axes):
            for n, d in enumerate(dirs):

                @pl.loop(chunks[k][0], sum(chunks[k]))
                def _(t):
                    ref = msg.at[t, part, fs[d], pl.ds(2 * n, 2)]
                    put(ref, merge([ref[...], rx1[t, part, n]]))

                copies.append(
                    wire.push((msg, span, part, fs[d]), (rx2, span, part, n), to_f[d])
                )
        return copies

    def reduce_3(k, copies):
        arrive(copies)
        span = pl.ds(*chunks[k])
        copies = []
        for part, (fs, es, to_f, to_e) in enumerate(axes):

            @pl.loop(2 * chunks[k][0], 2 * sum(chunks[k]))
            def _(at_):
                t, units = at_ // 2, pl.ds(2 * (at_ % 2), 2)
                ref = msg.at[t, part, fs[0], units]
                put(ref, merge([ref[...], rx2[t, part, 0, units], rx2[t, part, 1, units]]))

            for d in (1, 2, 3):
                src = (msg, span, part, fs[0], es[d])
                copies.append(wire.push(src, (rx3, span, part, d - 1), to_e[d]))
        return copies

    def reduce_4(k, copies):
        arrive(copies)

        @pl.loop(chunks[k][0], sum(chunks[k]))
        def _(t):
            for part, (fs, es, to_f, to_e) in enumerate(axes):
                put(
                    fin.at[t, part],
                    merge([msg[t, part, fs[0], es[0]]] + [rx3[t, part, d] for d in range(3)]),
                )

        finished.add(k)
        if {2 * (k // 2), 2 * (k // 2) + 1} <= finished:
            return [(k // 2, wire.push((fin, 2 * (k // 2) + other), (rxz, k // 2), partner))]
        return []

    def reduce_5(k, copies):
        for s, copy in copies:
            copy.wait_recv()
            out, peak, total = merge([fin[2 * s + z], rxz[s]])
            rows = pl.ds(s * QROWS, QROWS)
            heads[g, rows] = mm((out / total).astype(BF16), vup[...]).astype(BF16)
            for d in (1, 2, 3):
                ref = (heads, g, rows)
                headed.append(wire.push(ref, ref, mates[d]))

    state, finished, headed = [None] * len(chunks), set(), []

    def run(steps):
        for step, k in steps:
            state[k] = step(k, state[k])

    run([(gather_0, 0), (gather_0, 1)])
    for copy in loads[:6]:
        copy.wait()
    run([(gather_1, 0), (gather_1, 1), (gather_0, 2)])
    run([(gather_0, 3), (gather_3, 0), (gather_1, 2)])
    run([(gather_0, 4), (gather_3, 1), (gather_1, 3)])
    run([(gather_4, 0), (gather_1, 4), (gather_0, 5)])
    run([(gather_3, 2), (gather_4, 1), (gather_1, 5)])
    run([(gather_3, 3)])
    for copy in loads[6:10]:
        copy.wait()
    run([(gather_5, 0)])
    between = {
        1: [
            (gather_4, 2),
            (gather_3, 4),
            (reduce_1, 0),
            (gather_5, 1),
        ],
        2: [
            (gather_4, 3),
            (gather_3, 5),
            (reduce_1, 1),
            (gather_5, 2),
        ],
        3: [
            (gather_4, 4),
            (reduce_1, 2),
            (reduce_2, 0),
            (gather_5, 3),
        ],
        4: [
            (gather_4, 5),
            (gather_5, 4),
            (reduce_1, 3),
            (reduce_2, 1),
            (reduce_2, 2),
        ],
        5: [
            (gather_5, 5),
            (reduce_1, 4),
            (reduce_2, 3),
            (reduce_3, 0),
        ],
    }

    @pl.loop(0, 6)
    def _(t):
        for at_, steps in between.items():
            if steps:

                @pl.when(t == at_)
                def _():
                    run(steps)

        attend(t)

    run([(reduce_1, 5), (reduce_3, 2), (reduce_2, 4)])
    run([(reduce_3, 1), (reduce_3, 3), (reduce_4, 0)])
    run([(reduce_2, 5), (reduce_4, 2), (reduce_5, 0)])
    run([(reduce_3, 4), (reduce_4, 1), (reduce_5, 2)])
    run([(reduce_4, 3), (reduce_3, 5), (reduce_5, 1)])
    run([(reduce_4, 4), (reduce_5, 3), (reduce_4, 5)])
    run([(reduce_5, 4), (reduce_5, 5)])

    spread, gathered = [], []
    for part in range(2):
        seq, row = padded_row((128, 96), 0, part)
        j = iota((128, 96), 1)
        spread.append(
            ((seq < SEQS) & (j == seq * QROWS + row)).astype(F32).astype(BF16)
        )
        seq, row = padded_row((96, 128), 1, part)
        j = iota((96, 128), 0)
        gathered.append(
            ((seq < SEQS) & (j == seq * QROWS + row)).astype(F32).astype(BF16)
        )
    arrive(headed)
    loads[10].wait()
    own_resid[...] = jnp.zeros((16, QUARTER), BF16)
    own_resid[0:SEQS, :] = resid_ref[0, :, columns]
    lane = iota((1, 128), 1)
    gates = jnp.zeros((1, 128), F32)
    for s in range(SEQS):
        for r in range(4):
            here = lane == s * EXPERTS + routes_ref[s, :, r : r + 1]
            gates = gates + jnp.where(here, weight_ref[0, s : s + 1, r : r + 1].astype(F32), 0.0)
    for part in range(2):
        cols = pl.ds(part * HALF, HALF)
        seq, row = padded_row((128, 16), 0, part)
        mine = ((row == c) & (seq == iota((128, 16), 1)) & (seq < SEQS)).astype(F32).astype(BF16)
        value = mm(mine, own_resid[:, cols])
        for k in range(4):
            rows = mm(spread[part], heads[k]).astype(BF16)
            value = value + mm(rows, wout[k * DV : (k + 1) * DV, cols])
        pbuf[part] = value.astype(BF16).reshape(4, 32, HALF)
        if part == 0:
            seq, row = padded_row((128, 128), 0, part)
            head = jnp.where((seq == SEQS) & (row == c), gates, value[:, :128])
            pbuf[part, :, :, :128] = head.astype(BF16).reshape(4, 32, 128)

    def scatter(source, landing):
        copies = []
        for part, (fs, es, to_f, to_e) in enumerate(axes):
            for d in (1, 2, 3):
                copies.append(wire.push((source, part, fs[d]), (landing, part, d - 1), to_f[d]))
        return copies

    def summed(first, landing, part):
        value = first.astype(F32)
        for d in range(3):
            value = value + landing[part, d].astype(F32)
        return value

    copies = scatter(pbuf, rxa)
    arrive(copies)
    copies = []
    for part, (fs, es, to_f, to_e) in enumerate(axes):
        value = summed(pbuf[part, fs[0]], rxa, part)
        for k in range(4):
            ebuf[part, k] = fold(value[k * 8 : (k + 1) * 8])
        for d in (1, 2, 3):
            copies.append(wire.push((ebuf, part, es[d]), (rxb, part, d - 1), to_e[d]))
    arrive(copies)
    copies = []
    for part, (fs, es, to_f, to_e) in enumerate(axes):
        zbuf[part, z, es[0]] = summed(ebuf[part, es[0]], rxb, part).astype(BF16)
        ref = (zbuf, part, z, es[0])
        for peer in [far] + to_e[1:] + far_e[part][1:]:
            copies.append(wire.push(ref, ref, peer))
    arrive(copies)
    copies = []
    for part, (fs, es, to_f, to_e) in enumerate(axes):
        for k in range(4):
            hidf[part, k] = (
                (unfold(zbuf[part, 0, k]) + unfold(zbuf[part, 1, k])).astype(BF16).astype(F32)
            )
        hid[part, fs[0]] = hidf[part].reshape(32, HALF).astype(BF16)
        for d in (1, 2, 3):
            ref = (hid, part, fs[0])
            copies.append(wire.push(ref, ref, to_f[d]))
    arrive(copies)

    loads[11].wait()
    loads[12].wait()
    eye = iota((96, 128), 0) == iota((96, 128), 1)
    squares = jnp.zeros((96, 1), F32)
    gate = jnp.zeros((96, 512), F32)
    rise = jnp.zeros((96, 512), F32)
    for part in range(2):
        rows = mm(gathered[part], hid[part].reshape(128, HALF))
        squares = squares + jnp.sum(rows * rows, axis=-1, keepdims=True)
        cols = pl.ds(part * HALF, HALF)
        scaled = jnp.concatenate(
            [
                rows[:, n * 128 : (n + 1) * 128] * gain_ref[pl.ds(g * 14 + part * 7 + n, 1), :]
                for n in range(7)
            ],
            axis=1,
        ).astype(BF16)
        gate = gate + mm(scaled, wg[cols, :])
        rise = rise + mm(scaled, wu[cols, :])
    sq[...] = jnp.broadcast_to(
        jnp.sum(jnp.where(eye, squares, 0.0), axis=0, keepdims=True), (8, 128)
    )
    for j in range(4):
        gs[j, :, :128] = gate[:, j * 128 : (j + 1) * 128].astype(BF16)
        gs[j, :, 128:] = rise[:, j * 128 : (j + 1) * 128].astype(BF16)
    copies = []
    for d in (1, 2, 3):
        copies.append(wire.push((sq,), (rxs, d - 1), mates[d]))
        copies.append(wire.push((gs, gs_of[d]), (rxg, d - 1), mates[d]))
    table = hid[0, :, :, :128].reshape(128, 128)
    factors = []
    for part in range(2):
        seq, row = padded_row((128, 128), 0, part)
        pick = (iota((128, 128), 1) == row * 4 + SEQS).astype(F32).astype(BF16)
        here = iota((128, 128), 1) == seq * EXPERTS + c // SPLIT
        factors.append(
            jnp.sum(jnp.where(here, mm(pick, table), 0.0), axis=-1, keepdims=True)
        )
    arrive(copies)
    both = gs[g].astype(F32)
    total = sq[0:1, :]
    for d in range(3):
        both = both + rxg[d].astype(F32)
        total = total + rxs[d, 0:1, :]
    total = jnp.sum(jnp.where(eye, total, 0.0), axis=-1, keepdims=True)
    both = both * lax.rsqrt(total * (1.0 / D) + 1e-06)
    gate, rise = both[:, :128], both[:, 128:]
    units[g] = (gate / (1.0 + jnp.exp(-gate)) * rise).astype(BF16)
    copies = [wire.push((units, g), (units, g), mates[d]) for d in (1, 2, 3)]
    arrive(copies)
    loads[13].wait()
    for part in range(2):
        cols = pl.ds(part * HALF, HALF)
        value = jnp.zeros((128, HALF), F32)
        for k in range(4):
            rows = mm(spread[part], units[k]).astype(BF16)
            value = value + mm(rows, wd[k * 128 : (k + 1) * 128, cols])
        value = value.astype(BF16).astype(F32) * factors[part]
        part_buf[part] = value.astype(BF16).reshape(4, 32, HALF)
    copies = scatter(part_buf, rxq)
    arrive(copies)
    copies = []
    for part, (fs, es, to_f, to_e) in enumerate(axes):
        ybuf[part] = summed(part_buf[part, fs[0]], rxq, part).reshape(4, 8, HALF)
        for d in (1, 2, 3):
            copies.append(wire.push((ybuf, part, es[d]), (rxy, part, d - 1), to_e[d]))
    arrive(copies)
    for part, (fs, es, to_f, to_e) in enumerate(axes):
        wbuf[part] = summed(ybuf[part, es[0]], rxy, part)
    for part, (fs, es, to_f, to_e) in enumerate(axes):
        value, whole = wbuf[part], hidf[part, es[0]] + wbuf[part]
        fo[0, g, part * 4 : (part + 1) * 4, :] = jnp.where(z == 0, whole[0:4], whole[4:8])
        gone[part * 4 : (part + 1) * 4, :] = jnp.where(z == 0, value[4:8], value[0:4])
    copies = [wire.push((gone,), (fo, 1, g), far_mates[d]) for d in range(4)]
    copies += [wire.push((fo, 0, g), (fo, 0, g), mates[d]) for d in (1, 2, 3)]
    arrive(copies)
    for k in range(4):
        both = fo[0, k] + fo[1, k]
        for part in range(2):
            at_ = k * QUARTER + part * HALF
            out_ref[:, at_ : at_ + HALF] = both[part * 4 : part * 4 + SEQS].astype(BF16)
    wire.finish()


def vmem():
    return pl.BlockSpec(memory_space=pltpu.VMEM)


def hbm():
    return pl.BlockSpec(memory_space=pl.ANY)


def on_device(
    queries, cache, value_up_weight, w_out, resid, norm_gain, routes, route_weight,
    w_gate, w_up, w_down,
):
    g, c, x, y, z = place()
    pair, core = lax.rem(g // 2 + z, 2), g % 2
    by_column = queries.reshape(SEQS, 16, 8, QK)
    lower = lax.dynamic_index_in_dim(by_column, 2 * pair + core, 2, keepdims=False)
    upper = lax.dynamic_index_in_dim(by_column, 4 + 2 * (1 - pair) + core, 2, keepdims=False)
    mixed = pl.pallas_call(
        kernel,
        out_shape=jax.ShapeDtypeStruct((SEQS, D), BF16),
        in_specs=[vmem(), vmem(), hbm(), hbm(), hbm(), vmem(), vmem(), vmem(), vmem(), hbm(), hbm(), hbm()],
        out_specs=vmem(),
        scratch_shapes=[
            pltpu.VMEM((6, 4, 4, 2, 16, QK), BF16),
            pltpu.VMEM((SEQS, QK, CTX_DEV), BF16),
            pltpu.VMEM((256, CTX_DEV), F32),
            pltpu.VMEM((256, CTX_DEV), F32),
            pltpu.VMEM((256, CTX_DEV), BF16),
            pltpu.VMEM((256, CTX_DEV), BF16),
            pltpu.VMEM((2, 5, 256, 128), F32),
            pltpu.VMEM((6, 2, 4, 4, 16, QPAD), BF16),
            pltpu.VMEM((6, 2, 2, 2, 16, QPAD), BF16),
            pltpu.VMEM((6, 2, 2, 4, 16, QPAD), BF16),
            pltpu.VMEM((6, 2, 3, 16, QPAD), BF16),
            pltpu.VMEM((6, 2, 16, QPAD), BF16),
            pltpu.VMEM((SEQS, 2, 16, QPAD), BF16),
            pltpu.VMEM((KVL, DV), BF16),
            pltpu.VMEM((512, QUARTER), BF16),
            pltpu.VMEM((QUARTER, 512), BF16),
            pltpu.VMEM((QUARTER, 512), BF16),
            pltpu.VMEM((512, QUARTER), BF16),
            pltpu.VMEM((16, QUARTER), BF16),
            pltpu.VMEM((4, 96, DV), BF16),
            pltpu.VMEM((2, 4, 32, HALF), BF16),
            pltpu.VMEM((2, 3, 32, HALF), BF16),
            pltpu.VMEM((2, 4, 16, 512), BF16),
            pltpu.VMEM((2, 3, 16, 512), BF16),
            pltpu.VMEM((2, 2, 4, 16, 512), BF16),
            pltpu.VMEM((2, 4, 32, HALF), BF16),
            pltpu.VMEM((2, 4, 8, HALF), F32),
            pltpu.VMEM((8, 128), F32),
            pltpu.VMEM((3, 8, 128), F32),
            pltpu.VMEM((4, 96, 256), BF16),
            pltpu.VMEM((3, 96, 256), BF16),
            pltpu.VMEM((4, 96, 128), BF16),
            pltpu.VMEM((2, 4, 32, HALF), BF16),
            pltpu.VMEM((2, 3, 32, HALF), BF16),
            pltpu.VMEM((2, 4, 8, HALF), F32),
            pltpu.VMEM((2, 3, 8, HALF), F32),
            pltpu.VMEM((2, 8, HALF), F32),
            pltpu.VMEM((8, HALF), F32),
            pltpu.VMEM((2, 4, 8, HALF), F32),
            pltpu.SemaphoreType.DMA((250,)),
            pltpu.SemaphoreType.DMA((250,)),
            pltpu.SemaphoreType.DMA((14,)),
        ],
        compiler_params=pltpu.CompilerParams(
            collective_id=0, has_side_effects=True, vmem_limit_bytes=52 * 1024 * 1024
        ),
    )(
        lower,
        upper,
        jnp.swapaxes(cache, 1, 2),
        value_up_weight,
        w_out,
        jnp.swapaxes(resid, 0, 1),
        norm_gain.reshape(D // 128, 128),
        routes,
        jnp.swapaxes(route_weight, 0, 1),
        w_gate,
        w_up,
        w_down,
    )
    return mixed.reshape(SEQS, 1, D)


def solution(mesh):
    placed = (
        P(None, "cp", None),
        P(None, "cp", None),
        P("cp", None, None),
        P("cp", None),
        P(None, "cp", None),
        P(),
        P(None, "cp", None),
        P(None, "cp", None),
        P("cp", "grp", None),
        P("cp", "grp", None),
        P("cp", None, "grp"),
    )
    return jax.shard_map(
        on_device, mesh=mesh, in_specs=placed, out_specs=P(None, "cp", None), check_vma=False
    )
```

```python
import math

import jax
import jax.numpy as jnp
from jax import lax
from jax.experimental import pallas as pl
from jax.experimental.pallas import tpu as pltpu
from jax.sharding import PartitionSpec as P

D = 7168
KVL = 512
DV = 128
SPLIT = 4
QROWS = 32
CTX_DEV = 2048
QK = 576
QPAD = 640
SEQS = 3
EXPERTS = 8
QUARTER = D // 4
HALF = QUARTER // 2
N_CP = 32
CTX = CTX_DEV * N_CP

SCALE = 192.0 ** (-0.5)
SCALE2 = SCALE * math.log2(math.e)
MESH = pl.DeviceIdType.MESH
F32 = jnp.float32
BF16 = jnp.bfloat16


def place():
    g = lax.axis_index("grp")
    c = lax.axis_index("cp")
    return g, c, c // 8, (c // 2) % 4, c % 2


def mm(a, b):
    return jnp.dot(a, b, preferred_element_type=F32)


def mm_nt(a, b):
    return lax.dot_general(a, b, (((1,), (1,)), ((), ())), preferred_element_type=F32)


def iota(shape, axis):
    return lax.broadcasted_iota(jnp.int32, shape, axis)


def part_of(ref, *index):
    return ref.at[index] if index else ref


class Wire:
    def __init__(self, send_sems, recv_sems):
        self.send_sems, self.recv_sems = send_sems, recv_sems
        self.started = []

    def push(self, src, dst, device):
        copy = Copy(self, len(self.started), src, dst, device)
        self.started.append(copy)
        copy.make().start()
        return copy

    def finish(self):
        for copy in self.started:
            copy.make().wait_send()


class Copy:
    def __init__(self, wire, at, src, dst, device):
        self.wire, self.at, self.src, self.dst, self.device = wire, at, src, dst, device

    def make(self):
        return pltpu.make_async_remote_copy(
            src_ref=part_of(*self.src),
            dst_ref=part_of(*self.dst),
            send_sem=self.wire.send_sems.at[self.at],
            recv_sem=self.wire.recv_sems.at[self.at],
            device_id=self.device,
            device_id_type=MESH,
        )

    def wait_recv(self):
        self.make().wait_recv()


def arrive(copies):
    for copy in copies:
        copy.wait_recv()


def fold(value):
    rest = jnp.concatenate([value[:, 512:], jnp.zeros((8, 128), value.dtype)], axis=1)
    return jnp.concatenate([value[:, :512], rest], axis=0).astype(BF16)


def unfold(value):
    value = value.astype(F32)
    return jnp.concatenate([value[:8], value[8:, : HALF - 512]], axis=1)


def greet(peers):
    barrier = pltpu.get_barrier_semaphore()
    for peer in peers:
        pl.semaphore_signal(barrier, inc=1, device_id=peer, device_id_type=MESH)
    pl.semaphore_wait(barrier, len(peers))


def padded_row(shape, axis, part):
    r = iota(shape, axis)
    s, z, b, a = r % 4, (r // 4) % 2, (r // 8) % 4, r // 32
    x, y = (a, b) if part == 0 else (b, a)
    return s, (x * 4 + y) * 2 + z


def unpack(value):
    value = value.reshape(-1, QPAD).astype(F32)
    aux = value[:, KVL:]
    lane = iota(aux.shape, 1)
    peak = jnp.sum(jnp.where(lane == 0, aux, 0.0), axis=-1, keepdims=True)
    total = jnp.sum(jnp.where((lane == 1) | (lane == 2), aux, 0.0), axis=-1, keepdims=True)
    return value[:, :KVL], peak, total


def aux_lanes(peak, total):
    lane = iota((peak.shape[0], QPAD - KVL), 1)
    high = total.astype(BF16).astype(F32)
    low = total - high
    return jnp.where(
        lane == 0, peak, jnp.where(lane == 1, high, jnp.where(lane == 2, low, 0.0))
    )


def merge(values):
    items = [unpack(value) for value in values]
    peak = items[0][1]
    for item in items[1:]:
        peak = jnp.maximum(peak, item[1])
    out, total = None, None
    for item in items:
        factor = jnp.exp((item[1] - peak) * SCALE)
        if out is None:
            out, total = item[0] * factor, item[2] * factor
        else:
            out, total = out + item[0] * factor, total + item[2] * factor
    return out, peak, total


def put(ref, merged):
    out, peak, total = merged
    ref[..., :KVL] = out.astype(BF16).reshape(*ref.shape[:-1], KVL)
    ref[..., KVL:] = aux_lanes(peak, total).astype(BF16).reshape(*ref.shape[:-1], QPAD - KVL)


def kernel(
    lower_ref, upper_ref, cache_ref, vup_ref, wout_ref, resid_ref, gain_ref, routes_ref, weight_ref,
    wg_ref, wu_ref, wd_ref, out_ref,
    qbuf, kv, score_a, score_b, prob_a, prob_b, oscr, msg, rx1, rx2, rx3, fin, rxz,
    vup, wout, wg, wu, wd, own_resid, heads, pbuf, rxa, ebuf, rxb, zbuf, hid, hidf,
    sq, rxs, gs, rxg, units, part_buf, rxq, ybuf, rxy, wbuf, gone, fo,
    send_sems, recv_sems, local_sems,
):
    g, c, x, y, z = place()
    up = lambda v, d: lax.rem(v + d, 4)

    def at(px, py, pz):
        return (g, (px * 4 + py) * 2 + pz)

    xs = [x] + [up(x, d) for d in (1, 2, 3)]
    ys = [y] + [up(y, d) for d in (1, 2, 3)]
    to_x = [None] + [at(xs[d], y, z) for d in (1, 2, 3)]
    to_y = [None] + [at(x, ys[d], z) for d in (1, 2, 3)]
    partner = (lax.rem(g + 2, 4), (x * 4 + y) * 2 + (1 - z))
    far = at(x, y, 1 - z)
    far_x = [None] + [at(xs[d], y, 1 - z) for d in (1, 2, 3)]
    far_y = [None] + [at(x, ys[d], 1 - z) for d in (1, 2, 3)]
    gs_of = [g] + [up(g, d) for d in (1, 2, 3)]
    mates = [None] + [(gs_of[d], c) for d in (1, 2, 3)]
    far_mates = [(gs_of[d], (x * 4 + y) * 2 + (1 - z)) for d in range(4)]
    columns = pl.ds(pl.multiple_of(g * QUARTER, 128), QUARTER)
    q_refs = [(lower_ref, upper_ref)[t % 2].at[t // 2] for t in range(6)]
    pairs = [(q_refs[t], qbuf.at[t, x, y, z]) for t in range(6)]
    pairs += [(cache_ref.at[s], kv.at[s]) for s in range(SEQS)]
    pairs += [
        (vup_ref.at[g], vup),
        (wout_ref.at[:, columns], wout),
        (wg_ref.at[0], wg),
        (wu_ref.at[0], wu),
        (wd_ref.at[0], wd),
    ]
    loads = [
        pltpu.make_async_copy(src, dst, local_sems.at[n]) for n, (src, dst) in enumerate(pairs)
    ]
    for copy in loads:
        copy.start()

    greet(
        to_x[1:] + to_y[1:] + mates[1:] + far_x[1:] + far_y[1:] + far_mates
    )
    wire = Wire(send_sems, recv_sems)

    chunks = [(0, 1), (1, 1), (2, 1), (3, 1), (4, 1), (5, 1)]
    dirs = (1, 3)
    other = 1 - z

    def gather_0(k, _):
        return [wire.push((q_refs[k],), (qbuf, k, x, y, z), partner)]

    def gather_1(k, copies):
        arrive(copies)
        span = pl.ds(*chunks[k])
        copies = []
        for d in (1, 2, 3):
            ref = (qbuf, span, x, y, 0)
            copies.append(wire.push(ref, ref, to_x[d]))
            ref = (qbuf, span, x, y, 1)
            copies.append(wire.push(ref, ref, to_y[d]))
        return copies

    def gather_3(k, copies):
        arrive(copies)
        span = pl.ds(*chunks[k])
        copies = []
        for d in dirs:
            ref = (qbuf, span, slice(None), y, 0)
            copies.append(wire.push(ref, ref, to_y[d]))
            ref = (qbuf, span, x, slice(None), 1)
            copies.append(wire.push(ref, ref, to_x[d]))
        return copies

    def gather_4(k, copies):
        arrive(copies)
        span = pl.ds(*chunks[k])
        copies = []
        for n, d in enumerate(dirs):
            ref = (qbuf, span, pl.ds(2 * n, 2), ys[4 - d], 0)
            copies.append(wire.push(ref, ref, to_y[d]))
            ref = (qbuf, span, xs[4 - d], pl.ds(2 * n, 2), 1)
            copies.append(wire.push(ref, ref, to_x[d]))
        return copies

    def gather_5(k, copies):
        arrive(copies)

    def scores(t, s, part, score):
        q = qbuf[t, 2 * part : 2 * part + 2].reshape(256, QK)
        for n in range(4):
            keys = pl.ds(n * 512, 512)
            value = mm(q, kv[s, :, keys])
            if n < 3:
                score[:, keys] = value
            else:
                score[:, 1536:1920] = value[:, :384]
                row = 16 * part + iota((256, 128), 0) // 16
                position = c * CTX_DEV + 1920 + iota((256, 128), 1)
                score[:, 1920:] = jnp.where(
                    position <= CTX - QROWS + row, value[:, 384:], -1e30
                )

    def weigh(t, s, part, score, prob):
        peak = jnp.max(score[...], axis=-1, keepdims=True).astype(BF16).astype(F32)
        total = jnp.zeros((256, 128), F32)
        for n in range(4):
            keys = pl.ds(n * 512, 512)
            weight = jnp.exp2((score[:, keys] - peak) * SCALE2)
            for m in range(4):
                total = total + weight[:, m * 128 : (m + 1) * 128]
            prob[:, keys] = weight.astype(BF16)
        total = jnp.sum(total, axis=-1, keepdims=True)
        out = mm_nt(prob[...], kv[s, :KVL, :])
        for m in range(4):
            oscr[part, m] = out[:, m * 128 : (m + 1) * 128]
        oscr[part, 4] = aux_lanes(peak, total)
        for n in range(16):
            a, b = (n // 4, n % 4) if part == 0 else (n % 4, n // 4)
            for m in range(5):
                lanes = pl.ds(m * 128, 128)
                msg[t, part, a, b, :, lanes] = oscr[
                    part, m, pl.ds(n, 16, stride=16), :
                ].astype(BF16)

    def attend(t):
        s = t // 2
        scores(t, s, 0, score_a)
        scores(t, s, 1, score_b)
        weigh(t, s, 0, score_a, prob_a)
        weigh(t, s, 1, score_b, prob_b)

    axes = [(xs, ys, to_x, to_y), (ys, xs, to_y, to_x)]
    far_e = [far_y, far_x]

    def reduce_1(k, _):
        span = pl.ds(*chunks[k])
        copies = []
        for part, (fs, es, to_f, to_e) in enumerate(axes):
            for n, d in enumerate(dirs):
                src = (msg, span, part, fs[2], pl.ds(2 * n, 2))
                copies.append(wire.push(src, (rx1, span, part, n), to_f[d]))
        return copies

    def reduce_2(k, copies):
        arrive(copies)
        span = pl.ds(*chunks[k])
        copies = []
        for part, (fs, es, to_f, to_e) in enumerate(axes):
            for n, d in enumerate(dirs):

                @pl.loop(chunks[k][0], sum(chunks[k]))
                def _(t):
                    ref = msg.at[t, part, fs[d], pl.ds(2 * n, 2)]
                    put(ref, merge([ref[...], rx1[t, part, n]]))

                copies.append(
                    wire.push((msg, span, part, fs[d]), (rx2, span, part, n), to_f[d])
                )
        return copies

    def reduce_3(k, copies):
        arrive(copies)
        span = pl.ds(*chunks[k])
        copies = []
        for part, (fs, es, to_f, to_e) in enumerate(axes):

            @pl.loop(2 * chunks[k][0], 2 * sum(chunks[k]))
            def _(at_):
                t, units = at_ // 2, pl.ds(2 * (at_ % 2), 2)
                ref = msg.at[t, part, fs[0], units]
                put(ref, merge([ref[...], rx2[t, part, 0, units], rx2[t, part, 1, units]]))

            for d in (1, 2, 3):
                src = (msg, span, part, fs[0], es[d])
                copies.append(wire.push(src, (rx3, span, part, d - 1), to_e[d]))
        return copies

    def reduce_4(k, copies):
        arrive(copies)

        @pl.loop(chunks[k][0], sum(chunks[k]))
        def _(t):
            for part, (fs, es, to_f, to_e) in enumerate(axes):
                put(
                    fin.at[t, part],
                    merge([msg[t, part, fs[0], es[0]]] + [rx3[t, part, d] for d in range(3)]),
                )

        finished.add(k)
        if {2 * (k // 2), 2 * (k // 2) + 1} <= finished:
            return [(k // 2, wire.push((fin, 2 * (k // 2) + other), (rxz, k // 2), partner))]
        return []

    def reduce_5(k, copies):
        for s, copy in copies:
            copy.wait_recv()
            out, peak, total = merge([fin[2 * s + z], rxz[s]])
            rows = pl.ds(s * QROWS, QROWS)
            heads[g, rows] = mm((out / total).astype(BF16), vup[...]).astype(BF16)
            for d in (1, 2, 3):
                ref = (heads, g, rows)
                headed.append(wire.push(ref, ref, mates[d]))

    state, finished, headed = [None] * len(chunks), set(), []

    def run(steps):
        for step, k in steps:
            state[k] = step(k, state[k])

    run([(gather_0, 0), (gather_0, 1)])
    for copy in loads[:6]:
        copy.wait()
    run([(gather_1, 0), (gather_1, 1), (gather_0, 2)])
    run([(gather_0, 3), (gather_3, 0), (gather_1, 2)])
    run([(gather_0, 4), (gather_3, 1), (gather_1, 3)])
    run([(gather_4, 0), (gather_1, 4), (gather_0, 5)])
    run([(gather_3, 2), (gather_4, 1), (gather_1, 5)])
    run([(gather_3, 3)])
    for copy in loads[6:10]:
        copy.wait()
    run([(gather_5, 0)])
    between = {
        1: [
            (gather_4, 2),
            (gather_3, 4),
            (reduce_1, 0),
            (gather_5, 1),
        ],
        2: [
            (gather_4, 3),
            (gather_3, 5),
            (reduce_1, 1),
            (gather_5, 2),
        ],
        3: [
            (gather_4, 4),
            (reduce_1, 2),
            (reduce_2, 0),
            (gather_5, 3),
        ],
        4: [
            (gather_4, 5),
            (gather_5, 4),
            (reduce_1, 3),
            (reduce_2, 1),
            (reduce_2, 2),
        ],
        5: [
            (gather_5, 5),
            (reduce_1, 4),
            (reduce_2, 3),
            (reduce_3, 0),
        ],
    }

    @pl.loop(0, 6)
    def _(t):
        for at_, steps in between.items():
            if steps:

                @pl.when(t == at_)
                def _():
                    run(steps)

        attend(t)

    run([(reduce_1, 5), (reduce_3, 2), (reduce_2, 4)])
    run([(reduce_3, 1), (reduce_3, 3), (reduce_4, 0)])
    run([(reduce_2, 5), (reduce_4, 2), (reduce_5, 0)])
    run([(reduce_3, 4), (reduce_4, 1), (reduce_5, 2)])
    run([(reduce_4, 3), (reduce_3, 5), (reduce_5, 1)])
    run([(reduce_4, 4), (reduce_5, 3), (reduce_4, 5)])
    run([(reduce_5, 4), (reduce_5, 5)])

    spread, gathered = [], []
    for part in range(2):
        seq, row = padded_row((128, 96), 0, part)
        j = iota((128, 96), 1)
        spread.append(
            ((seq < SEQS) & (j == seq * QROWS + row)).astype(F32).astype(BF16)
        )
        seq, row = padded_row((96, 128), 1, part)
        j = iota((96, 128), 0)
        gathered.append(
            ((seq < SEQS) & (j == seq * QROWS + row)).astype(F32).astype(BF16)
        )
    arrive(headed)
    loads[10].wait()
    own_resid[...] = jnp.zeros((16, QUARTER), BF16)
    own_resid[0:SEQS, :] = resid_ref[0, :, columns]
    def scatter(source, landing, part):
        fs, es, to_f, to_e = axes[part]
        return [
            wire.push((source, part, fs[d]), (landing, part, d - 1), to_f[d]) for d in (1, 2, 3)
        ]

    def summed(first, landing, part):
        value = first.astype(F32)
        for d in range(3):
            value = value + landing[part, d].astype(F32)
        return value

    copies = []
    lane = iota((1, 128), 1)
    gates = jnp.zeros((1, 128), F32)
    for s in range(SEQS):
        for r in range(4):
            here = lane == s * EXPERTS + routes_ref[s, :, r : r + 1]
            gates = gates + jnp.where(here, weight_ref[0, s : s + 1, r : r + 1].astype(F32), 0.0)
    for part in range(2):
        cols = pl.ds(part * HALF, HALF)
        seq, row = padded_row((128, 16), 0, part)
        mine = ((row == c) & (seq == iota((128, 16), 1)) & (seq < SEQS)).astype(F32).astype(BF16)
        value = mm(mine, own_resid[:, cols])
        for k in range(4):
            rows = mm(spread[part], heads[k]).astype(BF16)
            value = value + mm(rows, wout[k * DV : (k + 1) * DV, cols])
        pbuf[part] = value.astype(BF16).reshape(4, 32, HALF)
        if part == 0:
            seq, row = padded_row((128, 128), 0, part)
            head = jnp.where((seq == SEQS) & (row == c), gates, value[:, :128])
            pbuf[part, :, :, :128] = head.astype(BF16).reshape(4, 32, 128)
        copies.append(scatter(pbuf, rxa, part))

    before, copies = copies, []
    for part, (fs, es, to_f, to_e) in enumerate(axes):
        arrive(before[part])
        value = summed(pbuf[part, fs[0]], rxa, part)
        for k in range(4):
            ebuf[part, k] = fold(value[k * 8 : (k + 1) * 8])
        copies.append(
            [wire.push((ebuf, part, es[d]), (rxb, part, d - 1), to_e[d]) for d in (1, 2, 3)]
        )
    before, copies = copies, []
    for part, (fs, es, to_f, to_e) in enumerate(axes):
        arrive(before[part])
        zbuf[part, z, es[0]] = summed(ebuf[part, es[0]], rxb, part).astype(BF16)
        ref = (zbuf, part, z, es[0])
        peers = [far] + to_e[1:] + far_e[part][1:]
        copies.append([wire.push(ref, ref, peer) for peer in peers])
    before, copies = copies, []
    for part, (fs, es, to_f, to_e) in enumerate(axes):
        arrive(before[part])
        for k in range(4):
            hidf[part, k] = (
                (unfold(zbuf[part, 0, k]) + unfold(zbuf[part, 1, k])).astype(BF16).astype(F32)
            )
        hid[part, fs[0]] = hidf[part].reshape(32, HALF).astype(BF16)
        ref = (hid, part, fs[0])
        copies.append([wire.push(ref, ref, to_f[d]) for d in (1, 2, 3)])

    loads[11].wait()
    loads[12].wait()
    eye = iota((96, 128), 0) == iota((96, 128), 1)
    squares = jnp.zeros((96, 1), F32)
    gate = jnp.zeros((96, 512), F32)
    rise = jnp.zeros((96, 512), F32)
    for part in range(2):
        arrive(copies[part])
        rows = mm(gathered[part], hid[part].reshape(128, HALF))
        squares = squares + jnp.sum(rows * rows, axis=-1, keepdims=True)
        cols = pl.ds(part * HALF, HALF)
        scaled = jnp.concatenate(
            [
                rows[:, n * 128 : (n + 1) * 128] * gain_ref[pl.ds(g * 14 + part * 7 + n, 1), :]
                for n in range(7)
            ],
            axis=1,
        ).astype(BF16)
        gate = gate + mm(scaled, wg[cols, :])
        rise = rise + mm(scaled, wu[cols, :])
    sq[...] = jnp.broadcast_to(
        jnp.sum(jnp.where(eye, squares, 0.0), axis=0, keepdims=True), (8, 128)
    )
    for j in range(4):
        gs[j, :, :128] = gate[:, j * 128 : (j + 1) * 128].astype(BF16)
        gs[j, :, 128:] = rise[:, j * 128 : (j + 1) * 128].astype(BF16)
    copies = []
    for d in (1, 2, 3):
        copies.append(wire.push((sq,), (rxs, d - 1), mates[d]))
        copies.append(wire.push((gs, gs_of[d]), (rxg, d - 1), mates[d]))
    table = hid[0, :, :, :128].reshape(128, 128)
    factors = []
    for part in range(2):
        seq, row = padded_row((128, 128), 0, part)
        pick = (iota((128, 128), 1) == row * 4 + SEQS).astype(F32).astype(BF16)
        here = iota((128, 128), 1) == seq * EXPERTS + c // SPLIT
        factors.append(
            jnp.sum(jnp.where(here, mm(pick, table), 0.0), axis=-1, keepdims=True)
        )
    arrive(copies)
    both = gs[g].astype(F32)
    total = sq[0:1, :]
    for d in range(3):
        both = both + rxg[d].astype(F32)
        total = total + rxs[d, 0:1, :]
    total = jnp.sum(jnp.where(eye, total, 0.0), axis=-1, keepdims=True)
    both = both * lax.rsqrt(total * (1.0 / D) + 1e-06)
    gate, rise = both[:, :128], both[:, 128:]
    units[g] = (gate / (1.0 + jnp.exp(-gate)) * rise).astype(BF16)
    copies = [wire.push((units, g), (units, g), mates[d]) for d in (1, 2, 3)]
    arrive(copies)
    before = []
    loads[13].wait()
    for part in range(2):
        cols = pl.ds(part * HALF, HALF)
        value = jnp.zeros((128, HALF), F32)
        for k in range(4):
            rows = mm(spread[part], units[k]).astype(BF16)
            value = value + mm(rows, wd[k * 128 : (k + 1) * 128, cols])
        value = value.astype(BF16).astype(F32) * factors[part]
        part_buf[part] = value.astype(BF16).reshape(4, 32, HALF)
        before.append(scatter(part_buf, rxq, part))
    copies = []
    for part, (fs, es, to_f, to_e) in enumerate(axes):
        arrive(before[part])
        ybuf[part] = summed(part_buf[part, fs[0]], rxq, part).reshape(4, 8, HALF)
        copies.append(
            [wire.push((ybuf, part, es[d]), (rxy, part, d - 1), to_e[d]) for d in (1, 2, 3)]
        )
    for part, (fs, es, to_f, to_e) in enumerate(axes):
        arrive(copies[part])
        wbuf[part] = summed(ybuf[part, es[0]], rxy, part)
    for part, (fs, es, to_f, to_e) in enumerate(axes):
        value, whole = wbuf[part], hidf[part, es[0]] + wbuf[part]
        fo[0, g, part * 4 : (part + 1) * 4, :] = jnp.where(z == 0, whole[0:4], whole[4:8])
        gone[part * 4 : (part + 1) * 4, :] = jnp.where(z == 0, value[4:8], value[0:4])
    copies = [wire.push((gone,), (fo, 1, g), far_mates[d]) for d in range(4)]
    copies += [wire.push((fo, 0, g), (fo, 0, g), mates[d]) for d in (1, 2, 3)]
    arrive(copies)
    for k in range(4):
        both = fo[0, k] + fo[1, k]
        for part in range(2):
            at_ = k * QUARTER + part * HALF
            out_ref[:, at_ : at_ + HALF] = both[part * 4 : part * 4 + SEQS].astype(BF16)
    wire.finish()


def vmem():
    return pl.BlockSpec(memory_space=pltpu.VMEM)


def hbm():
    return pl.BlockSpec(memory_space=pl.ANY)


def on_device(
    queries, cache, value_up_weight, w_out, resid, norm_gain, routes, route_weight,
    w_gate, w_up, w_down,
):
    g, c, x, y, z = place()
    pair, core = lax.rem(g // 2 + z, 2), g % 2
    by_column = queries.reshape(SEQS, 16, 8, QK)
    lower = lax.dynamic_index_in_dim(by_column, 2 * pair + core, 2, keepdims=False)
    upper = lax.dynamic_index_in_dim(by_column, 4 + 2 * (1 - pair) + core, 2, keepdims=False)
    mixed = pl.pallas_call(
        kernel,
        out_shape=jax.ShapeDtypeStruct((SEQS, D), BF16),
        in_specs=[vmem(), vmem(), hbm(), hbm(), hbm(), vmem(), vmem(), vmem(), vmem(), hbm(), hbm(), hbm()],
        out_specs=vmem(),
        scratch_shapes=[
            pltpu.VMEM((6, 4, 4, 2, 16, QK), BF16),
            pltpu.VMEM((SEQS, QK, CTX_DEV), BF16),
            pltpu.VMEM((256, CTX_DEV), F32),
            pltpu.VMEM((256, CTX_DEV), F32),
            pltpu.VMEM((256, CTX_DEV), BF16),
            pltpu.VMEM((256, CTX_DEV), BF16),
            pltpu.VMEM((2, 5, 256, 128), F32),
            pltpu.VMEM((6, 2, 4, 4, 16, QPAD), BF16),
            pltpu.VMEM((6, 2, 2, 2, 16, QPAD), BF16),
            pltpu.VMEM((6, 2, 2, 4, 16, QPAD), BF16),
            pltpu.VMEM((6, 2, 3, 16, QPAD), BF16),
            pltpu.VMEM((6, 2, 16, QPAD), BF16),
            pltpu.VMEM((SEQS, 2, 16, QPAD), BF16),
            pltpu.VMEM((KVL, DV), BF16),
            pltpu.VMEM((512, QUARTER), BF16),
            pltpu.VMEM((QUARTER, 512), BF16),
            pltpu.VMEM((QUARTER, 512), BF16),
            pltpu.VMEM((512, QUARTER), BF16),
            pltpu.VMEM((16, QUARTER), BF16),
            pltpu.VMEM((4, 96, DV), BF16),
            pltpu.VMEM((2, 4, 32, HALF), BF16),
            pltpu.VMEM((2, 3, 32, HALF), BF16),
            pltpu.VMEM((2, 4, 16, 512), BF16),
            pltpu.VMEM((2, 3, 16, 512), BF16),
            pltpu.VMEM((2, 2, 4, 16, 512), BF16),
            pltpu.VMEM((2, 4, 32, HALF), BF16),
            pltpu.VMEM((2, 4, 8, HALF), F32),
            pltpu.VMEM((8, 128), F32),
            pltpu.VMEM((3, 8, 128), F32),
            pltpu.VMEM((4, 96, 256), BF16),
            pltpu.VMEM((3, 96, 256), BF16),
            pltpu.VMEM((4, 96, 128), BF16),
            pltpu.VMEM((2, 4, 32, HALF), BF16),
            pltpu.VMEM((2, 3, 32, HALF), BF16),
            pltpu.VMEM((2, 4, 8, HALF), F32),
            pltpu.VMEM((2, 3, 8, HALF), F32),
            pltpu.VMEM((2, 8, HALF), F32),
            pltpu.VMEM((8, HALF), F32),
            pltpu.VMEM((2, 4, 8, HALF), F32),
            pltpu.SemaphoreType.DMA((250,)),
            pltpu.SemaphoreType.DMA((250,)),
            pltpu.SemaphoreType.DMA((14,)),
        ],
        compiler_params=pltpu.CompilerParams(
            collective_id=0, has_side_effects=True, vmem_limit_bytes=52 * 1024 * 1024
        ),
    )(
        lower,
        upper,
        jnp.swapaxes(cache, 1, 2),
        value_up_weight,
        w_out,
        jnp.swapaxes(resid, 0, 1),
        norm_gain.reshape(D // 128, 128),
        routes,
        jnp.swapaxes(route_weight, 0, 1),
        w_gate,
        w_up,
        w_down,
    )
    return mixed.reshape(SEQS, 1, D)


def solution(mesh):
    placed = (
        P(None, "cp", None),
        P(None, "cp", None),
        P("cp", None, None),
        P("cp", None),
        P(None, "cp", None),
        P(),
        P(None, "cp", None),
        P(None, "cp", None),
        P("cp", "grp", None),
        P("cp", "grp", None),
        P("cp", None, "grp"),
    )
    return jax.shard_map(
        on_device, mesh=mesh, in_specs=placed, out_specs=P(None, "cp", None), check_vma=False
    )
```
